32 devices in a mesh: ex: 8 (over y, x, core), tok: 4 (over z).
Axes of the slice: x: 2, y: 2, z: 4, core: 2. Of those that a mesh axis runs over, the one named last changes fastest.
Arguments:
- proj_rows: bfloat16 [65536, 128], P(('ex', 'tok')), may hold values from -6 to 6
- query_features: bfloat16 [512, 4096], P('ex'), may hold values from -0.09375 to 0.09375
- doc_lengths: int32 [8, 32], P('ex'), may hold values from 1 to 4096, 8192 in all within a row
- owner_map: int32 [8, 32], P('ex'), may hold values from 0 to 31, each once within a row
Outputs:
- scores: float32 [512, 256], P('ex', 'tok')
The draws below stay inside these ranges and needn't reach their ends.
Inputs may be any that keep to these rules, and one draw needn't show every extreme that they name: `owner_map`: each row lists the slots 0 to 31 once each. `doc_lengths`: each row sums to 8192; its largest entry is exactly 4096.
All inputs are finite; a program needn't handle non-finite values.
Results may differ from the reference program's by a relative error of at most 0.0029.
Values may be sent and summed in bfloat16 or wider, within the bound.
No kernel may reach another device: no remote copies, remote signals or barrier semaphores. Data moves between devices by JAX's collectives and lax.ppermute only.
A program may use at most 64 MiB of HBM per device.

```python
import math
import jax
import jax.numpy as jnp
import numpy as np
from jax import lax

P_SIZE = 64
FEAT = 4096
DOC_DEV = 8
TOK_GROUP = 8192
DOC_GROUP = 32
LEN_MOST = 4096
TOKENS = 65536
DOCS = 256
QUERIES = 512
N_EX = 8
N_TOK = 4


def block_scale(key, shape, cuts, smallest, high):
    def one(axis_at, blocks):
        heights = jax.random.uniform(jax.random.fold_in(jax.random.fold_in(key, 6), axis_at), (blocks,), jnp.float32, smallest / len(cuts), high / len(cuts))
        return jnp.repeat(jnp.exp(heights), shape[axis_at] // blocks).reshape((-1,) + (1,) * (len(shape) - axis_at - 1))

    level = one(*cuts[0])
    for cut in cuts[1:]:
        level = level * one(*cut)
    return level


def profile(count, total, bound, lean):
    loads = [(1 << 20) // math.isqrt(grade ** lean) + 1 for grade in range(2, count + 1)]
    rest, holding = total - bound - (count - 1), [1] * (count - 1)
    while rest > 0:
        free = [i for i in range(count - 1) if holding[i] < bound]
        whole, budget = sum([loads[i] for i in free]), rest
        for i in free:
            extra = min(bound - holding[i], max(1, budget * loads[i] // whole), rest)
            holding[i] = holding[i] + extra
            rest = rest - extra
    return np.array([bound] + holding)


def ragged_sizes(rng, amount, total, bound, lean):
    if amount == 2:
        one = jax.random.randint(rng, (), max(1, total - bound), min(bound, total - 1) + 1)
        return jnp.stack([one, total - one])
    sizes = jnp.asarray(profile(amount, total, bound, lean), jnp.int32)
    twos = (amount - 1) // 2
    giver, receiver = sizes[1:1 + 2 * twos:2], sizes[2:2 + 2 * twos:2]
    room = jnp.minimum(giver - 1, bound - receiver)
    shifted = jax.random.randint(jax.random.fold_in(rng, 1), (twos,), 0, 1 << 20) % (room + 1)
    sizes = sizes.at[1:1 + 2 * twos:2].set(giver - shifted).at[2:2 + 2 * twos:2].set(receiver + shifted)
    return sizes[jax.random.permutation(jax.random.fold_in(rng, 2), amount)]


def centred(stream_key, dims, deviation, limit, split=(), kind=jnp.bfloat16):
    gain = block_scale(stream_key, dims, split, -0.22, 0.18) if split else 1.0
    result = jax.random.normal(stream_key, dims, jnp.float32) * deviation * gain
    return jnp.minimum(jnp.maximum(result, -limit), limit).astype(kind)


def setup_inputs(seed: int = 0) -> dict:
    keys = jax.random.split(jax.random.key(seed), 5)
    proj_rows = centred(keys[0], (TOKENS, 2 * P_SIZE), 1.0, 6.0, ((0, 32),))
    query_features = centred(keys[1], (QUERIES, FEAT), FEAT ** -0.5, 0.09375, ((0, 8),))
    doc_lengths = jax.vmap(lambda own: ragged_sizes(own, DOC_GROUP, TOK_GROUP, LEN_MOST, 2))(jax.random.split(keys[2], N_EX)).reshape((N_EX, DOC_GROUP)).astype(jnp.int32)
    owner_map = jax.vmap(lambda own: jax.random.permutation(own, DOC_GROUP))(jax.random.split(keys[3], N_EX)).reshape((N_EX, DOC_GROUP)).astype(jnp.int32)
    return dict(proj_rows=proj_rows, query_features=query_features, doc_lengths=doc_lengths, owner_map=owner_map)


def group_features(packed):
    group_rows, group_lengths, owner_slots = packed
    doc_ends = jnp.cumsum(group_lengths)
    positions = jnp.arange(TOK_GROUP, dtype=jnp.int32)
    doc_index = lax.optimization_barrier(jnp.sum((positions[:, None] >= doc_ends[None, :]).astype(jnp.int32), axis=1))
    onehot = (doc_index[:, None] == jnp.arange(DOC_GROUP, dtype=jnp.int32)[None, :]).astype(jnp.float32)
    input_rows = group_rows[:, :P_SIZE].astype(jnp.float32)
    grad_rows = group_rows[:, P_SIZE:].astype(jnp.float32)
    spread = (onehot[:, :, None] * grad_rows[:, None, :]).reshape(TOK_GROUP, DOC_GROUP * P_SIZE)
    kron_sum = jnp.dot(spread.T, input_rows, precision=lax.Precision.HIGHEST).reshape(DOC_GROUP, P_SIZE * P_SIZE)
    features = kron_sum / jnp.sqrt(group_lengths.astype(jnp.float32))[:, None]
    placed = jnp.zeros((DOC_GROUP, P_SIZE * P_SIZE), jnp.float32).at[owner_slots].set(features)
    return placed.astype(jnp.bfloat16)

def reference(proj_rows, query_features, doc_lengths, owner_map):
    grouped = proj_rows.reshape(N_EX, TOK_GROUP, 2 * P_SIZE)
    features = lax.map(group_features, (grouped, doc_lengths, owner_map))
    doc_features = features.reshape(N_EX, N_TOK, DOC_DEV, P_SIZE * P_SIZE).transpose(1, 0, 2, 3).reshape(DOCS, P_SIZE * P_SIZE)
    return jnp.dot(query_features, doc_features.T, preferred_element_type=jnp.float32)
```

```python
import jax
import jax.numpy as jnp
from jax import lax
from jax.sharding import PartitionSpec as P

LOW = 4


def partial_features(rows, lengths, owner_slots, first):
    count, width = rows.shape[0], rows.shape[1] // 2
    docs = lengths.shape[0]
    high = docs // LOW
    ends = jnp.cumsum(lengths)
    positions = first + jnp.arange(count, dtype=jnp.int32)
    inside = (positions[:, None] >= (ends - lengths)[None, :]) & (positions[:, None] < ends[None, :])
    slots = jnp.sum(jnp.where(inside, owner_slots[None, :], 0), axis=1)
    by_slot = owner_slots[None, :] == jnp.arange(docs, dtype=jnp.int32)[:, None]
    slot_lengths = jnp.sum(jnp.where(by_slot, lengths[None, :], 0), axis=1)
    high_mask = (slots // LOW)[:, None] == jnp.arange(high, dtype=jnp.int32)[None, :]
    low_mask = (slots % LOW)[:, None] == jnp.arange(LOW, dtype=jnp.int32)[None, :]
    zero = jnp.zeros((), rows.dtype)
    grads = jnp.where(high_mask[:, :, None], rows[:, None, width:], zero).reshape(count, high * width)
    inputs = jnp.where(low_mask[:, :, None], rows[:, None, :width], zero).reshape(count, LOW * width)
    sums = jnp.einsum("ta,tb->ab", grads, inputs, preferred_element_type=jnp.float32)
    sums = sums.reshape(high, width, LOW, width).transpose(0, 2, 1, 3).reshape(docs, width * width)
    return (sums / jnp.sqrt(slot_lengths.astype(jnp.float32))[:, None]).astype(jnp.bfloat16)


def body(proj_rows, query_features, doc_lengths, owner_map):
    tok_count = lax.axis_size("tok")
    tok_index = lax.axis_index("tok")
    parts = partial_features(proj_rows, doc_lengths[0], owner_map[0], tok_index * proj_rows.shape[0])
    doc_dev = parts.shape[0] // tok_count

    def share(shift):
        start = ((tok_index + shift) % tok_count) * doc_dev
        return lax.dynamic_slice_in_dim(parts, start, doc_dev, axis=0)

    total = share(0).astype(jnp.float32)
    for shift in range(1, tok_count):
        pairs = [(i, (i + shift) % tok_count) for i in range(tok_count)]
        total = total + lax.ppermute(share(shift), "tok", pairs).astype(jnp.float32)
    features = total.astype(jnp.bfloat16)
    return jnp.einsum(
        "qf,df->qd",
        query_features,
        lax.all_gather(features, "ex", axis=0, tiled=True),
        preferred_element_type=jnp.float32,
    )


def solution(mesh):
    placed = (P(("ex", "tok"), None), P("ex", None), P("ex", None), P("ex", None))
    return jax.shard_map(
        body, mesh=mesh, in_specs=placed, out_specs=P("ex", "tok"), check_vma=False
    )
```

```python
import jax
import jax.numpy as jnp
from jax import lax
from jax.sharding import PartitionSpec as P

LOW = 4


def partial_features(rows, lengths, owner_slots, first):
    count, width = rows.shape[0], rows.shape[1] // 2
    docs = lengths.shape[0]
    high = docs // LOW
    ends = jnp.cumsum(lengths)
    positions = first + jnp.arange(count, dtype=jnp.int32)
    inside = (positions[:, None] >= (ends - lengths)[None, :]) & (positions[:, None] < ends[None, :])
    slots = jnp.sum(jnp.where(inside, owner_slots[None, :], 0), axis=1)
    by_slot = owner_slots[None, :] == jnp.arange(docs, dtype=jnp.int32)[:, None]
    slot_lengths = jnp.sum(jnp.where(by_slot, lengths[None, :], 0), axis=1)
    high_mask = (slots // LOW)[:, None] == jnp.arange(high, dtype=jnp.int32)[None, :]
    low_mask = (slots % LOW)[:, None] == jnp.arange(LOW, dtype=jnp.int32)[None, :]
    zero = jnp.zeros((), rows.dtype)
    grads = jnp.where(high_mask[:, :, None], rows[:, None, width:], zero).reshape(count, high * width)
    inputs = jnp.where(low_mask[:, :, None], rows[:, None, :width], zero).reshape(count, LOW * width)
    sums = jnp.einsum("ta,tb->ab", grads, inputs, preferred_element_type=jnp.float32)
    sums = sums.reshape(high, width, LOW, width).transpose(0, 2, 1, 3).reshape(docs, width * width)
    return (sums / jnp.sqrt(slot_lengths.astype(jnp.float32))[:, None]).astype(jnp.bfloat16)


def body(proj_rows, query_features, doc_lengths, owner_map):
    tok_count = lax.axis_size("tok")
    tok_index = lax.axis_index("tok")
    parts = partial_features(proj_rows, doc_lengths[0], owner_map[0], tok_index * proj_rows.shape[0])
    shares = parts.reshape(tok_count, -1, parts.shape[1])
    received = lax.all_to_all(shares, "tok", split_axis=0, concat_axis=0)
    total = jnp.sum(received.astype(jnp.float32), axis=0)
    features = total.astype(jnp.bfloat16)
    return jnp.einsum(
        "qf,df->qd",
        query_features,
        lax.all_gather(features, "ex", axis=0, tiled=True),
        preferred_element_type=jnp.float32,
    )


def solution(mesh):
    placed = (P(("ex", "tok"), None), P("ex", None), P("ex", None), P("ex", None))
    return jax.shard_map(
        body, mesh=mesh, in_specs=placed, out_specs=P("ex", "tok"), check_vma=False
    )
```

```python
import functools

import jax
import jax.numpy as jnp
from jax import lax
from jax.experimental import pallas as pl
from jax.experimental.pallas import tpu as pltpu
from jax.sharding import PartitionSpec as P

LANES = 128
ROW_BY_ROW = (((1,), (1,)), ((), ()))


def feature_kernel(lengths, owners, rows, *refs):
    *shares, grads, inputs, sums = refs
    count, width = rows.shape[0], rows.shape[1] // 2
    docs, tok_count = lengths.shape[1], len(shares)
    doc_dev = docs // tok_count
    tok = lax.axis_index("tok")

    blocks = count // LANES
    token = lax.broadcasted_iota(jnp.int32, (blocks, LANES), 0) * LANES
    token = tok * count + token + lax.broadcasted_iota(jnp.int32, (blocks, LANES), 1)
    share_of = jnp.zeros((blocks, LANES), jnp.int32)
    row_of = jnp.zeros((blocks, LANES), jnp.int32)
    size_row = lax.broadcasted_iota(jnp.int32, (doc_dev, LANES), 0)
    sizes = [jnp.ones((doc_dev, LANES), jnp.int32) for _ in shares]
    start = jnp.int32(0)
    for k in range(docs):
        slot = owners[0, k]
        share = lax.rem(lax.div(slot, doc_dev) - tok + tok_count, tok_count)
        row = lax.rem(slot, doc_dev)
        here = token >= start
        share_of = jnp.where(here, share, share_of)
        row_of = jnp.where(here, row, row_of)
        for s in range(tok_count):
            sizes[s] = jnp.where(size_row == jnp.where(share == s, row, -1), lengths[0, k], sizes[s])
        start = start + lengths[0, k]

    eye = (
        lax.broadcasted_iota(jnp.int32, (2 * width, 2 * width), 0)
        == lax.broadcasted_iota(jnp.int32, (2 * width, 2 * width), 1)
    ).astype(rows.dtype)
    for b in range(blocks):
        part = slice(b * LANES, (b + 1) * LANES)
        turned = lax.dot_general(eye, rows[part, :], ROW_BY_ROW, preferred_element_type=jnp.float32)
        for s in range(tok_count):
            kept = jnp.where(share_of[b : b + 1, :] == s, turned[:width], 0.0)
            inputs[s * width : (s + 1) * width, part] = kept.astype(inputs.dtype)
        for r in range(doc_dev):
            kept = jnp.where(row_of[b : b + 1, :] == r, turned[width:], 0.0)
            grads[r * width : (r + 1) * width, part] = kept.astype(grads.dtype)
    product = lax.dot_general(
        grads[...], inputs[...], ROW_BY_ROW, preferred_element_type=jnp.float32
    )
    for p in range(sums.shape[0]):
        sums[p] = product[:, p * LANES : (p + 1) * LANES]

    scales = [1.0 / jnp.sqrt(size.astype(jnp.float32)) for size in sizes]
    low_half = lax.broadcasted_iota(jnp.int32, (doc_dev, LANES), 1) < width
    for m in range(width // 2):
        out = slice(m * LANES, (m + 1) * LANES)
        for s in range(0, tok_count, 2):
            first = sums[s // 2, pl.ds(2 * m, doc_dev, stride=width), :]
            second = sums[s // 2, pl.ds(2 * m + 1, doc_dev, stride=width), :]
            left = jnp.where(low_half, first, pltpu.roll(second, width, 1))
            right = jnp.where(low_half, pltpu.roll(first, width, 1), second)
            shares[s][:, out] = (left * scales[s]).astype(shares[s].dtype)
            shares[s + 1][:, out] = (right * scales[s + 1]).astype(shares[s + 1].dtype)


def feature_shares(proj_rows, doc_lengths, owner_map, tok_count):
    count, width = proj_rows.shape[0], proj_rows.shape[1] // 2
    doc_dev = doc_lengths.shape[1] // tok_count
    feat = width * width
    small = pl.BlockSpec(memory_space=pltpu.SMEM)
    whole = pl.BlockSpec(memory_space=pltpu.VMEM)
    return pl.pallas_call(
        feature_kernel,
        out_shape=[
            jax.ShapeDtypeStruct((doc_dev, feat), jnp.bfloat16 if s else jnp.float32)
            for s in range(tok_count)
        ],
        in_specs=[small, small, whole],
        out_specs=[whole] * tok_count,
        scratch_shapes=[
            pltpu.VMEM((doc_dev * width, count), jnp.bfloat16),
            pltpu.VMEM((tok_count * width, count), jnp.bfloat16),
            pltpu.VMEM((tok_count // 2, doc_dev * width, LANES), jnp.float32),
        ],
        compiler_params=pltpu.CompilerParams(vmem_limit_bytes=32 * 1024 * 1024),
        name="features",
    )(doc_lengths, owner_map, proj_rows)


def body(proj_rows, query_features, doc_lengths, owner_map):
    tok_count = lax.axis_size("tok")
    shares = feature_shares(proj_rows, doc_lengths, owner_map, tok_count)
    total = shares[0]
    for shift in range(1, tok_count):
        pairs = [(i, (i + shift) % tok_count) for i in range(tok_count)]
        total = total + lax.ppermute(shares[shift], "tok", pairs).astype(jnp.float32)
    features = total.astype(jnp.bfloat16)
    return jnp.einsum(
        "qf,df->qd",
        query_features,
        lax.all_gather(features, "ex", axis=0, tiled=True),
        preferred_element_type=jnp.float32,
    )


def solution(mesh):
    placed = (P(("ex", "tok"), None), P("ex", None), P("ex", None), P("ex", None))
    return jax.shard_map(
        body, mesh=mesh, in_specs=placed, out_specs=P("ex", "tok"), check_vma=False
    )
```

```python
import jax
import jax.numpy as jnp
from jax import lax
from jax.experimental import pallas as pl
from jax.experimental.pallas import tpu as pltpu
from jax.sharding import PartitionSpec as P

LANES = 128
ROW_BY_ROW = (((1,), (1,)), ((), ()))


def feature_kernel(lengths_hbm, owners_hbm, rows_hbm, *refs):
    *shares, lengths, owners, rows, grads, inputs, sums, arrived = refs
    count, width = rows.shape[0], rows.shape[1] // 2
    copies = [
        pltpu.make_async_copy(source, target, arrived.at[i])
        for i, (source, target) in enumerate(
            ((lengths_hbm, lengths), (owners_hbm, owners), (rows_hbm, rows))
        )
    ]
    for copy in copies:
        copy.start()
    docs, tok_count = lengths.shape[1], len(shares)
    doc_dev = docs // tok_count
    tok = lax.axis_index("tok")

    copies[0].wait()
    copies[1].wait()
    blocks = count // LANES
    token = lax.broadcasted_iota(jnp.int32, (blocks, LANES), 0) * LANES
    token = tok * count + token + lax.broadcasted_iota(jnp.int32, (blocks, LANES), 1)
    share_of = jnp.zeros((blocks, LANES), jnp.int32)
    row_of = jnp.zeros((blocks, LANES), jnp.int32)
    size_row = lax.broadcasted_iota(jnp.int32, (doc_dev, LANES), 0)
    sizes = [jnp.ones((doc_dev, LANES), jnp.int32) for _ in shares]
    start = jnp.int32(0)
    for k in range(docs):
        slot = owners[0, k]
        share = lax.rem(lax.div(slot, doc_dev) - tok + tok_count, tok_count)
        row = lax.rem(slot, doc_dev)
        here = token >= start
        share_of = jnp.where(here, share, share_of)
        row_of = jnp.where(here, row, row_of)
        for s in range(tok_count):
            sizes[s] = jnp.where(size_row == jnp.where(share == s, row, -1), lengths[0, k], sizes[s])
        start = start + lengths[0, k]

    eye = (
        lax.broadcasted_iota(jnp.int32, (2 * width, 2 * width), 0)
        == lax.broadcasted_iota(jnp.int32, (2 * width, 2 * width), 1)
    ).astype(rows.dtype)
    copies[2].wait()
    for b in range(blocks):
        part = slice(b * LANES, (b + 1) * LANES)
        turned = lax.dot_general(eye, rows[part, :], ROW_BY_ROW, preferred_element_type=jnp.float32)
        for s in range(tok_count):
            kept = jnp.where(share_of[b : b + 1, :] == s, turned[:width], 0.0)
            inputs[s * width : (s + 1) * width, part] = kept.astype(inputs.dtype)
        for r in range(doc_dev):
            kept = jnp.where(row_of[b : b + 1, :] == r, turned[width:], 0.0)
            grads[r * width : (r + 1) * width, part] = kept.astype(grads.dtype)
    product = lax.dot_general(
        grads[...], inputs[...], ROW_BY_ROW, preferred_element_type=jnp.float32
    )
    for p in range(sums.shape[0]):
        sums[p] = product[:, p * LANES : (p + 1) * LANES]

    scales = [1.0 / jnp.sqrt(size.astype(jnp.float32)) for size in sizes]
    low_half = lax.broadcasted_iota(jnp.int32, (doc_dev, LANES), 1) < width
    for m in range(width // 2):
        out = slice(m * LANES, (m + 1) * LANES)
        for s in range(0, tok_count, 2):
            first = sums[s // 2, pl.ds(2 * m, doc_dev, stride=width), :]
            second = sums[s // 2, pl.ds(2 * m + 1, doc_dev, stride=width), :]
            left = jnp.where(low_half, first, pltpu.roll(second, width, 1))
            right = jnp.where(low_half, pltpu.roll(first, width, 1), second)
            shares[s][:, out] = (left * scales[s]).astype(shares[s].dtype)
            shares[s + 1][:, out] = (right * scales[s + 1]).astype(shares[s + 1].dtype)


def feature_shares(proj_rows, doc_lengths, owner_map, tok_count):
    count, width = proj_rows.shape[0], proj_rows.shape[1] // 2
    doc_dev = doc_lengths.shape[1] // tok_count
    feat = width * width
    far = pl.BlockSpec(memory_space=pltpu.HBM)
    whole = pl.BlockSpec(memory_space=pltpu.VMEM)
    return pl.pallas_call(
        feature_kernel,
        out_shape=[
            jax.ShapeDtypeStruct((doc_dev, feat), jnp.bfloat16 if s else jnp.float32)
            for s in range(tok_count)
        ],
        in_specs=[far, far, far],
        out_specs=[whole] * tok_count,
        scratch_shapes=[
            pltpu.SMEM(doc_lengths.shape, jnp.int32),
            pltpu.SMEM(owner_map.shape, jnp.int32),
            pltpu.VMEM(proj_rows.shape, proj_rows.dtype),
            pltpu.VMEM((doc_dev * width, count), jnp.bfloat16),
            pltpu.VMEM((tok_count * width, count), jnp.bfloat16),
            pltpu.VMEM((tok_count // 2, doc_dev * width, LANES), jnp.float32),
            pltpu.SemaphoreType.DMA((3,)),
        ],
        compiler_params=pltpu.CompilerParams(vmem_limit_bytes=32 * 1024 * 1024),
        name="features",
    )(doc_lengths, owner_map, proj_rows)


def score_kernel(query, *refs):
    *blocks, scores = refs
    doc_dev = blocks[0].shape[0]
    features = jnp.concatenate([block[...] for block in blocks], axis=0)
    products = lax.dot_general(
        features, query[...], ROW_BY_ROW, preferred_element_type=jnp.float32
    )
    parts = [products[i * doc_dev : (i + 1) * doc_dev] for i in range(len(blocks))]
    ex = lax.axis_index("ex")
    flip = 1
    while flip < len(blocks):
        swap = lax.rem(lax.div(ex, flip), 2) == 1
        parts = [jnp.where(swap, parts[i ^ flip], parts[i]) for i in range(len(parts))]
        flip *= 2
    scores[...] = jnp.concatenate(parts, axis=0).T


def block_scores(query_features, blocks):
    whole = pl.BlockSpec(memory_space=pltpu.VMEM)
    docs = len(blocks) * blocks[0].shape[0]
    return pl.pallas_call(
        score_kernel,
        out_shape=jax.ShapeDtypeStruct((query_features.shape[0], docs), jnp.float32),
        in_specs=[whole] * (1 + len(blocks)),
        out_specs=whole,
        name="scores",
    )(query_features, *blocks)


def body(proj_rows, query_features, doc_lengths, owner_map):
    tok_count = lax.axis_size("tok")
    shares = feature_shares(proj_rows, doc_lengths, owner_map, tok_count)
    total = shares[0]
    for shift in range(1, tok_count):
        pairs = [(i, (i + shift) % tok_count) for i in range(tok_count)]
        total = total + lax.ppermute(shares[shift], "tok", pairs).astype(jnp.float32)
    features = total.astype(jnp.bfloat16)
    ex_count = lax.axis_size("ex")
    if ex_count not in (2, 4, 8):
        gathered = lax.all_gather(features, "ex", axis=0, tiled=True)
        return jnp.einsum("qf,df->qd", query_features, gathered, preferred_element_type=jnp.float32)
    blocks = [features] + [None] * (ex_count - 1)
    for flip in range(ex_count - 1, 0, -1):
        blocks[flip] = lax.ppermute(features, "ex", [(i, i ^ flip) for i in range(ex_count)])
    return block_scores(query_features, blocks)


def solution(mesh):
    placed = (P(("ex", "tok"), None), P("ex", None), P("ex", None), P("ex", None))
    return jax.shard_map(
        body, mesh=mesh, in_specs=placed, out_specs=P("ex", "tok"), check_vma=False
    )
```

```python
import jax
import jax.numpy as jnp
from jax import lax
from jax.experimental import pallas as pl
from jax.experimental.pallas import tpu as pltpu
from jax.sharding import PartitionSpec as P

LANES = 128
ROW_BY_ROW = (((1,), (1,)), ((), ()))


def feature_kernel(lengths_hbm, owners_hbm, rows_hbm, *refs):
    *shares, lengths, owners, rows, grads, inputs, sums, arrived = refs
    count, width = rows.shape[0], rows.shape[1] // 2
    copies = [
        pltpu.make_async_copy(source, target, arrived.at[i])
        for i, (source, target) in enumerate(
            ((lengths_hbm, lengths), (owners_hbm, owners), (rows_hbm, rows))
        )
    ]
    for copy in copies:
        copy.start()
    docs, tok_count = lengths.shape[1], len(shares)
    doc_dev = docs // tok_count
    tok = lax.axis_index("tok")

    copies[0].wait()
    copies[1].wait()
    blocks = count // LANES
    token = lax.broadcasted_iota(jnp.int32, (blocks, LANES), 0) * LANES
    token = tok * count + token + lax.broadcasted_iota(jnp.int32, (blocks, LANES), 1)
    share_of = jnp.zeros((blocks, LANES), jnp.int32)
    row_of = jnp.zeros((blocks, LANES), jnp.int32)
    size_row = lax.broadcasted_iota(jnp.int32, (doc_dev, LANES), 0)
    sizes = [jnp.ones((doc_dev, LANES), jnp.int32) for _ in shares]
    start = jnp.int32(0)
    for k in range(docs):
        slot = owners[0, k]
        share = lax.div(slot, doc_dev) ^ tok
        row = lax.rem(slot, doc_dev)
        here = token >= start
        share_of = jnp.where(here, share, share_of)
        row_of = jnp.where(here, row, row_of)
        for s in range(tok_count):
            sizes[s] = jnp.where(size_row == jnp.where(share == s, row, -1), lengths[0, k], sizes[s])
        start = start + lengths[0, k]

    eye = (
        lax.broadcasted_iota(jnp.int32, (2 * width, 2 * width), 0)
        == lax.broadcasted_iota(jnp.int32, (2 * width, 2 * width), 1)
    ).astype(rows.dtype)
    copies[2].wait()
    for b in range(blocks):
        part = slice(b * LANES, (b + 1) * LANES)
        turned = lax.dot_general(eye, rows[part, :], ROW_BY_ROW, preferred_element_type=jnp.float32)
        for s in range(tok_count):
            kept = jnp.where(share_of[b : b + 1, :] == s, turned[:width], 0.0)
            inputs[s * width : (s + 1) * width, part] = kept.astype(inputs.dtype)
        for r in range(doc_dev):
            kept = jnp.where(row_of[b : b + 1, :] == r, turned[width:], 0.0)
            grads[r * width : (r + 1) * width, part] = kept.astype(grads.dtype)
    product = lax.dot_general(
        grads[...], inputs[...], ROW_BY_ROW, preferred_element_type=jnp.float32
    )
    for p in range(sums.shape[0]):
        sums[p] = product[:, p * LANES : (p + 1) * LANES]

    scales = [1.0 / jnp.sqrt(size.astype(jnp.float32)) for size in sizes]
    low_half = lax.broadcasted_iota(jnp.int32, (doc_dev, LANES), 1) < width
    for m in range(width // 2):
        out = slice(m * LANES, (m + 1) * LANES)
        for s in range(0, tok_count, 2):
            first = sums[s // 2, pl.ds(2 * m, doc_dev, stride=width), :]
            second = sums[s // 2, pl.ds(2 * m + 1, doc_dev, stride=width), :]
            left = jnp.where(low_half, first, pltpu.roll(second, width, 1))
            right = jnp.where(low_half, pltpu.roll(first, width, 1), second)
            shares[s][:, out] = (left * scales[s]).astype(shares[s].dtype)
            shares[s + 1][:, out] = (right * scales[s + 1]).astype(shares[s + 1].dtype)


def feature_shares(proj_rows, doc_lengths, owner_map, tok_count):
    count, width = proj_rows.shape[0], proj_rows.shape[1] // 2
    doc_dev = doc_lengths.shape[1] // tok_count
    feat = width * width
    far = pl.BlockSpec(memory_space=pltpu.HBM)
    whole = pl.BlockSpec(memory_space=pltpu.VMEM)
    return pl.pallas_call(
        feature_kernel,
        out_shape=[
            jax.ShapeDtypeStruct((doc_dev, feat), jnp.bfloat16 if s else jnp.float32)
            for s in range(tok_count)
        ],
        in_specs=[far, far, far],
        out_specs=[whole] * tok_count,
        scratch_shapes=[
            pltpu.SMEM(doc_lengths.shape, jnp.int32),
            pltpu.SMEM(owner_map.shape, jnp.int32),
            pltpu.VMEM(proj_rows.shape, proj_rows.dtype),
            pltpu.VMEM((doc_dev * width, count), jnp.bfloat16),
            pltpu.VMEM((tok_count * width, count), jnp.bfloat16),
            pltpu.VMEM((tok_count // 2, doc_dev * width, LANES), jnp.float32),
            pltpu.SemaphoreType.DMA((3,)),
        ],
        compiler_params=pltpu.CompilerParams(vmem_limit_bytes=32 * 1024 * 1024),
        name="features",
    )(*(pltpu.with_memory_space_constraint(x, pltpu.HBM) for x in (doc_lengths, owner_map, proj_rows)))


def score_kernel(query, *refs):
    *blocks, scores = refs
    doc_dev = blocks[0].shape[0]
    features = jnp.concatenate([block[...] for block in blocks], axis=0)
    products = lax.dot_general(
        features, query[...], ROW_BY_ROW, preferred_element_type=jnp.float32
    )
    parts = [products[i * doc_dev : (i + 1) * doc_dev] for i in range(len(blocks))]
    ex = lax.axis_index("ex")
    flip = 1
    while flip < len(blocks):
        swap = lax.rem(lax.div(ex, flip), 2) == 1
        parts = [jnp.where(swap, parts[i ^ flip], parts[i]) for i in range(len(parts))]
        flip *= 2
    scores[...] = jnp.concatenate(parts, axis=0).T


def block_scores(query_features, blocks):
    whole = pl.BlockSpec(memory_space=pltpu.VMEM)
    docs = len(blocks) * blocks[0].shape[0]
    return pl.pallas_call(
        score_kernel,
        out_shape=jax.ShapeDtypeStruct((query_features.shape[0], docs), jnp.float32),
        in_specs=[whole] * (1 + len(blocks)),
        out_specs=whole,
        compiler_params=pltpu.CompilerParams(vmem_limit_bytes=16 * 1024 * 1024),
        name="scores",
    )(*(pltpu.with_memory_space_constraint(x, pltpu.VMEM) for x in (query_features, *blocks)))


def exchange(block, axis, flip):
    return lax.ppermute(block, axis, [(i, i ^ flip) for i in range(lax.axis_size(axis))])


def body(proj_rows, query_features, doc_lengths, owner_map):
    tok_count = lax.axis_size("tok")
    shares = feature_shares(proj_rows, doc_lengths, owner_map, tok_count)
    total = shares[0]
    for shift in range(tok_count - 1, 0, -1):
        total = total + exchange(shares[shift], "tok", shift).astype(jnp.float32)
    features = total.astype(jnp.bfloat16)
    ex_count = lax.axis_size("ex")
    if ex_count != 8:
        gathered = lax.all_gather(features, "ex", axis=0, tiled=True)
        return jnp.einsum("qf,df->qd", query_features, gathered, preferred_element_type=jnp.float32)
    blocks = [features] + [None] * (ex_count - 1)
    for flip in (6, 4, 2):
        blocks[flip] = exchange(features, "ex", flip)
    for flip in (0, 2, 4, 6):
        blocks[flip + 1] = exchange(blocks[flip], "ex", 1)
    return block_scores(query_features, blocks)


def solution(mesh):
    placed = (P(("ex", "tok"), None), P("ex", None), P("ex", None), P("ex", None))
    return jax.shard_map(
        body, mesh=mesh, in_specs=placed, out_specs=P("ex", "tok"), check_vma=False
    )
```

```python
import jax
import jax.numpy as jnp
from jax import lax
from jax.experimental import pallas as pl
from jax.experimental.pallas import tpu as pltpu
from jax.sharding import PartitionSpec as P

LANES = 128
ROW_BY_ROW = (((1,), (1,)), ((), ()))


def feature_kernel(lengths_hbm, owners_hbm, rows_hbm, *refs):
    *shares, lengths, owners, rows, grads, inputs, sums, arrived = refs
    count, width = rows.shape[0], rows.shape[1] // 2
    copies = [
        pltpu.make_async_copy(source, target, arrived.at[i])
        for i, (source, target) in enumerate(
            ((lengths_hbm, lengths), (owners_hbm, owners), (rows_hbm, rows))
        )
    ]
    for copy in copies:
        copy.start()
    docs, tok_count = lengths.shape[1], len(shares)
    doc_dev = docs // tok_count
    tok = lax.axis_index("tok")

    copies[0].wait()
    copies[1].wait()
    blocks = count // LANES
    token = lax.broadcasted_iota(jnp.int32, (blocks, LANES), 0) * LANES
    token = tok * count + token + lax.broadcasted_iota(jnp.int32, (blocks, LANES), 1)
    share_of = jnp.zeros((blocks, LANES), jnp.int32)
    row_of = jnp.zeros((blocks, LANES), jnp.int32)
    size_row = lax.broadcasted_iota(jnp.int32, (doc_dev, LANES), 0)
    sizes = [jnp.ones((doc_dev, LANES), jnp.int32) for _ in shares]
    start = jnp.int32(0)
    for k in range(docs):
        slot = owners[0, k]
        share = lax.div(slot, doc_dev) ^ tok
        row = lax.rem(slot, doc_dev)
        here = token >= start
        share_of = jnp.where(here, share, share_of)
        row_of = jnp.where(here, row, row_of)
        for s in range(tok_count):
            sizes[s] = jnp.where(size_row == jnp.where(share == s, row, -1), lengths[0, k], sizes[s])
        start = start + lengths[0, k]

    eye = (
        lax.broadcasted_iota(jnp.int32, (2 * width, 2 * width), 0)
        == lax.broadcasted_iota(jnp.int32, (2 * width, 2 * width), 1)
    ).astype(rows.dtype)
    copies[2].wait()
    for b in range(blocks):
        part = slice(b * LANES, (b + 1) * LANES)
        turned = lax.dot_general(eye, rows[part, :], ROW_BY_ROW, preferred_element_type=jnp.float32)
        for s in range(tok_count):
            kept = jnp.where(share_of[b : b + 1, :] == s, turned[:width], 0.0)
            inputs[s * width : (s + 1) * width, part] = kept.astype(inputs.dtype)
        for r in range(doc_dev):
            kept = jnp.where(row_of[b : b + 1, :] == r, turned[width:], 0.0)
            grads[r * width : (r + 1) * width, part] = kept.astype(grads.dtype)
    product = lax.dot_general(
        grads[...], inputs[...], ROW_BY_ROW, preferred_element_type=jnp.float32
    )
    for p in range(sums.shape[0]):
        sums[p] = product[:, p * LANES : (p + 1) * LANES]

    scales = [1.0 / jnp.sqrt(size.astype(jnp.float32)) for size in sizes]
    low_half = lax.broadcasted_iota(jnp.int32, (doc_dev, LANES), 1) < width
    for m in range(width // 2):
        out = slice(m * LANES, (m + 1) * LANES)
        for s in range(0, tok_count, 2):
            first = sums[s // 2, pl.ds(2 * m, doc_dev, stride=width), :]
            second = sums[s // 2, pl.ds(2 * m + 1, doc_dev, stride=width), :]
            left = jnp.where(low_half, first, pltpu.roll(second, width, 1))
            right = jnp.where(low_half, pltpu.roll(first, width, 1), second)
            shares[s][:, out] = (left * scales[s]).astype(shares[s].dtype)
            shares[s + 1][:, out] = (right * scales[s + 1]).astype(shares[s + 1].dtype)


def feature_shares(proj_rows, doc_lengths, owner_map, tok_count):
    count, width = proj_rows.shape[0], proj_rows.shape[1] // 2
    doc_dev = doc_lengths.shape[1] // tok_count
    feat = width * width
    far = pl.BlockSpec(memory_space=pltpu.HBM)
    whole = pl.BlockSpec(memory_space=pltpu.VMEM)
    return pl.pallas_call(
        feature_kernel,
        out_shape=[
            jax.ShapeDtypeStruct((doc_dev, feat), jnp.bfloat16 if s else jnp.float32)
            for s in range(tok_count)
        ],
        in_specs=[far, far, far],
        out_specs=[whole] * tok_count,
        scratch_shapes=[
            pltpu.SMEM(doc_lengths.shape, jnp.int32),
            pltpu.SMEM(owner_map.shape, jnp.int32),
            pltpu.VMEM(proj_rows.shape, proj_rows.dtype),
            pltpu.VMEM((doc_dev * width, count), jnp.bfloat16),
            pltpu.VMEM((tok_count * width, count), jnp.bfloat16),
            pltpu.VMEM((tok_count // 2, doc_dev * width, LANES), jnp.float32),
            pltpu.SemaphoreType.DMA((3,)),
        ],
        compiler_params=pltpu.CompilerParams(vmem_limit_bytes=32 * 1024 * 1024),
        name="features",
    )(*(pltpu.with_memory_space_constraint(x, pltpu.HBM) for x in (doc_lengths, owner_map, proj_rows)))


def score_kernel(query, *refs):
    *blocks, scores = refs
    doc_dev = blocks[0].shape[0]
    features = jnp.concatenate([block[...] for block in blocks], axis=0)
    products = lax.dot_general(
        features, query[...], ROW_BY_ROW, preferred_element_type=jnp.float32
    )
    parts = [products[i * doc_dev : (i + 1) * doc_dev] for i in range(len(blocks))]
    ex = lax.axis_index("ex")
    flip = 1
    while flip < len(blocks):
        swap = lax.rem(lax.div(ex, flip), 2) == 1
        parts = [jnp.where(swap, parts[i ^ flip], parts[i]) for i in range(len(parts))]
        flip *= 2
    scores[...] = jnp.concatenate(parts, axis=0).T


def block_scores(query_features, blocks):
    whole = pl.BlockSpec(memory_space=pltpu.VMEM)
    docs = len(blocks) * blocks[0].shape[0]
    return pl.pallas_call(
        score_kernel,
        out_shape=jax.ShapeDtypeStruct((query_features.shape[0], docs), jnp.float32),
        in_specs=[whole] * (1 + len(blocks)),
        out_specs=whole,
        compiler_params=pltpu.CompilerParams(vmem_limit_bytes=16 * 1024 * 1024),
        name="scores",
    )(*(pltpu.with_memory_space_constraint(x, pltpu.VMEM) for x in (query_features, *blocks)))


def exchange(block, axis, flip):
    return lax.ppermute(block, axis, [(i, i ^ flip) for i in range(lax.axis_size(axis))])


def body(proj_rows, query_features, doc_lengths, owner_map):
    tok_count = lax.axis_size("tok")
    shares = feature_shares(proj_rows, doc_lengths, owner_map, tok_count)
    total = shares[0]
    for shift in sorted(range(1, tok_count), key=lambda flip: (flip < 2, flip)):
        total = total + exchange(shares[shift], "tok", shift).astype(jnp.float32)
    features = total.astype(jnp.bfloat16)
    ex_count = lax.axis_size("ex")
    if ex_count != 8:
        gathered = lax.all_gather(features, "ex", axis=0, tiled=True)
        return jnp.einsum("qf,df->qd", query_features, gathered, preferred_element_type=jnp.float32)
    blocks = [features] + [None] * (ex_count - 1)
    for flip in (4, 2, 6):
        blocks[flip] = exchange(features, "ex", flip)
    for flip in (0, 4, 2, 6):
        blocks[flip + 1] = exchange(blocks[flip], "ex", 1)
    return block_scores(query_features, blocks)


def solution(mesh):
    placed = (P(("ex", "tok"), None), P("ex", None), P("ex", None), P("ex", None))
    return jax.shard_map(
        body, mesh=mesh, in_specs=placed, out_specs=P("ex", "tok"), check_vma=False
    )
```

```python
import functools

import jax
import jax.numpy as jnp
from jax import lax
from jax.experimental import pallas as pl
from jax.experimental.pallas import tpu as pltpu
from jax.sharding import PartitionSpec as P

LANES = 128
ROW_BY_ROW = (((1,), (1,)), ((), ()))


def feature_kernel(lengths_hbm, owners_hbm, rows_hbm, *refs):
    *shares, lengths, owners, rows, grads, inputs, sums, arrived = refs
    count, width = rows.shape[0], rows.shape[1] // 2
    copies = [
        pltpu.make_async_copy(source, target, arrived.at[i])
        for i, (source, target) in enumerate(
            ((lengths_hbm, lengths), (owners_hbm, owners), (rows_hbm, rows))
        )
    ]
    for copy in copies:
        copy.start()
    docs, tok_count = lengths.shape[1], len(shares)
    doc_dev = docs // tok_count
    tok = lax.axis_index("tok")

    copies[0].wait()
    copies[1].wait()
    blocks = count // LANES
    token = lax.broadcasted_iota(jnp.int32, (blocks, LANES), 0) * LANES
    token = tok * count + token + lax.broadcasted_iota(jnp.int32, (blocks, LANES), 1)
    share_of = jnp.zeros((blocks, LANES), jnp.int32)
    row_of = jnp.zeros((blocks, LANES), jnp.int32)
    size_row = lax.broadcasted_iota(jnp.int32, (doc_dev, LANES), 0)
    sizes = [jnp.ones((doc_dev, LANES), jnp.int32) for _ in shares]
    start = jnp.int32(0)
    for k in range(docs):
        slot = owners[0, k]
        share = lax.div(slot, doc_dev) ^ tok
        row = lax.rem(slot, doc_dev)
        here = token >= start
        share_of = jnp.where(here, share, share_of)
        row_of = jnp.where(here, row, row_of)
        for s in range(tok_count):
            sizes[s] = jnp.where(size_row == jnp.where(share == s, row, -1), lengths[0, k], sizes[s])
        start = start + lengths[0, k]

    eye = (
        lax.broadcasted_iota(jnp.int32, (2 * width, 2 * width), 0)
        == lax.broadcasted_iota(jnp.int32, (2 * width, 2 * width), 1)
    ).astype(rows.dtype)
    copies[2].wait()
    for b in range(blocks):
        part = slice(b * LANES, (b + 1) * LANES)
        turned = lax.dot_general(eye, rows[part, :], ROW_BY_ROW, preferred_element_type=jnp.float32)
        for s in range(tok_count):
            kept = jnp.where(share_of[b : b + 1, :] == s, turned[:width], 0.0)
            inputs[s * width : (s + 1) * width, part] = kept.astype(inputs.dtype)
        for r in range(doc_dev):
            kept = jnp.where(row_of[b : b + 1, :] == r, turned[width:], 0.0)
            grads[r * width : (r + 1) * width, part] = kept.astype(grads.dtype)
    product = lax.dot_general(
        grads[...], inputs[...], ROW_BY_ROW, preferred_element_type=jnp.float32
    )
    for p in range(sums.shape[0]):
        sums[p] = product[:, p * LANES : (p + 1) * LANES]

    scales = [1.0 / jnp.sqrt(size.astype(jnp.float32)) for size in sizes]
    low_half = lax.broadcasted_iota(jnp.int32, (doc_dev, LANES), 1) < width
    for m in range(width // 2):
        out = slice(m * LANES, (m + 1) * LANES)
        for s in range(0, tok_count, 2):
            first = sums[s // 2, pl.ds(2 * m, doc_dev, stride=width), :]
            second = sums[s // 2, pl.ds(2 * m + 1, doc_dev, stride=width), :]
            left = jnp.where(low_half, first, pltpu.roll(second, width, 1))
            right = jnp.where(low_half, pltpu.roll(first, width, 1), second)
            shares[s][:, out] = (left * scales[s]).astype(shares[s].dtype)
            shares[s + 1][:, out] = (right * scales[s + 1]).astype(shares[s + 1].dtype)


def feature_shares(proj_rows, doc_lengths, owner_map, tok_count):
    count, width = proj_rows.shape[0], proj_rows.shape[1] // 2
    doc_dev = doc_lengths.shape[1] // tok_count
    feat = width * width
    far = pl.BlockSpec(memory_space=pltpu.HBM)
    whole = pl.BlockSpec(memory_space=pltpu.VMEM)
    return pl.pallas_call(
        feature_kernel,
        out_shape=[
            jax.ShapeDtypeStruct((doc_dev, feat), jnp.bfloat16 if s % 2 else jnp.float32)
            for s in range(tok_count)
        ],
        in_specs=[far, far, far],
        out_specs=[whole] * tok_count,
        scratch_shapes=[
            pltpu.SMEM(doc_lengths.shape, jnp.int32),
            pltpu.SMEM(owner_map.shape, jnp.int32),
            pltpu.VMEM(proj_rows.shape, proj_rows.dtype),
            pltpu.VMEM((doc_dev * width, count), jnp.bfloat16),
            pltpu.VMEM((tok_count * width, count), jnp.bfloat16),
            pltpu.VMEM((tok_count // 2, doc_dev * width, LANES), jnp.float32),
            pltpu.SemaphoreType.DMA((3,)),
        ],
        compiler_params=pltpu.CompilerParams(vmem_limit_bytes=32 * 1024 * 1024),
        name="features",
    )(*(pltpu.with_memory_space_constraint(x, pltpu.HBM) for x in (doc_lengths, owner_map, proj_rows)))


def score_kernel(flips, query, *refs):
    *blocks, scores = refs
    doc_dev = blocks[0].shape[0]
    features = jnp.concatenate([block[...] for block in blocks], axis=0)
    products = lax.dot_general(
        features, query[...], ROW_BY_ROW, preferred_element_type=jnp.float32
    )
    places = [flips.index(i) for i in range(len(flips))]
    parts = [products[i * doc_dev : (i + 1) * doc_dev] for i in places]
    ex = lax.axis_index("ex")
    flip = 1
    while flip < len(blocks):
        swap = lax.rem(lax.div(ex, flip), 2) == 1
        parts = [jnp.where(swap, parts[i ^ flip], parts[i]) for i in range(len(parts))]
        flip *= 2
    scores[...] = jnp.concatenate(parts, axis=0).T


def block_scores(query_features, blocks):
    whole = pl.BlockSpec(memory_space=pltpu.VMEM)
    docs = len(blocks) * blocks[0].shape[0]
    return pl.pallas_call(
        functools.partial(score_kernel, tuple(blocks)),
        out_shape=jax.ShapeDtypeStruct((query_features.shape[0], docs), jnp.float32),
        in_specs=[whole] * (1 + len(blocks)),
        out_specs=whole,
        compiler_params=pltpu.CompilerParams(vmem_limit_bytes=16 * 1024 * 1024),
        name="scores",
    )(*(pltpu.with_memory_space_constraint(x, pltpu.VMEM) for x in (query_features, *blocks.values())))


def exchange(block, axis, flip):
    return lax.ppermute(block, axis, [(i, i ^ flip) for i in range(lax.axis_size(axis))])


def body(proj_rows, query_features, doc_lengths, owner_map):
    tok_count = lax.axis_size("tok")
    shares = feature_shares(proj_rows, doc_lengths, owner_map, tok_count)
    if tok_count == 4:
        passed = exchange(shares[3], "tok", 1).astype(jnp.float32)
        near = exchange(shares[1], "tok", 1).astype(jnp.float32)
        far = exchange((shares[2] + passed).astype(jnp.bfloat16), "tok", 2).astype(jnp.float32)
        total = shares[0] + near + far
    else:
        total = shares[0]
        for flip in range(1, tok_count):
            total = total + exchange(shares[flip].astype(jnp.bfloat16), "tok", flip).astype(jnp.float32)
    features = total.astype(jnp.bfloat16)
    ex_count = lax.axis_size("ex")
    if ex_count != 8:
        gathered = lax.all_gather(features, "ex", axis=0, tiled=True)
        return jnp.einsum("qf,df->qd", query_features, gathered, preferred_element_type=jnp.float32)
    blocks = {0: features}
    for flip in (4, 2, 6):
        blocks[flip] = exchange(features, "ex", flip)
    for flip in (0, 4, 2, 6):
        blocks[flip + 1] = exchange(blocks[flip], "ex", 1)
    return block_scores(query_features, {flip: blocks[flip] for flip in (0, 1, 6, 7, 2, 3, 4, 5)})


def solution(mesh):
    placed = (P(("ex", "tok"), None), P("ex", None), P("ex", None), P("ex", None))
    return jax.shard_map(
        body, mesh=mesh, in_specs=placed, out_specs=P("ex", "tok"), check_vma=False
    )
```

```python
import jax
import jax.numpy as jnp
from jax import lax
from jax.experimental import pallas as pl
from jax.experimental.pallas import tpu as pltpu
from jax.sharding import PartitionSpec as P

LANES = 128
ROW_BY_ROW = (((1,), (1,)), ((), ()))


def feature_kernel(lengths_hbm, owners_hbm, rows_hbm, *refs):
    *shares, lengths, owners, rows, grads, inputs, sums, arrived = refs
    count, width = rows.shape[0], rows.shape[1] // 2
    copies = [
        pltpu.make_async_copy(source, target, arrived.at[i])
        for i, (source, target) in enumerate(
            ((lengths_hbm, lengths), (owners_hbm, owners), (rows_hbm, rows))
        )
    ]
    for copy in copies:
        copy.start()
    docs, tok_count = lengths.shape[1], len(shares)
    doc_dev = docs // tok_count
    tok = lax.axis_index("tok")

    copies[0].wait()
    copies[1].wait()
    blocks = count // LANES
    token = lax.broadcasted_iota(jnp.int32, (blocks, LANES), 0) * LANES
    token = tok * count + token + lax.broadcasted_iota(jnp.int32, (blocks, LANES), 1)
    share_of = jnp.zeros((blocks, LANES), jnp.int32)
    row_of = jnp.zeros((blocks, LANES), jnp.int32)
    size_row = lax.broadcasted_iota(jnp.int32, (doc_dev, LANES), 0)
    sizes = [jnp.ones((doc_dev, LANES), jnp.int32) for _ in shares]
    start = jnp.int32(0)
    for k in range(docs):
        slot = owners[0, k]
        share = lax.div(slot, doc_dev) ^ tok
        row = lax.rem(slot, doc_dev)
        here = token >= start
        share_of = jnp.where(here, share, share_of)
        row_of = jnp.where(here, row, row_of)
        for s in range(tok_count):
            sizes[s] = jnp.where(size_row == jnp.where(share == s, row, -1), lengths[0, k], sizes[s])
        start = start + lengths[0, k]

    eye = (
        lax.broadcasted_iota(jnp.int32, (2 * width, 2 * width), 0)
        == lax.broadcasted_iota(jnp.int32, (2 * width, 2 * width), 1)
    ).astype(rows.dtype)
    copies[2].wait()
    for b in range(blocks):
        part = slice(b * LANES, (b + 1) * LANES)
        turned = lax.dot_general(eye, rows[part, :], ROW_BY_ROW, preferred_element_type=jnp.float32)
        for s in range(tok_count):
            kept = jnp.where(share_of[b : b + 1, :] == s, turned[:width], 0.0)
            inputs[s * width : (s + 1) * width, part] = kept.astype(inputs.dtype)
        for r in range(doc_dev):
            kept = jnp.where(row_of[b : b + 1, :] == r, turned[width:], 0.0)
            grads[r * width : (r + 1) * width, part] = kept.astype(grads.dtype)
    product = lax.dot_general(
        grads[...], inputs[...], ROW_BY_ROW, preferred_element_type=jnp.float32
    )
    for p in range(sums.shape[0]):
        sums[p] = product[:, p * LANES : (p + 1) * LANES]

    scales = [1.0 / jnp.sqrt(size.astype(jnp.float32)) for size in sizes]
    low_half = lax.broadcasted_iota(jnp.int32, (doc_dev, LANES), 1) < width
    for m in range(width // 2):
        out = slice(m * LANES, (m + 1) * LANES)
        for s in range(0, tok_count, 2):
            first = sums[s // 2, pl.ds(2 * m, doc_dev, stride=width), :]
            second = sums[s // 2, pl.ds(2 * m + 1, doc_dev, stride=width), :]
            left = jnp.where(low_half, first, pltpu.roll(second, width, 1))
            right = jnp.where(low_half, pltpu.roll(first, width, 1), second)
            shares[s][:, out] = (left * scales[s]).astype(shares[s].dtype)
            shares[s + 1][:, out] = (right * scales[s + 1]).astype(shares[s + 1].dtype)


def feature_shares(proj_rows, doc_lengths, owner_map, tok_count):
    count, width = proj_rows.shape[0], proj_rows.shape[1] // 2
    doc_dev = doc_lengths.shape[1] // tok_count
    feat = width * width
    far = pl.BlockSpec(memory_space=pltpu.HBM)
    whole = pl.BlockSpec(memory_space=pltpu.VMEM)
    return pl.pallas_call(
        feature_kernel,
        out_shape=[
            jax.ShapeDtypeStruct((doc_dev, feat), jnp.bfloat16 if s % 2 else jnp.float32)
            for s in range(tok_count)
        ],
        in_specs=[far, far, far],
        out_specs=[whole] * tok_count,
        scratch_shapes=[
            pltpu.SMEM(doc_lengths.shape, jnp.int32),
            pltpu.SMEM(owner_map.shape, jnp.int32),
            pltpu.VMEM(proj_rows.shape, proj_rows.dtype),
            pltpu.VMEM((doc_dev * width, count), jnp.bfloat16),
            pltpu.VMEM((tok_count * width, count), jnp.bfloat16),
            pltpu.VMEM((tok_count // 2, doc_dev * width, LANES), jnp.float32),
            pltpu.SemaphoreType.DMA((3,)),
        ],
        compiler_params=pltpu.CompilerParams(vmem_limit_bytes=32 * 1024 * 1024),
        name="features",
    )(*(pltpu.with_memory_space_constraint(x, pltpu.HBM) for x in (doc_lengths, owner_map, proj_rows)))


def score_kernel(query, *refs):
    *blocks, scores = refs
    doc_dev = blocks[0].shape[0]
    features = jnp.concatenate([block[...] for block in blocks], axis=0)
    products = lax.dot_general(
        features, query[...], ROW_BY_ROW, preferred_element_type=jnp.float32
    )
    own, first, second, third, own_next, first_next, second_next, third_next = (
        products[i * doc_dev : (i + 1) * doc_dev] for i in range(len(blocks))
    )
    ex = lax.axis_index("ex")
    odd = lax.rem(ex, 2) == 1
    parts = [
        own,
        own_next,
        jnp.where(odd, first, second),
        jnp.where(odd, second_next, first_next),
        jnp.where(odd, second, first),
        jnp.where(odd, first_next, second_next),
        third,
        third_next,
    ]
    flip = 1
    while flip < len(parts):
        swap = lax.rem(lax.div(ex, flip), 2) == 1
        parts = [jnp.where(swap, parts[i ^ flip], parts[i]) for i in range(len(parts))]
        flip *= 2
    scores[...] = jnp.concatenate(parts, axis=0).T


def block_scores(query_features, held, held_next):
    whole = pl.BlockSpec(memory_space=pltpu.VMEM)
    operands = (query_features, *held, *held_next)
    docs = (len(operands) - 1) * held[0].shape[0]
    return pl.pallas_call(
        score_kernel,
        out_shape=jax.ShapeDtypeStruct((query_features.shape[0], docs), jnp.float32),
        in_specs=[whole] * len(operands),
        out_specs=whole,
        compiler_params=pltpu.CompilerParams(vmem_limit_bytes=16 * 1024 * 1024),
        name="scores",
    )(*(pltpu.with_memory_space_constraint(x, pltpu.VMEM) for x in operands))


def exchange(block, axis, flip):
    return lax.ppermute(block, axis, [(i, i ^ flip) for i in range(lax.axis_size(axis))])


def body(proj_rows, query_features, doc_lengths, owner_map):
    tok_count = lax.axis_size("tok")
    shares = feature_shares(proj_rows, doc_lengths, owner_map, tok_count)
    if tok_count == 4:
        passed = exchange(shares[3], "tok", 1)
        near, passed = lax.optimization_barrier((shares[1], passed))
        far = (shares[2] + passed.astype(jnp.float32)).astype(jnp.bfloat16)
        near = exchange(near, "tok", 1).astype(jnp.float32)
        far = exchange(far, "tok", 2).astype(jnp.float32)
        total = shares[0] + far + near
    else:
        total = shares[0]
        for flip in range(1, tok_count):
            total = total + exchange(shares[flip].astype(jnp.bfloat16), "tok", flip).astype(jnp.float32)
    features = total.astype(jnp.bfloat16)
    ex_count = lax.axis_size("ex")
    if ex_count != 8:
        gathered = lax.all_gather(features, "ex", axis=0, tiled=True)
        return jnp.einsum("qf,df->qd", query_features, gathered, preferred_element_type=jnp.float32)
    turns = [[(i, i ^ (first if i % 2 else 6 - first)) for i in range(ex_count)] for first in (2, 4)]
    first = lax.ppermute(features, "ex", turns[0])
    second = lax.ppermute(features, "ex", turns[1])
    third = lax.ppermute(first, "ex", turns[1])
    held = (features, first, second, third)
    return block_scores(query_features, held, [exchange(block, "ex", 1) for block in held])


def solution(mesh):
    placed = (P(("ex", "tok"), None), P("ex", None), P("ex", None), P("ex", None))
    return jax.shard_map(
        body, mesh=mesh, in_specs=placed, out_specs=P("ex", "tok"), check_vma=False
    )
```

```python
import functools

import jax
import jax.numpy as jnp
from jax import lax
from jax.experimental import pallas as pl
from jax.experimental.pallas import tpu as pltpu
from jax.sharding import PartitionSpec as P

LANES = 128
ROW_BY_ROW = (((1,), (1,)), ((), ()))


def feature_kernel(lengths_hbm, owners_hbm, rows_hbm, *refs):
    *shares, lengths, owners, rows, grads, inputs, sums, arrived = refs
    count, width = rows.shape[0], rows.shape[1] // 2
    copies = [
        pltpu.make_async_copy(source, target, arrived.at[i])
        for i, (source, target) in enumerate(
            ((lengths_hbm, lengths), (owners_hbm, owners), (rows_hbm, rows))
        )
    ]
    for copy in copies:
        copy.start()
    docs, tok_count = lengths.shape[1], len(shares)
    doc_dev = docs // tok_count
    tok = lax.axis_index("tok")

    copies[0].wait()
    copies[1].wait()
    blocks = count // LANES
    token = lax.broadcasted_iota(jnp.int32, (blocks, LANES), 0) * LANES
    token = tok * count + token + lax.broadcasted_iota(jnp.int32, (blocks, LANES), 1)
    share_of = jnp.zeros((blocks, LANES), jnp.int32)
    row_of = jnp.zeros((blocks, LANES), jnp.int32)
    size_row = lax.broadcasted_iota(jnp.int32, (doc_dev, LANES), 0)
    sizes = [jnp.ones((doc_dev, LANES), jnp.int32) for _ in shares]
    start = jnp.int32(0)
    for k in range(docs):
        slot = owners[0, k]
        share = lax.div(slot, doc_dev) ^ tok
        row = lax.rem(slot, doc_dev)
        here = token >= start
        share_of = jnp.where(here, share, share_of)
        row_of = jnp.where(here, row, row_of)
        for s in range(tok_count):
            sizes[s] = jnp.where(size_row == jnp.where(share == s, row, -1), lengths[0, k], sizes[s])
        start = start + lengths[0, k]

    eye = (
        lax.broadcasted_iota(jnp.int32, (2 * width, 2 * width), 0)
        == lax.broadcasted_iota(jnp.int32, (2 * width, 2 * width), 1)
    ).astype(rows.dtype)
    copies[2].wait()
    for b in range(blocks):
        part = slice(b * LANES, (b + 1) * LANES)
        turned = lax.dot_general(eye, rows[part, :], ROW_BY_ROW, preferred_element_type=jnp.float32)
        for s in range(tok_count):
            kept = jnp.where(share_of[b : b + 1, :] == s, turned[:width], 0.0)
            inputs[s * width : (s + 1) * width, part] = kept.astype(inputs.dtype)
        for r in range(doc_dev):
            kept = jnp.where(row_of[b : b + 1, :] == r, turned[width:], 0.0)
            grads[r * width : (r + 1) * width, part] = kept.astype(grads.dtype)
    product = lax.dot_general(
        grads[...], inputs[...], ROW_BY_ROW, preferred_element_type=jnp.float32
    )
    for p in range(sums.shape[0]):
        sums[p] = product[:, p * LANES : (p + 1) * LANES]

    scales = [1.0 / jnp.sqrt(size.astype(jnp.float32)) for size in sizes]
    low_half = lax.broadcasted_iota(jnp.int32, (doc_dev, LANES), 1) < width
    for m in range(width // 2):
        out = slice(m * LANES, (m + 1) * LANES)
        for s in range(0, tok_count, 2):
            first = sums[s // 2, pl.ds(2 * m, doc_dev, stride=width), :]
            second = sums[s // 2, pl.ds(2 * m + 1, doc_dev, stride=width), :]
            left = jnp.where(low_half, first, pltpu.roll(second, width, 1))
            right = jnp.where(low_half, pltpu.roll(first, width, 1), second)
            shares[s][:, out] = (left * scales[s]).astype(shares[s].dtype)
            shares[s + 1][:, out] = (right * scales[s + 1]).astype(shares[s + 1].dtype)


def feature_shares(proj_rows, doc_lengths, owner_map, tok_count):
    count, width = proj_rows.shape[0], proj_rows.shape[1] // 2
    doc_dev = doc_lengths.shape[1] // tok_count
    feat = width * width
    far = pl.BlockSpec(memory_space=pltpu.HBM)
    whole = pl.BlockSpec(memory_space=pltpu.VMEM)
    return pl.pallas_call(
        feature_kernel,
        out_shape=[
            jax.ShapeDtypeStruct((doc_dev, feat), jnp.bfloat16 if s else jnp.float32)
            for s in range(tok_count)
        ],
        in_specs=[far, far, far],
        out_specs=[whole] * tok_count,
        scratch_shapes=[
            pltpu.SMEM(doc_lengths.shape, jnp.int32),
            pltpu.SMEM(owner_map.shape, jnp.int32),
            pltpu.VMEM(proj_rows.shape, proj_rows.dtype),
            pltpu.VMEM((doc_dev * width, count), jnp.bfloat16),
            pltpu.VMEM((tok_count * width, count), jnp.bfloat16),
            pltpu.VMEM((tok_count // 2, doc_dev * width, LANES), jnp.float32),
            pltpu.SemaphoreType.DMA((3,)),
        ],
        compiler_params=pltpu.CompilerParams(vmem_limit_bytes=32 * 1024 * 1024),
        name="features",
    )(*(pltpu.with_memory_space_constraint(x, pltpu.HBM) for x in (doc_lengths, owner_map, proj_rows)))


def score_kernel(doc_dev, query, mine, other, scores):
    features = jnp.concatenate([mine[...], other[...]], axis=0)
    products = lax.dot_general(
        features, query[...], ROW_BY_ROW, preferred_element_type=jnp.float32
    )
    half = mine.shape[0]
    odd = lax.rem(lax.axis_index("ex"), 2) == 1
    parts = []
    for i in range(0, half, doc_dev):
        first, second = products[i : i + doc_dev], products[half + i : half + i + doc_dev]
        parts += [jnp.where(odd, second, first), jnp.where(odd, first, second)]
    scores[...] = jnp.concatenate(parts, axis=0).T


def block_scores(query_features, mine, other, doc_dev):
    whole = pl.BlockSpec(memory_space=pltpu.VMEM)
    return pl.pallas_call(
        functools.partial(score_kernel, doc_dev),
        out_shape=jax.ShapeDtypeStruct(
            (query_features.shape[0], mine.shape[0] + other.shape[0]), jnp.float32
        ),
        in_specs=[whole] * 3,
        out_specs=whole,
        compiler_params=pltpu.CompilerParams(vmem_limit_bytes=16 * 1024 * 1024),
        name="scores",
    )(*(pltpu.with_memory_space_constraint(x, pltpu.VMEM) for x in (query_features, mine, other)))


def exchange(block, axis, flip):
    return lax.ppermute(block, axis, [(i, i ^ flip) for i in range(lax.axis_size(axis))])


def body(proj_rows, query_features, doc_lengths, owner_map):
    tok_count = lax.axis_size("tok")
    shares = feature_shares(proj_rows, doc_lengths, owner_map, tok_count)
    total = shares[0]
    for shift in sorted(range(1, tok_count), key=lambda flip: (flip < 2, flip)):
        total = total + exchange(shares[shift], "tok", shift).astype(jnp.float32)
    features = total.astype(jnp.bfloat16)
    ex_count = lax.axis_size("ex")
    if ex_count != 8:
        gathered = lax.all_gather(features, "ex", axis=0, tiled=True)
        return jnp.einsum("qf,df->qd", query_features, gathered, preferred_element_type=jnp.float32)
    cores = [list(range(core, ex_count, 2)) for core in range(2)]
    mine = lax.all_gather(features, "ex", axis=0, tiled=True, axis_index_groups=cores)
    return block_scores(query_features, mine, exchange(mine, "ex", 1), features.shape[0])


def solution(mesh):
    placed = (P(("ex", "tok"), None), P("ex", None), P("ex", None), P("ex", None))
    return jax.shard_map(
        body, mesh=mesh, in_specs=placed, out_specs=P("ex", "tok"), check_vma=False
    )
```

```python
import jax
import jax.numpy as jnp
from jax import lax
from jax.experimental import pallas as pl
from jax.experimental.pallas import tpu as pltpu
from jax.sharding import PartitionSpec as P

LANES = 128
ROW_BY_ROW = (((1,), (1,)), ((), ()))


def feature_kernel(lengths_hbm, owners_hbm, rows_hbm, *refs):
    *shares, lengths, owners, rows, grads, inputs, sums, arrived = refs
    count, width = rows.shape[0], rows.shape[1] // 2
    copies = [
        pltpu.make_async_copy(source, target, arrived.at[i])
        for i, (source, target) in enumerate(
            ((lengths_hbm, lengths), (owners_hbm, owners), (rows_hbm, rows))
        )
    ]
    for copy in copies:
        copy.start()
    docs, tok_count = lengths.shape[1], len(shares)
    doc_dev = docs // tok_count
    tok = lax.axis_index("tok")

    copies[0].wait()
    copies[1].wait()
    blocks, shift = count // LANES, doc_dev.bit_length() - 1
    token = lax.broadcasted_iota(jnp.int32, (blocks, LANES), 0) * LANES
    token = tok * count + token + lax.broadcasted_iota(jnp.int32, (blocks, LANES), 1)
    slot_of = jnp.zeros((blocks, LANES), jnp.int32)
    size_row = lax.broadcasted_iota(jnp.int32, (doc_dev, LANES), 0)
    size_slots = [((tok ^ s) << shift) + size_row for s in range(tok_count)]
    sizes = [jnp.ones((doc_dev, LANES), jnp.int32) for _ in shares]
    start = jnp.int32(0)
    for k in range(docs):
        slot, length = owners[0, k], lengths[0, k]
        slot_of = jnp.where(token >= start, slot, slot_of)
        sizes = [jnp.where(at == slot, length, size) for at, size in zip(size_slots, sizes)]
        start = start + length
    share_of, row_of = (slot_of >> shift) ^ tok, slot_of & (doc_dev - 1)

    eye = (
        lax.broadcasted_iota(jnp.int32, (2 * width, 2 * width), 0)
        == lax.broadcasted_iota(jnp.int32, (2 * width, 2 * width), 1)
    ).astype(rows.dtype)
    copies[2].wait()
    for b in range(blocks):
        part = slice(b * LANES, (b + 1) * LANES)
        turned = lax.dot_general(eye, rows[part, :], ROW_BY_ROW, preferred_element_type=jnp.float32)
        for digits, values, target in (
            (share_of, turned[:width], inputs),
            (row_of, turned[width:], grads),
        ):
            digit = jnp.broadcast_to(digits[b : b + 1, :], (8, LANES))[None]
            values = values.reshape(-1, 8, LANES)
            for at in range(target.shape[0] // width):
                kept = jnp.where(digit == at, values, 0.0).reshape(width, LANES)
                target[at * width : (at + 1) * width, part] = kept.astype(target.dtype)
    product = lax.dot_general(
        grads[...], inputs[...], ROW_BY_ROW, preferred_element_type=jnp.float32
    )
    for p in range(sums.shape[0]):
        sums[p] = product[:, p * LANES : (p + 1) * LANES]

    scales = [1.0 / jnp.sqrt(size.astype(jnp.float32)) for size in sizes]
    low_half = lax.broadcasted_iota(jnp.int32, (doc_dev, LANES), 1) < width
    for m in range(width // 2):
        out = slice(m * LANES, (m + 1) * LANES)
        for s in range(0, tok_count, 2):
            first = sums[s // 2, pl.ds(2 * m, doc_dev, stride=width), :]
            second = sums[s // 2, pl.ds(2 * m + 1, doc_dev, stride=width), :]
            left = jnp.where(low_half, first, pltpu.roll(second, width, 1))
            right = jnp.where(low_half, pltpu.roll(first, width, 1), second)
            shares[s][:, out] = (left * scales[s]).astype(shares[s].dtype)
            shares[s + 1][:, out] = (right * scales[s + 1]).astype(shares[s + 1].dtype)


def feature_shares(proj_rows, doc_lengths, owner_map, tok_count):
    count, width = proj_rows.shape[0], proj_rows.shape[1] // 2
    doc_dev = doc_lengths.shape[1] // tok_count
    feat = width * width
    far = pl.BlockSpec(memory_space=pltpu.HBM)
    whole = pl.BlockSpec(memory_space=pltpu.VMEM)
    return pl.pallas_call(
        feature_kernel,
        out_shape=[
            jax.ShapeDtypeStruct((doc_dev, feat), jnp.bfloat16 if s else jnp.float32)
            for s in range(tok_count)
        ],
        in_specs=[far, far, far],
        out_specs=[whole] * tok_count,
        scratch_shapes=[
            pltpu.SMEM(doc_lengths.shape, jnp.int32),
            pltpu.SMEM(owner_map.shape, jnp.int32),
            pltpu.VMEM(proj_rows.shape, proj_rows.dtype),
            pltpu.VMEM((doc_dev * width, count), jnp.bfloat16),
            pltpu.VMEM((tok_count * width, count), jnp.bfloat16),
            pltpu.VMEM((tok_count // 2, doc_dev * width, LANES), jnp.float32),
            pltpu.SemaphoreType.DMA((3,)),
        ],
        compiler_params=pltpu.CompilerParams(vmem_limit_bytes=32 * 1024 * 1024),
        name="features",
    )(*(pltpu.with_memory_space_constraint(x, pltpu.HBM) for x in (doc_lengths, owner_map, proj_rows)))


def score_kernel(query, *refs):
    *blocks, scores = refs
    doc_dev = blocks[0].shape[0]
    features = jnp.concatenate([block[...] for block in blocks], axis=0)
    depth = features.shape[1] // 4
    products = sum(
        lax.dot_general(
            features[:, at : at + depth], query[:, at : at + depth], ROW_BY_ROW,
            preferred_element_type=jnp.float32,
        )
        for at in range(0, features.shape[1], depth)
    )
    parts = [products[i * doc_dev : (i + 1) * doc_dev] for i in range(len(blocks))]
    ex = lax.axis_index("ex")
    flip = 1
    while flip < len(blocks):
        swap = lax.rem(lax.div(ex, flip), 2) == 1
        parts = [jnp.where(swap, parts[i ^ flip], parts[i]) for i in range(len(parts))]
        flip *= 2
    scores[...] = jnp.concatenate(parts, axis=0).T


def block_scores(query_features, blocks):
    whole = pl.BlockSpec(memory_space=pltpu.VMEM)
    docs = len(blocks) * blocks[0].shape[0]
    return pl.pallas_call(
        score_kernel,
        out_shape=jax.ShapeDtypeStruct((query_features.shape[0], docs), jnp.float32),
        in_specs=[whole] * (1 + len(blocks)),
        out_specs=whole,
        compiler_params=pltpu.CompilerParams(vmem_limit_bytes=16 * 1024 * 1024),
        name="scores",
    )(*(pltpu.with_memory_space_constraint(x, pltpu.VMEM) for x in (query_features, *blocks)))


def exchange(block, axis, flip):
    return lax.ppermute(block, axis, [(i, i ^ flip) for i in range(lax.axis_size(axis))])


def body(proj_rows, query_features, doc_lengths, owner_map):
    tok_count = lax.axis_size("tok")
    shares = feature_shares(proj_rows, doc_lengths, owner_map, tok_count)
    total = shares[0]
    for shift in sorted(range(1, tok_count), key=lambda flip: (flip < 2, flip)):
        total = total + exchange(shares[shift], "tok", shift).astype(jnp.float32)
    features = total.astype(jnp.bfloat16)
    ex_count = lax.axis_size("ex")
    if ex_count != 8:
        gathered = lax.all_gather(features, "ex", axis=0, tiled=True)
        return jnp.einsum("qf,df->qd", query_features, gathered, preferred_element_type=jnp.float32)
    blocks = [features] + [None] * (ex_count - 1)
    for flip in (4, 2, 6):
        blocks[flip] = exchange(features, "ex", flip)
    for flip in (0, 4, 2, 6):
        blocks[flip + 1] = exchange(blocks[flip], "ex", 1)
    return block_scores(query_features, blocks)


def solution(mesh):
    placed = (P(("ex", "tok"), None), P("ex", None), P("ex", None), P("ex", None))
    return jax.shard_map(
        body, mesh=mesh, in_specs=placed, out_specs=P("ex", "tok"), check_vma=False
    )
```

```python
import jax
import jax.numpy as jnp
from jax import lax
from jax.experimental import pallas as pl
from jax.experimental.pallas import tpu as pltpu
from jax.sharding import PartitionSpec as P

LANES = 128
ROW_BY_ROW = (((1,), (1,)), ((), ()))


def feature_kernel(lengths_hbm, owners_hbm, rows_hbm, *refs):
    *shares, lengths, owners, rows, digits, grads, inputs, sums, arrived = refs
    count, width = rows.shape[0], rows.shape[1] // 2
    copies = [
        pltpu.make_async_copy(source, target, arrived.at[i])
        for i, (source, target) in enumerate(
            ((lengths_hbm, lengths), (owners_hbm, owners), (rows_hbm, rows))
        )
    ]
    for copy in copies:
        copy.start()
    docs, tok_count = lengths.shape[1], len(shares)
    doc_dev = docs // tok_count
    tok = lax.axis_index("tok")

    copies[0].wait()
    copies[1].wait()
    blocks, shift = count // LANES, doc_dev.bit_length() - 1
    token = lax.broadcasted_iota(jnp.int32, (blocks, LANES), 0) * LANES
    token = tok * count + token + lax.broadcasted_iota(jnp.int32, (blocks, LANES), 1)
    size_row = lax.broadcasted_iota(jnp.int32, (doc_dev, LANES), 0)
    size_slots = [((tok ^ s) << shift) + size_row for s in range(tok_count)]

    def place(k, carry):
        start, slot_of, *sizes = carry
        slot, length = owners[0, k], lengths[0, k]
        slot_of = jnp.where(token >= start, slot, slot_of)
        sizes = [jnp.where(at == slot, length, size) for at, size in zip(size_slots, sizes)]
        return (start + length, slot_of, *sizes)

    _, slot_of, *sizes = lax.fori_loop(
        0,
        docs,
        place,
        (jnp.int32(0), jnp.zeros((blocks, LANES), jnp.int32))
        + (jnp.ones((doc_dev, LANES), jnp.int32),) * tok_count,
        unroll=4,
    )
    digits[0] = (slot_of >> shift) ^ tok
    digits[1] = slot_of & (doc_dev - 1)

    eye = (
        lax.broadcasted_iota(jnp.int32, (2 * width, 2 * width), 0)
        == lax.broadcasted_iota(jnp.int32, (2 * width, 2 * width), 1)
    ).astype(rows.dtype)
    copies[2].wait()

    @pl.loop(0, blocks)
    def _(b):
        part = pl.ds(pl.multiple_of(b * LANES, LANES), LANES)
        turned = lax.dot_general(eye, rows[part, :], ROW_BY_ROW, preferred_element_type=jnp.float32)
        for i, target in enumerate((inputs, grads)):
            digit = jnp.broadcast_to(digits[i, pl.ds(b, 1), :], (8, LANES))[None]
            values = turned[i * width : (i + 1) * width].reshape(-1, 8, LANES)
            for at in range(target.shape[0] // width):
                kept = jnp.where(digit == at, values, 0.0).reshape(width, LANES)
                target[at * width : (at + 1) * width, part] = kept.astype(target.dtype)

    sums[...] = jnp.zeros_like(sums)
    depth = count // 4

    @pl.loop(0, 4)
    def _(c):
        part = pl.ds(pl.multiple_of(c * depth, depth), depth)
        product = lax.dot_general(
            grads[:, part], inputs[:, part], ROW_BY_ROW, preferred_element_type=jnp.float32
        )
        for p in range(sums.shape[0]):
            sums[p] += product[:, p * LANES : (p + 1) * LANES]

    scales = [1.0 / jnp.sqrt(size.astype(jnp.float32)) for size in sizes]
    low_half = lax.broadcasted_iota(jnp.int32, (doc_dev, LANES), 1) < width

    @pl.loop(0, width // 2, unroll=4)
    def _(m):
        out = pl.ds(pl.multiple_of(m * LANES, LANES), LANES)
        for s in range(0, tok_count, 2):
            first = sums[s // 2, pl.ds(2 * m, doc_dev, stride=width), :]
            second = sums[s // 2, pl.ds(2 * m + 1, doc_dev, stride=width), :]
            left = jnp.where(low_half, first, pltpu.roll(second, width, 1))
            right = jnp.where(low_half, pltpu.roll(first, width, 1), second)
            shares[s][:, out] = (left * scales[s]).astype(shares[s].dtype)
            shares[s + 1][:, out] = (right * scales[s + 1]).astype(shares[s + 1].dtype)


def feature_shares(proj_rows, doc_lengths, owner_map, tok_count):
    count, width = proj_rows.shape[0], proj_rows.shape[1] // 2
    doc_dev = doc_lengths.shape[1] // tok_count
    feat = width * width
    far = pl.BlockSpec(memory_space=pltpu.HBM)
    whole = pl.BlockSpec(memory_space=pltpu.VMEM)
    return pl.pallas_call(
        feature_kernel,
        out_shape=[
            jax.ShapeDtypeStruct((doc_dev, feat), jnp.bfloat16 if s else jnp.float32)
            for s in range(tok_count)
        ],
        in_specs=[far, far, far],
        out_specs=[whole] * tok_count,
        scratch_shapes=[
            pltpu.SMEM(doc_lengths.shape, jnp.int32),
            pltpu.SMEM(owner_map.shape, jnp.int32),
            pltpu.VMEM(proj_rows.shape, proj_rows.dtype),
            pltpu.VMEM((2, count // LANES, LANES), jnp.int32),
            pltpu.VMEM((doc_dev * width, count), jnp.bfloat16),
            pltpu.VMEM((tok_count * width, count), jnp.bfloat16),
            pltpu.VMEM((tok_count // 2, doc_dev * width, LANES), jnp.float32),
            pltpu.SemaphoreType.DMA((3,)),
        ],
        compiler_params=pltpu.CompilerParams(vmem_limit_bytes=32 * 1024 * 1024),
        name="features",
    )(*(pltpu.with_memory_space_constraint(x, pltpu.HBM) for x in (doc_lengths, owner_map, proj_rows)))


def score_kernel(query, *refs):
    *blocks, scores = refs
    doc_dev = blocks[0].shape[0]
    docs, depth = len(blocks) * doc_dev, query.shape[1] // 4

    def add(c, total):
        part = pl.ds(pl.multiple_of(c * depth, depth), depth)
        features = jnp.concatenate([block[:, part] for block in blocks], axis=0)
        return total + lax.dot_general(
            features, query[:, part], ROW_BY_ROW, preferred_element_type=jnp.float32
        )

    products = lax.fori_loop(0, 4, add, jnp.zeros((docs, query.shape[0]), jnp.float32))
    parts = [products[i * doc_dev : (i + 1) * doc_dev] for i in range(len(blocks))]
    ex = lax.axis_index("ex")
    flip = 1
    while flip < len(blocks):
        swap = lax.rem(lax.div(ex, flip), 2) == 1
        parts = [jnp.where(swap, parts[i ^ flip], parts[i]) for i in range(len(parts))]
        flip *= 2
    scores[...] = jnp.concatenate(parts, axis=0).T


def block_scores(query_features, blocks):
    whole = pl.BlockSpec(memory_space=pltpu.VMEM)
    docs = len(blocks) * blocks[0].shape[0]
    return pl.pallas_call(
        score_kernel,
        out_shape=jax.ShapeDtypeStruct((query_features.shape[0], docs), jnp.float32),
        in_specs=[whole] * (1 + len(blocks)),
        out_specs=whole,
        compiler_params=pltpu.CompilerParams(vmem_limit_bytes=16 * 1024 * 1024),
        name="scores",
    )(*(pltpu.with_memory_space_constraint(x, pltpu.VMEM) for x in (query_features, *blocks)))


def exchange(block, axis, flip):
    return lax.ppermute(block, axis, [(i, i ^ flip) for i in range(lax.axis_size(axis))])


def body(proj_rows, query_features, doc_lengths, owner_map):
    tok_count = lax.axis_size("tok")
    shares = feature_shares(proj_rows, doc_lengths, owner_map, tok_count)
    total = shares[0]
    for shift in sorted(range(1, tok_count), key=lambda flip: (flip < 2, flip)):
        total = total + exchange(shares[shift], "tok", shift).astype(jnp.float32)
    features = total.astype(jnp.bfloat16)
    ex_count = lax.axis_size("ex")
    if ex_count != 8:
        gathered = lax.all_gather(features, "ex", axis=0, tiled=True)
        return jnp.einsum("qf,df->qd", query_features, gathered, preferred_element_type=jnp.float32)
    blocks = [features] + [None] * (ex_count - 1)
    for flip in (4, 2, 6):
        blocks[flip] = exchange(features, "ex", flip)
    for flip in (0, 4, 2, 6):
        blocks[flip + 1] = exchange(blocks[flip], "ex", 1)
    return block_scores(query_features, blocks)


def solution(mesh):
    placed = (P(("ex", "tok"), None), P("ex", None), P("ex", None), P("ex", None))
    return jax.shard_map(
        body, mesh=mesh, in_specs=placed, out_specs=P("ex", "tok"), check_vma=False
    )
```

```python
import jax
import jax.numpy as jnp
from jax import lax
from jax.experimental import pallas as pl
from jax.experimental.pallas import tpu as pltpu
from jax.sharding import PartitionSpec as P

LANES = 128
ROW_BY_ROW = (((1,), (1,)), ((), ()))


def feature_kernel(lengths_hbm, owners_hbm, rows_hbm, *refs):
    *shares, lengths, owners, rows, grads, inputs, sums, arrived = refs
    count, width = rows.shape[0], rows.shape[1] // 2
    copies = [
        pltpu.make_async_copy(source, target, arrived.at[i])
        for i, (source, target) in enumerate(
            ((lengths_hbm, lengths), (owners_hbm, owners), (rows_hbm, rows))
        )
    ]
    for copy in copies:
        copy.start()
    docs, tok_count = lengths.shape[1], len(shares)
    doc_dev = docs // tok_count
    tok = lax.axis_index("tok")

    copies[0].wait()
    copies[1].wait()
    blocks, shift = count // LANES, doc_dev.bit_length() - 1
    token = lax.broadcasted_iota(jnp.int32, (blocks, LANES), 0) * LANES
    token = tok * count + token + lax.broadcasted_iota(jnp.int32, (blocks, LANES), 1)
    slot_of = jnp.zeros((blocks, LANES), jnp.int32)
    size_row = lax.broadcasted_iota(jnp.int32, (doc_dev, LANES), 0)
    size_slots = [((tok ^ s) << shift) + size_row for s in range(tok_count)]
    sizes = [jnp.ones((doc_dev, LANES), jnp.int32) for _ in shares]
    start = jnp.int32(0)
    for k in range(docs):
        slot, length = owners[0, k], lengths[0, k]
        slot_of = jnp.where(token >= start, slot, slot_of)
        sizes = [jnp.where(at == slot, length, size) for at, size in zip(size_slots, sizes)]
        start = start + length
    share_of, row_of = (slot_of >> shift) ^ tok, slot_of & (doc_dev - 1)

    pick = (
        lax.broadcasted_iota(jnp.int32, (width, 2 * width), 0) + width
        == lax.broadcasted_iota(jnp.int32, (width, 2 * width), 1)
    ).astype(rows.dtype)
    share_columns = share_of.T
    half = lax.broadcasted_iota(jnp.int32, (LANES, LANES), 1) // width
    copies[2].wait()
    for b in range(0, blocks, 2):
        both = slice(b * LANES, (b + 2) * LANES)
        turned = lax.dot_general(pick, rows[both, :], ROW_BY_ROW, preferred_element_type=jnp.float32)
        for c in (b, b + 1):
            part = slice(c * LANES, (c + 1) * LANES)
            digit = jnp.broadcast_to(row_of[c : c + 1, :], (8, LANES))[None]
            values = turned[:, (c - b) * LANES : (c - b + 1) * LANES].reshape(-1, 8, LANES)
            for at in range(doc_dev):
                kept = jnp.where(digit == at, values, 0.0).reshape(width, LANES)
                grads[at * width : (at + 1) * width, part] = kept.astype(grads.dtype)
            values = rows[part, :].astype(jnp.float32)
            values = jnp.where(half == 0, values, pltpu.roll(values, width, 1))
            digit = jnp.broadcast_to(share_columns[:, c : c + 1], (LANES, LANES)) - half
            for at in range(0, tok_count, 2):
                kept = jnp.where(digit == at, values, 0.0)
                inputs[part, at * width : at * width + LANES] = kept.astype(inputs.dtype)
    product = jnp.dot(grads[...], inputs[...], preferred_element_type=jnp.float32)
    for p in range(sums.shape[0]):
        sums[p] = product[:, p * LANES : (p + 1) * LANES]

    scales = [1.0 / jnp.sqrt(size.astype(jnp.float32)) for size in sizes]
    low_half = lax.broadcasted_iota(jnp.int32, (doc_dev, LANES), 1) < width
    for m in range(width // 2):
        out = slice(m * LANES, (m + 1) * LANES)
        for s in range(0, tok_count, 2):
            first = sums[s // 2, pl.ds(2 * m, doc_dev, stride=width), :]
            second = sums[s // 2, pl.ds(2 * m + 1, doc_dev, stride=width), :]
            left = jnp.where(low_half, first, pltpu.roll(second, width, 1))
            right = jnp.where(low_half, pltpu.roll(first, width, 1), second)
            shares[s][:, out] = (left * scales[s]).astype(shares[s].dtype)
            shares[s + 1][:, out] = (right * scales[s + 1]).astype(shares[s + 1].dtype)


def feature_shares(proj_rows, doc_lengths, owner_map, tok_count):
    count, width = proj_rows.shape[0], proj_rows.shape[1] // 2
    doc_dev = doc_lengths.shape[1] // tok_count
    feat = width * width
    far = pl.BlockSpec(memory_space=pltpu.HBM)
    whole = pl.BlockSpec(memory_space=pltpu.VMEM)
    return pl.pallas_call(
        feature_kernel,
        out_shape=[
            jax.ShapeDtypeStruct((doc_dev, feat), jnp.bfloat16 if s else jnp.float32)
            for s in range(tok_count)
        ],
        in_specs=[far, far, far],
        out_specs=[whole] * tok_count,
        scratch_shapes=[
            pltpu.SMEM(doc_lengths.shape, jnp.int32),
            pltpu.SMEM(owner_map.shape, jnp.int32),
            pltpu.VMEM(proj_rows.shape, proj_rows.dtype),
            pltpu.VMEM((doc_dev * width, count), jnp.bfloat16),
            pltpu.VMEM((count, tok_count * width), jnp.bfloat16),
            pltpu.VMEM((tok_count // 2, doc_dev * width, LANES), jnp.float32),
            pltpu.SemaphoreType.DMA((3,)),
        ],
        compiler_params=pltpu.CompilerParams(vmem_limit_bytes=32 * 1024 * 1024),
        name="features",
    )(*(pltpu.with_memory_space_constraint(x, pltpu.HBM) for x in (doc_lengths, owner_map, proj_rows)))


def turn_kernel(query, turned):
    turned[...] = query[...].T


def turned_query(query_features):
    whole = pl.BlockSpec(memory_space=pltpu.VMEM)
    shape = query_features.shape[::-1]
    return pl.pallas_call(
        turn_kernel,
        out_shape=jax.ShapeDtypeStruct(shape, query_features.dtype),
        in_specs=[whole],
        out_specs=whole,
        cost_estimate=pl.CostEstimate(flops=0, bytes_accessed=2 * query_features.nbytes, transcendentals=0),
        compiler_params=pltpu.CompilerParams(vmem_limit_bytes=16 * 1024 * 1024),
        name="turned_query",
    )(pltpu.with_memory_space_constraint(query_features, pltpu.VMEM))


def score_kernel(query, *refs):
    *blocks, scores = refs
    doc_dev = blocks[0].shape[0]
    features = jnp.concatenate([block[...] for block in blocks], axis=0)
    products = jnp.dot(features, query[...], preferred_element_type=jnp.float32)
    parts = [products[i * doc_dev : (i + 1) * doc_dev] for i in range(len(blocks))]
    ex = lax.axis_index("ex")
    flip = 1
    while flip < len(blocks):
        swap = lax.rem(lax.div(ex, flip), 2) == 1
        parts = [jnp.where(swap, parts[i ^ flip], parts[i]) for i in range(len(parts))]
        flip *= 2
    scores[...] = jnp.concatenate(parts, axis=0).T


def block_scores(query, blocks):
    whole = pl.BlockSpec(memory_space=pltpu.VMEM)
    docs = len(blocks) * blocks[0].shape[0]
    return pl.pallas_call(
        score_kernel,
        out_shape=jax.ShapeDtypeStruct((query.shape[1], docs), jnp.float32),
        in_specs=[whole] * (1 + len(blocks)),
        out_specs=whole,
        compiler_params=pltpu.CompilerParams(vmem_limit_bytes=16 * 1024 * 1024),
        name="scores",
    )(*(pltpu.with_memory_space_constraint(x, pltpu.VMEM) for x in (query, *blocks)))


def exchange(block, axis, flip):
    return lax.ppermute(block, axis, [(i, i ^ flip) for i in range(lax.axis_size(axis))])


def body(proj_rows, query_features, doc_lengths, owner_map):
    tok_count = lax.axis_size("tok")
    shares = feature_shares(proj_rows, doc_lengths, owner_map, tok_count)
    total = shares[0]
    for shift in sorted(range(1, tok_count), key=lambda flip: (flip < 2, flip)):
        total = total + exchange(shares[shift], "tok", shift).astype(jnp.float32)
    features = total.astype(jnp.bfloat16)
    ex_count = lax.axis_size("ex")
    if ex_count != 8:
        gathered = lax.all_gather(features, "ex", axis=0, tiled=True)
        return jnp.einsum("qf,df->qd", query_features, gathered, preferred_element_type=jnp.float32)
    blocks = [features] + [None] * (ex_count - 1)
    for flip in (4, 2, 6):
        blocks[flip] = exchange(features, "ex", flip)
    for flip in (0, 4, 2, 6):
        blocks[flip + 1] = exchange(blocks[flip], "ex", 1)
    return block_scores(turned_query(query_features), blocks)


def solution(mesh):
    placed = (P(("ex", "tok"), None), P("ex", None), P("ex", None), P("ex", None))
    return jax.shard_map(
        body, mesh=mesh, in_specs=placed, out_specs=P("ex", "tok"), check_vma=False
    )
```

```python
import jax
import jax.numpy as jnp
from jax import lax
from jax.experimental import pallas as pl
from jax.experimental.pallas import tpu as pltpu
from jax.sharding import PartitionSpec as P

LANES = 128
ROW_BY_ROW = (((1,), (1,)), ((), ()))


def feature_kernel(lengths_hbm, owners_hbm, rows_hbm, *refs):
    *shares, lengths, owners, rows, grads, inputs, arrived = refs
    count, width = rows.shape[0], rows.shape[1] // 2
    copies = [
        pltpu.make_async_copy(source, target, arrived.at[i])
        for i, (source, target) in enumerate(
            ((lengths_hbm, lengths), (owners_hbm, owners), (rows_hbm, rows))
        )
    ]
    for copy in copies:
        copy.start()
    docs, tok_count = lengths.shape[1], len(shares)
    doc_dev = docs // tok_count
    tok = lax.axis_index("tok")

    copies[0].wait()
    copies[1].wait()
    blocks, shift = count // LANES, doc_dev.bit_length() - 1
    token = lax.broadcasted_iota(jnp.int32, (blocks, LANES), 0) * LANES
    token = tok * count + token + lax.broadcasted_iota(jnp.int32, (blocks, LANES), 1)
    slot_of = jnp.zeros((blocks, LANES), jnp.int32)
    size_row = lax.broadcasted_iota(jnp.int32, (doc_dev, LANES), 0)
    size_slots = [((tok ^ s) << shift) + size_row for s in range(tok_count)]
    sizes = [jnp.ones((doc_dev, LANES), jnp.int32) for _ in shares]
    start = jnp.int32(0)
    for k in range(docs):
        slot, length = owners[0, k], lengths[0, k]
        slot_of = jnp.where(token >= start, slot, slot_of)
        sizes = [jnp.where(at == slot, length, size) for at, size in zip(size_slots, sizes)]
        start = start + length
    share_of, row_of = (slot_of >> shift) ^ tok, slot_of & (doc_dev - 1)

    spread = doc_dev * width
    pick = (
        lax.broadcasted_iota(jnp.int32, (spread, 2 * width), 0) // doc_dev + width
        == lax.broadcasted_iota(jnp.int32, (spread, 2 * width), 1)
    ).astype(rows.dtype)
    share_columns = share_of.T
    half = lax.broadcasted_iota(jnp.int32, (LANES, LANES), 1) // width
    copies[2].wait()
    for b in range(0, blocks, 2):
        both = slice(b * LANES, (b + 2) * LANES)
        turned = lax.dot_general(pick, rows[both, :], ROW_BY_ROW, preferred_element_type=jnp.float32)
        for c in (b, b + 1):
            part = slice(c * LANES, (c + 1) * LANES)
            values = turned[:, (c - b) * LANES : (c - b + 1) * LANES].reshape(width, doc_dev, LANES)
            kept = jnp.where((row_of[c : c + 1, :] == size_row)[None], values, 0.0)
            grads[:, part] = kept.reshape(spread, LANES).astype(grads.dtype)
            values = rows[part, :].astype(jnp.float32)
            values = jnp.where(half == 0, values, pltpu.roll(values, width, 1))
            digit = jnp.broadcast_to(share_columns[:, c : c + 1], (LANES, LANES)) - half
            for at in range(0, tok_count, 2):
                kept = jnp.where(digit == at, values, 0.0)
                inputs[part, at * width : at * width + LANES] = kept.astype(inputs.dtype)
    product = jnp.dot(grads[...], inputs[...], preferred_element_type=jnp.float32)

    scales = [1.0 / jnp.sqrt(size.astype(jnp.float32)) for size in sizes]
    low_half = lax.broadcasted_iota(jnp.int32, (doc_dev, LANES), 1) < width
    for m in range(width // 2):
        out = slice(m * LANES, (m + 1) * LANES)
        for s in range(0, tok_count, 2):
            pair = slice(s * width, s * width + LANES)
            first = product[2 * m * doc_dev : (2 * m + 1) * doc_dev, pair]
            second = product[(2 * m + 1) * doc_dev : (2 * m + 2) * doc_dev, pair]
            left = jnp.where(low_half, first, pltpu.roll(second, width, 1))
            right = jnp.where(low_half, pltpu.roll(first, width, 1), second)
            shares[s][:, out] = (left * scales[s]).astype(shares[s].dtype)
            shares[s + 1][:, out] = (right * scales[s + 1]).astype(shares[s + 1].dtype)


def feature_shares(proj_rows, doc_lengths, owner_map, tok_count):
    count, width = proj_rows.shape[0], proj_rows.shape[1] // 2
    doc_dev = doc_lengths.shape[1] // tok_count
    feat = width * width
    far = pl.BlockSpec(memory_space=pltpu.HBM)
    whole = pl.BlockSpec(memory_space=pltpu.VMEM)
    return pl.pallas_call(
        feature_kernel,
        out_shape=[
            jax.ShapeDtypeStruct((doc_dev, feat), jnp.bfloat16 if s else jnp.float32)
            for s in range(tok_count)
        ],
        in_specs=[far, far, far],
        out_specs=[whole] * tok_count,
        scratch_shapes=[
            pltpu.SMEM(doc_lengths.shape, jnp.int32),
            pltpu.SMEM(owner_map.shape, jnp.int32),
            pltpu.VMEM(proj_rows.shape, proj_rows.dtype),
            pltpu.VMEM((doc_dev * width, count), jnp.bfloat16),
            pltpu.VMEM((count, tok_count * width), jnp.bfloat16),
            pltpu.SemaphoreType.DMA((3,)),
        ],
        compiler_params=pltpu.CompilerParams(vmem_limit_bytes=32 * 1024 * 1024),
        name="features",
    )(*(pltpu.with_memory_space_constraint(x, pltpu.HBM) for x in (doc_lengths, owner_map, proj_rows)))


def score_kernel(query, *refs):
    *blocks, scores = refs
    doc_dev = blocks[0].shape[0]
    features = jnp.concatenate([block[...] for block in blocks], axis=0)
    depth = features.shape[1] // 4
    products = sum(
        lax.dot_general(
            features[:, at : at + depth], query[:, at : at + depth], ROW_BY_ROW,
            preferred_element_type=jnp.float32,
        )
        for at in range(0, features.shape[1], depth)
    )
    parts = [products[i * doc_dev : (i + 1) * doc_dev] for i in range(len(blocks))]
    ex = lax.axis_index("ex")
    flip = 1
    while flip < len(blocks):
        swap = lax.rem(lax.div(ex, flip), 2) == 1
        parts = [jnp.where(swap, parts[i ^ flip], parts[i]) for i in range(len(parts))]
        flip *= 2
    scores[...] = jnp.concatenate(parts, axis=0).T


def block_scores(query_features, blocks):
    whole = pl.BlockSpec(memory_space=pltpu.VMEM)
    docs = len(blocks) * blocks[0].shape[0]
    return pl.pallas_call(
        score_kernel,
        out_shape=jax.ShapeDtypeStruct((query_features.shape[0], docs), jnp.float32),
        in_specs=[whole] * (1 + len(blocks)),
        out_specs=whole,
        compiler_params=pltpu.CompilerParams(vmem_limit_bytes=16 * 1024 * 1024),
        name="scores",
    )(*(pltpu.with_memory_space_constraint(x, pltpu.VMEM) for x in (query_features, *blocks)))


def exchange(block, axis, flip):
    return lax.ppermute(block, axis, [(i, i ^ flip) for i in range(lax.axis_size(axis))])


def body(proj_rows, query_features, doc_lengths, owner_map):
    tok_count = lax.axis_size("tok")
    shares = feature_shares(proj_rows, doc_lengths, owner_map, tok_count)
    total = shares[0]
    for shift in sorted(range(1, tok_count), key=lambda flip: (flip < 2, flip)):
        total = total + exchange(shares[shift], "tok", shift).astype(jnp.float32)
    features = total.astype(jnp.bfloat16)
    ex_count = lax.axis_size("ex")
    if ex_count != 8:
        gathered = lax.all_gather(features, "ex", axis=0, tiled=True)
        return jnp.einsum("qf,df->qd", query_features, gathered, preferred_element_type=jnp.float32)
    blocks = [features] + [None] * (ex_count - 1)
    for flip in (4, 2, 6):
        blocks[flip] = exchange(features, "ex", flip)
    for flip in (0, 4, 2, 6):
        blocks[flip + 1] = exchange(blocks[flip], "ex", 1)
    return block_scores(query_features, blocks)


def solution(mesh):
    placed = (P(("ex", "tok"), None), P("ex", None), P("ex", None), P("ex", None))
    return jax.shard_map(
        body, mesh=mesh, in_specs=placed, out_specs=P("ex", "tok"), check_vma=False
    )
```

```python
import jax
import jax.numpy as jnp
from jax import lax
from jax.experimental import pallas as pl
from jax.experimental.pallas import tpu as pltpu
from jax.sharding import PartitionSpec as P

LANES = 128
ROW_BY_ROW = (((1,), (1,)), ((), ()))


def feature_kernel(lengths_hbm, owners_hbm, rows_hbm, *refs):
    *shares, lengths, owners, rows, grads, inputs, arrived = refs
    count, width = rows.shape[0], rows.shape[1] // 2
    piece = 2 * LANES
    pieces = [pl.ds(at, piece) for at in range(0, count, piece)]
    pairs = [(lengths_hbm, lengths), (owners_hbm, owners)]
    pairs += [(rows_hbm.at[part], rows.at[part]) for part in pieces]
    copies = [
        pltpu.make_async_copy(source, target, arrived.at[i])
        for i, (source, target) in enumerate(pairs)
    ]
    for copy in copies:
        copy.start()
    docs, tok_count = lengths.shape[1], len(shares)
    doc_dev = docs // tok_count
    tok = lax.axis_index("tok")

    copies[0].wait()
    copies[1].wait()
    blocks, shift = count // LANES, doc_dev.bit_length() - 1
    token = lax.broadcasted_iota(jnp.int32, (blocks, LANES), 0) * LANES
    token = tok * count + token + lax.broadcasted_iota(jnp.int32, (blocks, LANES), 1)
    slot_of = jnp.zeros((blocks, LANES), jnp.int32)
    size_row = lax.broadcasted_iota(jnp.int32, (doc_dev, LANES), 0)
    size_slots = [((tok ^ s) << shift) + size_row for s in range(tok_count)]
    sizes = [jnp.ones((doc_dev, LANES), jnp.int32) for _ in shares]
    start = jnp.int32(0)
    for k in range(docs):
        slot, length = owners[0, k], lengths[0, k]
        slot_of = jnp.where(token >= start, slot, slot_of)
        sizes = [jnp.where(at == slot, length, size) for at, size in zip(size_slots, sizes)]
        start = start + length
    share_of, row_of = (slot_of >> shift) ^ tok, slot_of & (doc_dev - 1)

    spread = doc_dev * width
    pick = (
        lax.broadcasted_iota(jnp.int32, (spread, 2 * width), 0) // doc_dev + width
        == lax.broadcasted_iota(jnp.int32, (spread, 2 * width), 1)
    ).astype(rows.dtype)
    share_columns = share_of.T
    half = lax.broadcasted_iota(jnp.int32, (LANES, LANES), 1) // width
    for b in range(0, blocks, 2):
        copies[2 + b // 2].wait()
        both = slice(b * LANES, (b + 2) * LANES)
        turned = lax.dot_general(pick, rows[both, :], ROW_BY_ROW, preferred_element_type=jnp.float32)
        for c in (b, b + 1):
            part = slice(c * LANES, (c + 1) * LANES)
            values = turned[:, (c - b) * LANES : (c - b + 1) * LANES].reshape(width, doc_dev, LANES)
            kept = jnp.where((row_of[c : c + 1, :] == size_row)[None], values, 0.0)
            grads[:, part] = kept.reshape(spread, LANES).astype(grads.dtype)
            values = rows[part, :].astype(jnp.float32)
            values = jnp.where(half == 0, values, pltpu.roll(values, width, 1))
            digit = jnp.broadcast_to(share_columns[:, c : c + 1], (LANES, LANES)) - half
            for at in range(0, tok_count, 2):
                kept = jnp.where(digit == at, values, 0.0)
                inputs[part, at * width : at * width + LANES] = kept.astype(inputs.dtype)
    product = jnp.dot(grads[...], inputs[...], preferred_element_type=jnp.float32)

    scales = [1.0 / jnp.sqrt(size.astype(jnp.float32)) for size in sizes]
    low_half = lax.broadcasted_iota(jnp.int32, (doc_dev, LANES), 1) < width
    for m in range(width // 2):
        out = slice(m * LANES, (m + 1) * LANES)
        for s in range(0, tok_count, 2):
            pair = slice(s * width, s * width + LANES)
            first = product[2 * m * doc_dev : (2 * m + 1) * doc_dev, pair]
            second = product[(2 * m + 1) * doc_dev : (2 * m + 2) * doc_dev, pair]
            left = jnp.where(low_half, first, pltpu.roll(second, width, 1))
            right = jnp.where(low_half, pltpu.roll(first, width, 1), second)
            shares[s][:, out] = (left * scales[s]).astype(shares[s].dtype)
            shares[s + 1][:, out] = (right * scales[s + 1]).astype(shares[s + 1].dtype)


def feature_shares(proj_rows, doc_lengths, owner_map, tok_count):
    count, width = proj_rows.shape[0], proj_rows.shape[1] // 2
    doc_dev = doc_lengths.shape[1] // tok_count
    feat = width * width
    far = pl.BlockSpec(memory_space=pltpu.HBM)
    whole = pl.BlockSpec(memory_space=pltpu.VMEM)
    return pl.pallas_call(
        feature_kernel,
        out_shape=[
            jax.ShapeDtypeStruct((doc_dev, feat), jnp.bfloat16 if s else jnp.float32)
            for s in range(tok_count)
        ],
        in_specs=[far, far, far],
        out_specs=[whole] * tok_count,
        scratch_shapes=[
            pltpu.SMEM(doc_lengths.shape, jnp.int32),
            pltpu.SMEM(owner_map.shape, jnp.int32),
            pltpu.VMEM(proj_rows.shape, proj_rows.dtype),
            pltpu.VMEM((doc_dev * width, count), jnp.bfloat16),
            pltpu.VMEM((count, tok_count * width), jnp.bfloat16),
            pltpu.SemaphoreType.DMA((2 + count // (2 * LANES),)),
        ],
        compiler_params=pltpu.CompilerParams(vmem_limit_bytes=32 * 1024 * 1024),
        name="features",
    )(*(pltpu.with_memory_space_constraint(x, pltpu.HBM) for x in (doc_lengths, owner_map, proj_rows)))


def score_kernel(query, *refs):
    *blocks, scores = refs
    doc_dev = blocks[0].shape[0]
    features = jnp.concatenate([block[...] for block in blocks], axis=0)
    depth = features.shape[1] // 4
    products = sum(
        lax.dot_general(
            features[:, at : at + depth], query[:, at : at + depth], ROW_BY_ROW,
            preferred_element_type=jnp.float32,
        )
        for at in range(0, features.shape[1], depth)
    )
    parts = [products[i * doc_dev : (i + 1) * doc_dev] for i in range(len(blocks))]
    ex = lax.axis_index("ex")
    flip = 1
    while flip < len(blocks):
        swap = lax.rem(lax.div(ex, flip), 2) == 1
        parts = [jnp.where(swap, parts[i ^ flip], parts[i]) for i in range(len(parts))]
        flip *= 2
    scores[...] = jnp.concatenate(parts, axis=0).T


def block_scores(query_features, blocks):
    whole = pl.BlockSpec(memory_space=pltpu.VMEM)
    docs = len(blocks) * blocks[0].shape[0]
    return pl.pallas_call(
        score_kernel,
        out_shape=jax.ShapeDtypeStruct((query_features.shape[0], docs), jnp.float32),
        in_specs=[whole] * (1 + len(blocks)),
        out_specs=whole,
        compiler_params=pltpu.CompilerParams(vmem_limit_bytes=16 * 1024 * 1024),
        name="scores",
    )(*(pltpu.with_memory_space_constraint(x, pltpu.VMEM) for x in (query_features, *blocks)))


def exchange(block, axis, flip):
    return lax.ppermute(block, axis, [(i, i ^ flip) for i in range(lax.axis_size(axis))])


def body(proj_rows, query_features, doc_lengths, owner_map):
    tok_count = lax.axis_size("tok")
    shares = feature_shares(proj_rows, doc_lengths, owner_map, tok_count)
    total = shares[0]
    for shift in sorted(range(1, tok_count), key=lambda flip: (flip < 2, flip)):
        total = total + exchange(shares[shift], "tok", shift).astype(jnp.float32)
    features = total.astype(jnp.bfloat16)
    ex_count = lax.axis_size("ex")
    if ex_count != 8:
        gathered = lax.all_gather(features, "ex", axis=0, tiled=True)
        return jnp.einsum("qf,df->qd", query_features, gathered, preferred_element_type=jnp.float32)
    blocks = [features] + [None] * (ex_count - 1)
    for flip in (4, 2, 6):
        blocks[flip] = exchange(features, "ex", flip)
    for flip in (0, 4, 2, 6):
        blocks[flip + 1] = exchange(blocks[flip], "ex", 1)
    return block_scores(query_features, blocks)


def solution(mesh):
    placed = (P(("ex", "tok"), None), P("ex", None), P("ex", None), P("ex", None))
    return jax.shard_map(
        body, mesh=mesh, in_specs=placed, out_specs=P("ex", "tok"), check_vma=False
    )
```

```python
import jax
import jax.numpy as jnp
from jax import lax
from jax.experimental import pallas as pl
from jax.experimental.pallas import tpu as pltpu
from jax.sharding import PartitionSpec as P

LANES = 128
ROW_BY_ROW = (((1,), (1,)), ((), ()))


def feature_kernel(lengths_hbm, owners_hbm, rows_hbm, *refs):
    *shares, lengths, owners, rows, grads, inputs, sums, arrived = refs
    count, width = rows.shape[0], rows.shape[1] // 2
    copies = [
        pltpu.make_async_copy(source, target, arrived.at[i])
        for i, (source, target) in enumerate(
            ((lengths_hbm, lengths), (owners_hbm, owners), (rows_hbm, rows))
        )
    ]
    for copy in copies:
        copy.start()
    docs, tok_count = lengths.shape[1], len(shares)
    doc_dev = docs // tok_count
    tok = lax.axis_index("tok")

    copies[0].wait()
    copies[1].wait()
    blocks, shift = count // LANES, doc_dev.bit_length() - 1
    token = lax.broadcasted_iota(jnp.int32, (blocks, LANES), 0) * LANES
    token = tok * count + token + lax.broadcasted_iota(jnp.int32, (blocks, LANES), 1)
    slot_of = jnp.zeros((blocks, LANES), jnp.int32)
    size_row = lax.broadcasted_iota(jnp.int32, (doc_dev, LANES), 0)
    size_slots = [((tok ^ s) << shift) + size_row for s in range(tok_count)]
    sizes = [jnp.ones((doc_dev, LANES), jnp.int32) for _ in shares]
    start = jnp.int32(0)
    for k in range(docs):
        slot, length = owners[0, k], lengths[0, k]
        slot_of = jnp.where(token >= start, slot, slot_of)
        sizes = [jnp.where(at == slot, length, size) for at, size in zip(size_slots, sizes)]
        start = start + length
    share_of, row_of = (slot_of >> shift) ^ tok, slot_of & (doc_dev - 1)

    pick = (
        lax.broadcasted_iota(jnp.int32, (width, 2 * width), 0) + width
        == lax.broadcasted_iota(jnp.int32, (width, 2 * width), 1)
    ).astype(rows.dtype)
    share_columns = share_of.T
    half = lax.broadcasted_iota(jnp.int32, (LANES, LANES), 1) // width
    copies[2].wait()
    product, run = 0.0, 4 * LANES
    for b in range(0, blocks, 2):
        both = slice(b * LANES, (b + 2) * LANES)
        turned = lax.dot_general(pick, rows[both, :], ROW_BY_ROW, preferred_element_type=jnp.float32)
        for c in (b, b + 1):
            part = slice(c * LANES, (c + 1) * LANES)
            digit = jnp.broadcast_to(row_of[c : c + 1, :], (8, LANES))[None]
            values = turned[:, (c - b) * LANES : (c - b + 1) * LANES].reshape(-1, 8, LANES)
            for at in range(doc_dev):
                kept = jnp.where(digit == at, values, 0.0).reshape(width, LANES)
                grads[at * width : (at + 1) * width, part] = kept.astype(grads.dtype)
            values = rows[part, :].astype(jnp.float32)
            values = jnp.where(half == 0, values, pltpu.roll(values, width, 1))
            digit = jnp.broadcast_to(share_columns[:, c : c + 1], (LANES, LANES)) - half
            for at in range(0, tok_count, 2):
                kept = jnp.where(digit == at, values, 0.0)
                inputs[part, at * width : at * width + LANES] = kept.astype(inputs.dtype)
        if (b + 2) * LANES % run == 0:
            done = slice((b + 2) * LANES - run, (b + 2) * LANES)
            product += jnp.dot(
                grads[:, done], inputs[done, :], preferred_element_type=jnp.float32
            )
    for p in range(sums.shape[0]):
        sums[p] = product[:, p * LANES : (p + 1) * LANES]

    scales = [1.0 / jnp.sqrt(size.astype(jnp.float32)) for size in sizes]
    low_half = lax.broadcasted_iota(jnp.int32, (doc_dev, LANES), 1) < width
    for m in range(width // 2):
        out = slice(m * LANES, (m + 1) * LANES)
        for s in range(0, tok_count, 2):
            first = sums[s // 2, pl.ds(2 * m, doc_dev, stride=width), :]
            second = sums[s // 2, pl.ds(2 * m + 1, doc_dev, stride=width), :]
            left = jnp.where(low_half, first, pltpu.roll(second, width, 1))
            right = jnp.where(low_half, pltpu.roll(first, width, 1), second)
            shares[s][:, out] = (left * scales[s]).astype(shares[s].dtype)
            shares[s + 1][:, out] = (right * scales[s + 1]).astype(shares[s + 1].dtype)


def feature_shares(proj_rows, doc_lengths, owner_map, tok_count):
    count, width = proj_rows.shape[0], proj_rows.shape[1] // 2
    doc_dev = doc_lengths.shape[1] // tok_count
    feat = width * width
    far = pl.BlockSpec(memory_space=pltpu.HBM)
    whole = pl.BlockSpec(memory_space=pltpu.VMEM)
    return pl.pallas_call(
        feature_kernel,
        out_shape=[
            jax.ShapeDtypeStruct((doc_dev, feat), jnp.bfloat16 if s else jnp.float32)
            for s in range(tok_count)
        ],
        in_specs=[far, far, far],
        out_specs=[whole] * tok_count,
        scratch_shapes=[
            pltpu.SMEM(doc_lengths.shape, jnp.int32),
            pltpu.SMEM(owner_map.shape, jnp.int32),
            pltpu.VMEM(proj_rows.shape, proj_rows.dtype),
            pltpu.VMEM((doc_dev * width, count), jnp.bfloat16),
            pltpu.VMEM((count, tok_count * width), jnp.bfloat16),
            pltpu.VMEM((tok_count // 2, doc_dev * width, LANES), jnp.float32),
            pltpu.SemaphoreType.DMA((3,)),
        ],
        compiler_params=pltpu.CompilerParams(vmem_limit_bytes=32 * 1024 * 1024),
        name="features",
    )(*(pltpu.with_memory_space_constraint(x, pltpu.HBM) for x in (doc_lengths, owner_map, proj_rows)))


def score_kernel(query, *refs):
    *blocks, scores = refs
    doc_dev = blocks[0].shape[0]
    features = jnp.concatenate([block[...] for block in blocks], axis=0)
    depth = features.shape[1] // 4
    products = sum(
        lax.dot_general(
            features[:, at : at + depth], query[:, at : at + depth], ROW_BY_ROW,
            preferred_element_type=jnp.float32,
        )
        for at in range(0, features.shape[1], depth)
    )
    parts = [products[i * doc_dev : (i + 1) * doc_dev] for i in range(len(blocks))]
    ex = lax.axis_index("ex")
    flip = 1
    while flip < len(blocks):
        swap = lax.rem(lax.div(ex, flip), 2) == 1
        parts = [jnp.where(swap, parts[i ^ flip], parts[i]) for i in range(len(parts))]
        flip *= 2
    scores[...] = jnp.concatenate(parts, axis=0).T


def block_scores(query_features, blocks):
    whole = pl.BlockSpec(memory_space=pltpu.VMEM)
    docs = len(blocks) * blocks[0].shape[0]
    return pl.pallas_call(
        score_kernel,
        out_shape=jax.ShapeDtypeStruct((query_features.shape[0], docs), jnp.float32),
        in_specs=[whole] * (1 + len(blocks)),
        out_specs=whole,
        compiler_params=pltpu.CompilerParams(vmem_limit_bytes=16 * 1024 * 1024),
        name="scores",
    )(*(pltpu.with_memory_space_constraint(x, pltpu.VMEM) for x in (query_features, *blocks)))


def exchange(block, axis, flip):
    return lax.ppermute(block, axis, [(i, i ^ flip) for i in range(lax.axis_size(axis))])


def body(proj_rows, query_features, doc_lengths, owner_map):
    tok_count = lax.axis_size("tok")
    shares = feature_shares(proj_rows, doc_lengths, owner_map, tok_count)
    total = shares[0]
    for shift in sorted(range(1, tok_count), key=lambda flip: (flip < 2, flip)):
        total = total + exchange(shares[shift], "tok", shift).astype(jnp.float32)
    features = total.astype(jnp.bfloat16)
    ex_count = lax.axis_size("ex")
    if ex_count != 8:
        gathered = lax.all_gather(features, "ex", axis=0, tiled=True)
        return jnp.einsum("qf,df->qd", query_features, gathered, preferred_element_type=jnp.float32)
    blocks = [features] + [None] * (ex_count - 1)
    for flip in (4, 2, 6):
        blocks[flip] = exchange(features, "ex", flip)
    for flip in (0, 4, 2, 6):
        blocks[flip + 1] = exchange(blocks[flip], "ex", 1)
    return block_scores(query_features, blocks)


def solution(mesh):
    placed = (P(("ex", "tok"), None), P("ex", None), P("ex", None), P("ex", None))
    return jax.shard_map(
        body, mesh=mesh, in_specs=placed, out_specs=P("ex", "tok"), check_vma=False
    )
```

```python
import jax
import jax.numpy as jnp
from jax import lax
from jax.experimental import pallas as pl
from jax.experimental.pallas import tpu as pltpu
from jax.sharding import PartitionSpec as P

LANES = 128
ROW_BY_ROW = (((1,), (1,)), ((), ()))


def feature_kernel(lengths_hbm, owners_hbm, rows_hbm, *refs):
    *shares, lengths, owners, rows, grads, inputs, sums, arrived = refs
    count, width = rows.shape[0], rows.shape[1] // 2
    copies = [
        pltpu.make_async_copy(source, target, arrived.at[i])
        for i, (source, target) in enumerate(
            ((lengths_hbm, lengths), (owners_hbm, owners), (rows_hbm, rows))
        )
    ]
    for copy in copies:
        copy.start()
    docs, tok_count = lengths.shape[1], len(shares)
    doc_dev = docs // tok_count
    tok = lax.axis_index("tok")

    copies[0].wait()
    copies[1].wait()
    blocks, shift = count // LANES, doc_dev.bit_length() - 1
    token = lax.broadcasted_iota(jnp.int32, (blocks, LANES), 0) * LANES
    token = tok * count + token + lax.broadcasted_iota(jnp.int32, (blocks, LANES), 1)
    slot_of = jnp.zeros((blocks, LANES), jnp.int32)
    size_row = lax.broadcasted_iota(jnp.int32, (doc_dev, LANES), 0)
    end = (tok == 0) | (tok == tok_count - 1)
    owner_of = [tok ^ jnp.where(end & (s % 2 == 1), tok_count - s, s) for s in range(tok_count)]
    size_slots = [(owner << shift) + size_row for owner in owner_of]
    sizes = [jnp.ones((doc_dev, LANES), jnp.int32) for _ in shares]
    start = jnp.int32(0)
    for k in range(docs):
        slot, length = owners[0, k], lengths[0, k]
        slot_of = jnp.where(token >= start, slot, slot_of)
        sizes = [jnp.where(at == slot, length, size) for at, size in zip(size_slots, sizes)]
        start = start + length
    share_of, row_of = (slot_of >> shift) ^ tok, slot_of & (doc_dev - 1)
    share_of = jnp.where(end & (share_of % 2 == 1), tok_count - share_of, share_of)

    eye = (
        lax.broadcasted_iota(jnp.int32, (2 * width, 2 * width), 0)
        == lax.broadcasted_iota(jnp.int32, (2 * width, 2 * width), 1)
    ).astype(rows.dtype)
    copies[2].wait()
    for b in range(blocks):
        part = slice(b * LANES, (b + 1) * LANES)
        turned = lax.dot_general(eye, rows[part, :], ROW_BY_ROW, preferred_element_type=jnp.float32)
        for digits, values, target in (
            (share_of, turned[:width], inputs),
            (row_of, turned[width:], grads),
        ):
            digit = jnp.broadcast_to(digits[b : b + 1, :], (8, LANES))[None]
            values = values.reshape(-1, 8, LANES)
            for at in range(target.shape[0] // width):
                kept = jnp.where(digit == at, values, 0.0).reshape(width, LANES)
                target[at * width : (at + 1) * width, part] = kept.astype(target.dtype)
    product = lax.dot_general(
        grads[...], inputs[...], ROW_BY_ROW, preferred_element_type=jnp.float32
    )
    for p in range(sums.shape[0]):
        sums[p] = product[:, p * LANES : (p + 1) * LANES]

    scales = [1.0 / jnp.sqrt(size.astype(jnp.float32)) for size in sizes]
    low_half = lax.broadcasted_iota(jnp.int32, (doc_dev, LANES), 1) < width
    for m in range(width // 2):
        out = slice(m * LANES, (m + 1) * LANES)
        for s in range(0, tok_count, 2):
            first = sums[s // 2, pl.ds(2 * m, doc_dev, stride=width), :]
            second = sums[s // 2, pl.ds(2 * m + 1, doc_dev, stride=width), :]
            left = jnp.where(low_half, first, pltpu.roll(second, width, 1))
            right = jnp.where(low_half, pltpu.roll(first, width, 1), second)
            shares[s][:, out] = (left * scales[s]).astype(shares[s].dtype)
            shares[s + 1][:, out] = (right * scales[s + 1]).astype(shares[s + 1].dtype)


def feature_shares(proj_rows, doc_lengths, owner_map, tok_count):
    count, width = proj_rows.shape[0], proj_rows.shape[1] // 2
    doc_dev = doc_lengths.shape[1] // tok_count
    feat = width * width
    far = pl.BlockSpec(memory_space=pltpu.HBM)
    whole = pl.BlockSpec(memory_space=pltpu.VMEM)
    return pl.pallas_call(
        feature_kernel,
        out_shape=[
            jax.ShapeDtypeStruct((doc_dev, feat), jnp.bfloat16 if s else jnp.float32)
            for s in range(tok_count)
        ],
        in_specs=[far, far, far],
        out_specs=[whole] * tok_count,
        scratch_shapes=[
            pltpu.SMEM(doc_lengths.shape, jnp.int32),
            pltpu.SMEM(owner_map.shape, jnp.int32),
            pltpu.VMEM(proj_rows.shape, proj_rows.dtype),
            pltpu.VMEM((doc_dev * width, count), jnp.bfloat16),
            pltpu.VMEM((tok_count * width, count), jnp.bfloat16),
            pltpu.VMEM((tok_count // 2, doc_dev * width, LANES), jnp.float32),
            pltpu.SemaphoreType.DMA((3,)),
        ],
        compiler_params=pltpu.CompilerParams(vmem_limit_bytes=32 * 1024 * 1024),
        name="features",
    )(*(pltpu.with_memory_space_constraint(x, pltpu.HBM) for x in (doc_lengths, owner_map, proj_rows)))


def score_kernel(query, *refs):
    *blocks, scores = refs
    doc_dev = blocks[0].shape[0]
    features = jnp.concatenate([block[...] for block in blocks], axis=0)
    depth = features.shape[1] // 4
    products = sum(
        lax.dot_general(
            features[:, at : at + depth], query[:, at : at + depth], ROW_BY_ROW,
            preferred_element_type=jnp.float32,
        )
        for at in range(0, features.shape[1], depth)
    )
    parts = [products[i * doc_dev : (i + 1) * doc_dev] for i in range(len(blocks))]
    ex = lax.axis_index("ex")
    flip = 1
    while flip < len(blocks):
        swap = lax.rem(lax.div(ex, flip), 2) == 1
        parts = [jnp.where(swap, parts[i ^ flip], parts[i]) for i in range(len(parts))]
        flip *= 2
    scores[...] = jnp.concatenate(parts, axis=0).T


def block_scores(query_features, blocks):
    whole = pl.BlockSpec(memory_space=pltpu.VMEM)
    docs = len(blocks) * blocks[0].shape[0]
    return pl.pallas_call(
        score_kernel,
        out_shape=jax.ShapeDtypeStruct((query_features.shape[0], docs), jnp.float32),
        in_specs=[whole] * (1 + len(blocks)),
        out_specs=whole,
        compiler_params=pltpu.CompilerParams(vmem_limit_bytes=16 * 1024 * 1024),
        name="scores",
    )(*(pltpu.with_memory_space_constraint(x, pltpu.VMEM) for x in (query_features, *blocks)))


def exchange(block, axis, flip):
    return lax.ppermute(block, axis, [(i, i ^ flip) for i in range(lax.axis_size(axis))])


def body(proj_rows, query_features, doc_lengths, owner_map):
    tok_count = lax.axis_size("tok")
    shares = feature_shares(proj_rows, doc_lengths, owner_map, tok_count)
    def send(block, *pairs):
        return lax.ppermute(block, "tok", pairs)

    own, first, across, last = shares
    end = (lax.axis_index("tok") % 3) == 0
    near = send(first, (0, 1), (1, 0), (2, 3), (3, 2))
    near, later = lax.optimization_barrier((near, last))
    near = near.astype(jnp.float32)
    inner = send(last, (1, 2), (2, 1)).astype(jnp.float32)
    inward = send(across, (0, 2), (3, 1)).astype(jnp.float32)
    passed = (across.astype(jnp.float32) + near).astype(jnp.bfloat16)
    outward = send(passed, (1, 3), (2, 0)).astype(jnp.float32)
    beside = send(later, (0, 1), (3, 2)).astype(jnp.float32)
    total = own + jnp.where(end, near, 0.0) + inner + inward + outward + beside
    features = total.astype(jnp.bfloat16)
    ex_count = lax.axis_size("ex")
    if ex_count != 8:
        gathered = lax.all_gather(features, "ex", axis=0, tiled=True)
        return jnp.einsum("qf,df->qd", query_features, gathered, preferred_element_type=jnp.float32)
    blocks = [features] + [None] * (ex_count - 1)
    for flip in (4, 2, 6):
        blocks[flip] = exchange(features, "ex", flip)
    for flip in (0, 4, 2, 6):
        blocks[flip + 1] = exchange(blocks[flip], "ex", 1)
    return block_scores(query_features, blocks)


def solution(mesh):
    placed = (P(("ex", "tok"), None), P("ex", None), P("ex", None), P("ex", None))
    return jax.shard_map(
        body, mesh=mesh, in_specs=placed, out_specs=P("ex", "tok"), check_vma=False
    )
```

```python
import jax
import jax.numpy as jnp
from jax import lax
from jax.experimental import pallas as pl
from jax.experimental.pallas import tpu as pltpu
from jax.sharding import PartitionSpec as P

LANES = 128
ROW_BY_ROW = (((1,), (1,)), ((), ()))


def feature_kernel(lengths_hbm, owners_hbm, rows_hbm, *refs):
    *shares, lengths, owners, rows, grads, inputs, sums, arrived = refs
    count, width = rows.shape[0], rows.shape[1] // 2
    copies = [
        pltpu.make_async_copy(source, target, arrived.at[i])
        for i, (source, target) in enumerate(
            ((lengths_hbm, lengths), (owners_hbm, owners), (rows_hbm, rows))
        )
    ]
    for copy in copies:
        copy.start()
    docs, tok_count = lengths.shape[1], len(shares)
    doc_dev = docs // tok_count
    tok = lax.axis_index("tok")

    copies[0].wait()
    copies[1].wait()
    blocks, shift = count // LANES, doc_dev.bit_length() - 1
    token = lax.broadcasted_iota(jnp.int32, (blocks, LANES), 0) * LANES
    token = tok * count + token + lax.broadcasted_iota(jnp.int32, (blocks, LANES), 1)
    slot_of = jnp.zeros((blocks, LANES), jnp.int32)
    size_row = lax.broadcasted_iota(jnp.int32, (doc_dev, LANES), 0)
    size_slots = [((tok ^ s) << shift) + size_row for s in range(tok_count)]
    sizes = [jnp.ones((doc_dev, LANES), jnp.int32) for _ in shares]
    start = jnp.int32(0)
    for k in range(docs):
        slot, length = owners[0, k], lengths[0, k]
        slot_of = jnp.where(token >= start, slot, slot_of)
        sizes = [jnp.where(at == slot, length, size) for at, size in zip(size_slots, sizes)]
        start = start + length
    share_of, row_of = (slot_of >> shift) ^ tok, slot_of & (doc_dev - 1)

    eye = (
        lax.broadcasted_iota(jnp.int32, (2 * width, 2 * width), 0)
        == lax.broadcasted_iota(jnp.int32, (2 * width, 2 * width), 1)
    ).astype(rows.dtype)
    copies[2].wait()
    for b in range(blocks):
        part = slice(b * LANES, (b + 1) * LANES)
        turned = lax.dot_general(eye, rows[part, :], ROW_BY_ROW, preferred_element_type=jnp.float32)
        for digits, values, target in (
            (share_of, turned[:width], inputs),
            (row_of, turned[width:], grads),
        ):
            digit = jnp.broadcast_to(digits[b : b + 1, :], (8, LANES))[None]
            values = values.reshape(-1, 8, LANES)
            for at in range(target.shape[0] // width):
                kept = jnp.where(digit == at, values, 0.0).reshape(width, LANES)
                target[at * width : (at + 1) * width, part] = kept.astype(target.dtype)
    product = lax.dot_general(
        grads[...], inputs[...], ROW_BY_ROW, preferred_element_type=jnp.float32
    )
    for p in range(sums.shape[0]):
        sums[p] = product[:, p * LANES : (p + 1) * LANES]

    scales = [1.0 / jnp.sqrt(size.astype(jnp.float32)) for size in sizes]
    low_half = lax.broadcasted_iota(jnp.int32, (doc_dev, LANES), 1) < width
    for m in range(width // 2):
        out = slice(m * LANES, (m + 1) * LANES)
        for s in range(0, tok_count, 2):
            first = sums[s // 2, pl.ds(2 * m, doc_dev, stride=width), :]
            second = sums[s // 2, pl.ds(2 * m + 1, doc_dev, stride=width), :]
            left = jnp.where(low_half, first, pltpu.roll(second, width, 1))
            right = jnp.where(low_half, pltpu.roll(first, width, 1), second)
            shares[s][:, out] = (left * scales[s]).astype(shares[s].dtype)
            shares[s + 1][:, out] = (right * scales[s + 1]).astype(shares[s + 1].dtype)


def feature_shares(proj_rows, doc_lengths, owner_map, tok_count):
    count, width = proj_rows.shape[0], proj_rows.shape[1] // 2
    doc_dev = doc_lengths.shape[1] // tok_count
    feat = width * width
    far = pl.BlockSpec(memory_space=pltpu.HBM)
    whole = pl.BlockSpec(memory_space=pltpu.VMEM)
    return pl.pallas_call(
        feature_kernel,
        out_shape=[
            jax.ShapeDtypeStruct((doc_dev, feat), jnp.bfloat16 if s else jnp.float32)
            for s in range(tok_count)
        ],
        in_specs=[far, far, far],
        out_specs=[whole] * tok_count,
        scratch_shapes=[
            pltpu.SMEM(doc_lengths.shape, jnp.int32),
            pltpu.SMEM(owner_map.shape, jnp.int32),
            pltpu.VMEM(proj_rows.shape, proj_rows.dtype),
            pltpu.VMEM((doc_dev * width, count), jnp.bfloat16),
            pltpu.VMEM((tok_count * width, count), jnp.bfloat16),
            pltpu.VMEM((tok_count // 2, doc_dev * width, LANES), jnp.float32),
            pltpu.SemaphoreType.DMA((3,)),
        ],
        compiler_params=pltpu.CompilerParams(vmem_limit_bytes=32 * 1024 * 1024),
        name="features",
    )(*(pltpu.with_memory_space_constraint(x, pltpu.HBM) for x in (doc_lengths, owner_map, proj_rows)))


def score_kernel(query, *refs):
    *blocks, scores = refs
    doc_dev = blocks[0].shape[0]
    features = jnp.concatenate([block[...] for block in blocks], axis=0)
    products = lax.dot_general(
        features, query[...], ROW_BY_ROW, preferred_element_type=jnp.float32
    )
    own, second, first, third, own_next, second_next, first_next, third_next = (
        products[i * doc_dev : (i + 1) * doc_dev] for i in range(len(blocks))
    )
    ex = lax.axis_index("ex")
    odd = lax.rem(ex, 2) == 1
    parts = [
        own,
        own_next,
        jnp.where(odd, first, second),
        jnp.where(odd, second_next, first_next),
        jnp.where(odd, second, first),
        jnp.where(odd, first_next, second_next),
        third,
        third_next,
    ]
    flip = 1
    while flip < len(parts):
        swap = lax.rem(lax.div(ex, flip), 2) == 1
        parts = [jnp.where(swap, parts[i ^ flip], parts[i]) for i in range(len(parts))]
        flip *= 2
    scores[...] = jnp.concatenate(parts, axis=0).T


def block_scores(query_features, held, held_next):
    whole = pl.BlockSpec(memory_space=pltpu.VMEM)
    operands = (query_features, *held, *held_next)
    docs = (len(operands) - 1) * held[0].shape[0]
    return pl.pallas_call(
        score_kernel,
        out_shape=jax.ShapeDtypeStruct((query_features.shape[0], docs), jnp.float32),
        in_specs=[whole] * len(operands),
        out_specs=whole,
        compiler_params=pltpu.CompilerParams(vmem_limit_bytes=16 * 1024 * 1024),
        name="scores",
    )(*(pltpu.with_memory_space_constraint(x, pltpu.VMEM) for x in operands))


def exchange(block, axis, flip):
    return lax.ppermute(block, axis, [(i, i ^ flip) for i in range(lax.axis_size(axis))])


def body(proj_rows, query_features, doc_lengths, owner_map):
    tok_count = lax.axis_size("tok")
    shares = feature_shares(proj_rows, doc_lengths, owner_map, tok_count)
    total = shares[0]
    for shift in sorted(range(1, tok_count), key=lambda flip: (flip < 2, flip)):
        total = total + exchange(shares[shift], "tok", shift).astype(jnp.float32)
    features = total.astype(jnp.bfloat16)
    ex_count = lax.axis_size("ex")
    if ex_count != 8:
        gathered = lax.all_gather(features, "ex", axis=0, tiled=True)
        return jnp.einsum("qf,df->qd", query_features, gathered, preferred_element_type=jnp.float32)
    turns = [[(i, i ^ (first if i % 2 else 6 - first)) for i in range(ex_count)] for first in (2, 4)]
    third = exchange(features, "ex", 6)
    first, second = (lax.ppermute(features, "ex", turn) for turn in turns)
    held = (features, second, first, third)
    return block_scores(query_features, held, [exchange(block, "ex", 1) for block in held])


def solution(mesh):
    placed = (P(("ex", "tok"), None), P("ex", None), P("ex", None), P("ex", None))
    return jax.shard_map(
        body, mesh=mesh, in_specs=placed, out_specs=P("ex", "tok"), check_vma=False
    )
```

```python
import jax
import jax.numpy as jnp
from jax import lax
from jax.experimental import pallas as pl
from jax.experimental.pallas import tpu as pltpu
from jax.sharding import PartitionSpec as P

LANES = 128
ROW_BY_ROW = (((1,), (1,)), ((), ()))


def feature_kernel(lengths_hbm, owners_hbm, rows_hbm, *refs):
    *shares, lengths, owners, rows, grads, inputs, sums, arrived = refs
    count, width = rows.shape[0], rows.shape[1] // 2
    copies = [
        pltpu.make_async_copy(source, target, arrived.at[i])
        for i, (source, target) in enumerate(
            ((lengths_hbm, lengths), (owners_hbm, owners), (rows_hbm, rows))
        )
    ]
    for copy in copies:
        copy.start()
    docs, tok_count = lengths.shape[1], len(shares)
    doc_dev = docs // tok_count
    tok = lax.axis_index("tok")

    copies[0].wait()
    copies[1].wait()
    blocks, shift = count // LANES, doc_dev.bit_length() - 1
    token = lax.broadcasted_iota(jnp.int32, (blocks, LANES), 0) * LANES
    token = tok * count + token + lax.broadcasted_iota(jnp.int32, (blocks, LANES), 1)
    slot_of = jnp.zeros((blocks, LANES), jnp.int32)
    size_row = lax.broadcasted_iota(jnp.int32, (doc_dev, LANES), 0)
    size_slots = [((tok ^ s) << shift) + size_row for s in range(tok_count)]
    sizes = [jnp.ones((doc_dev, LANES), jnp.int32) for _ in shares]
    start = jnp.int32(0)
    for k in range(docs):
        slot, length = owners[0, k], lengths[0, k]
        slot_of = jnp.where(token >= start, slot, slot_of)
        sizes = [jnp.where(at == slot, length, size) for at, size in zip(size_slots, sizes)]
        start = start + length
    share_of, row_of = (slot_of >> shift) ^ tok, slot_of & (doc_dev - 1)

    eye = (
        lax.broadcasted_iota(jnp.int32, (2 * width, 2 * width), 0)
        == lax.broadcasted_iota(jnp.int32, (2 * width, 2 * width), 1)
    ).astype(rows.dtype)
    copies[2].wait()
    for b in range(blocks):
        part = slice(b * LANES, (b + 1) * LANES)
        turned = lax.dot_general(eye, rows[part, :], ROW_BY_ROW, preferred_element_type=jnp.float32)
        turned = turned.astype(rows.dtype)
        for digits, values, target in (
            (share_of, turned[:width], inputs),
            (row_of, turned[width:], grads),
        ):
            digit = jnp.broadcast_to(digits[b : b + 1, :], (16, LANES))
            values = values.reshape(-1, 16, LANES)
            for at in range(target.shape[0] // width):
                mask = jnp.where(digit == at, 1.0, 0.0).astype(values.dtype)
                target[at * width : (at + 1) * width, part] = (values * mask[None]).reshape(width, LANES)
    product = lax.dot_general(
        grads[...], inputs[...], ROW_BY_ROW, preferred_element_type=jnp.float32
    )
    for p in range(sums.shape[0]):
        sums[p] = product[:, p * LANES : (p + 1) * LANES]

    scales = [1.0 / jnp.sqrt(size.astype(jnp.float32)) for size in sizes]
    low_half = lax.broadcasted_iota(jnp.int32, (doc_dev, LANES), 1) < width
    for m in range(width // 2):
        out = slice(m * LANES, (m + 1) * LANES)
        for s in range(0, tok_count, 2):
            first = sums[s // 2, pl.ds(2 * m, doc_dev, stride=width), :]
            second = sums[s // 2, pl.ds(2 * m + 1, doc_dev, stride=width), :]
            left = jnp.where(low_half, first, pltpu.roll(second, width, 1))
            right = jnp.where(low_half, pltpu.roll(first, width, 1), second)
            shares[s][:, out] = (left * scales[s]).astype(shares[s].dtype)
            shares[s + 1][:, out] = (right * scales[s + 1]).astype(shares[s + 1].dtype)


def feature_shares(proj_rows, doc_lengths, owner_map, tok_count):
    count, width = proj_rows.shape[0], proj_rows.shape[1] // 2
    doc_dev = doc_lengths.shape[1] // tok_count
    feat = width * width
    far = pl.BlockSpec(memory_space=pltpu.HBM)
    whole = pl.BlockSpec(memory_space=pltpu.VMEM)
    return pl.pallas_call(
        feature_kernel,
        out_shape=[
            jax.ShapeDtypeStruct((doc_dev, feat), jnp.bfloat16 if s else jnp.float32)
            for s in range(tok_count)
        ],
        in_specs=[far, far, far],
        out_specs=[whole] * tok_count,
        scratch_shapes=[
            pltpu.SMEM(doc_lengths.shape, jnp.int32),
            pltpu.SMEM(owner_map.shape, jnp.int32),
            pltpu.VMEM(proj_rows.shape, proj_rows.dtype),
            pltpu.VMEM((doc_dev * width, count), jnp.bfloat16),
            pltpu.VMEM((tok_count * width, count), jnp.bfloat16),
            pltpu.VMEM((tok_count // 2, doc_dev * width, LANES), jnp.float32),
            pltpu.SemaphoreType.DMA((3,)),
        ],
        compiler_params=pltpu.CompilerParams(vmem_limit_bytes=32 * 1024 * 1024),
        name="features",
    )(*(pltpu.with_memory_space_constraint(x, pltpu.HBM) for x in (doc_lengths, owner_map, proj_rows)))


def score_kernel(query, *refs):
    *blocks, scores = refs
    doc_dev = blocks[0].shape[0]
    features = jnp.concatenate([block[...] for block in blocks], axis=0)
    products = lax.dot_general(
        features, query[...], ROW_BY_ROW, preferred_element_type=jnp.float32
    )
    own, second, first, third, own_next, second_next, first_next, third_next = (
        products[i * doc_dev : (i + 1) * doc_dev] for i in range(len(blocks))
    )
    ex = lax.axis_index("ex")
    odd = lax.rem(ex, 2) == 1
    parts = [
        own,
        own_next,
        jnp.where(odd, first, second),
        jnp.where(odd, second_next, first_next),
        jnp.where(odd, second, first),
        jnp.where(odd, first_next, second_next),
        third,
        third_next,
    ]
    flip = 1
    while flip < len(parts):
        swap = lax.rem(lax.div(ex, flip), 2) == 1
        parts = [jnp.where(swap, parts[i ^ flip], parts[i]) for i in range(len(parts))]
        flip *= 2
    scores[...] = jnp.concatenate(parts, axis=0).T


def block_scores(query_features, held, held_next):
    whole = pl.BlockSpec(memory_space=pltpu.VMEM)
    operands = (query_features, *held, *held_next)
    docs = (len(operands) - 1) * held[0].shape[0]
    return pl.pallas_call(
        score_kernel,
        out_shape=jax.ShapeDtypeStruct((query_features.shape[0], docs), jnp.float32),
        in_specs=[whole] * len(operands),
        out_specs=whole,
        compiler_params=pltpu.CompilerParams(vmem_limit_bytes=16 * 1024 * 1024),
        name="scores",
    )(*(pltpu.with_memory_space_constraint(x, pltpu.VMEM) for x in operands))


def exchange(block, axis, flip):
    return lax.ppermute(block, axis, [(i, i ^ flip) for i in range(lax.axis_size(axis))])


def body(proj_rows, query_features, doc_lengths, owner_map):
    tok_count = lax.axis_size("tok")
    shares = feature_shares(proj_rows, doc_lengths, owner_map, tok_count)
    total = shares[0]
    for shift in sorted(range(1, tok_count), key=lambda flip: (flip < 2, flip)):
        total = total + exchange(shares[shift], "tok", shift).astype(jnp.float32)
    features = total.astype(jnp.bfloat16)
    ex_count = lax.axis_size("ex")
    if ex_count != 8:
        gathered = lax.all_gather(features, "ex", axis=0, tiled=True)
        return jnp.einsum("qf,df->qd", query_features, gathered, preferred_element_type=jnp.float32)
    turns = [[(i, i ^ (first if i % 2 else 6 - first)) for i in range(ex_count)] for first in (2, 4)]
    third = exchange(features, "ex", 6)
    first, second = (lax.ppermute(features, "ex", turn) for turn in turns)
    held = (features, second, first, third)
    return block_scores(query_features, held, [exchange(block, "ex", 1) for block in held])


def solution(mesh):
    placed = (P(("ex", "tok"), None), P("ex", None), P("ex", None), P("ex", None))
    return jax.shard_map(
        body, mesh=mesh, in_specs=placed, out_specs=P("ex", "tok"), check_vma=False
    )
```

```python
import jax
import jax.numpy as jnp
from jax import lax
from jax.experimental import pallas as pl
from jax.experimental.pallas import tpu as pltpu
from jax.sharding import PartitionSpec as P

LANES = 128
ROW_BY_ROW = (((1,), (1,)), ((), ()))


def feature_kernel(lengths_hbm, owners_hbm, rows_hbm, *refs):
    *shares, lengths, owners, rows, grads, inputs, sums, arrived = refs
    count, width = rows.shape[0], rows.shape[1] // 2
    copies = [
        pltpu.make_async_copy(source, target, arrived.at[i])
        for i, (source, target) in enumerate(
            ((lengths_hbm, lengths), (owners_hbm, owners), (rows_hbm, rows))
        )
    ]
    for copy in copies:
        copy.start()
    docs, tok_count = lengths.shape[1], len(shares)
    doc_dev = docs // tok_count
    tok = lax.axis_index("tok")

    copies[0].wait()
    copies[1].wait()
    blocks, shift = count // LANES, doc_dev.bit_length() - 1
    token = lax.broadcasted_iota(jnp.int32, (blocks, LANES), 0) * LANES
    token = tok * count + token + lax.broadcasted_iota(jnp.int32, (blocks, LANES), 1)
    slot_of = jnp.zeros((blocks, LANES), jnp.int32)
    size_row = lax.broadcasted_iota(jnp.int32, (doc_dev, LANES), 0)
    size_slots = [(lax.rem(tok + s, tok_count) << shift) + size_row for s in range(tok_count)]
    sizes = [jnp.ones((doc_dev, LANES), jnp.int32) for _ in shares]
    start = jnp.int32(0)
    for k in range(docs):
        slot, length = owners[0, k], lengths[0, k]
        slot_of = jnp.where(token >= start, slot, slot_of)
        sizes = [jnp.where(at == slot, length, size) for at, size in zip(size_slots, sizes)]
        start = start + length
    share_of = (slot_of >> shift) - tok
    share_of, row_of = jnp.where(share_of < 0, share_of + tok_count, share_of), slot_of & (doc_dev - 1)

    eye = (
        lax.broadcasted_iota(jnp.int32, (2 * width, 2 * width), 0)
        == lax.broadcasted_iota(jnp.int32, (2 * width, 2 * width), 1)
    ).astype(rows.dtype)
    copies[2].wait()
    for b in range(blocks):
        part = slice(b * LANES, (b + 1) * LANES)
        turned = lax.dot_general(eye, rows[part, :], ROW_BY_ROW, preferred_element_type=jnp.float32)
        for digits, values, target in (
            (share_of, turned[:width], inputs),
            (row_of, turned[width:], grads),
        ):
            digit = jnp.broadcast_to(digits[b : b + 1, :], (8, LANES))[None]
            values = values.reshape(-1, 8, LANES)
            for at in range(target.shape[0] // width):
                kept = jnp.where(digit == at, values, 0.0).reshape(width, LANES)
                target[at * width : (at + 1) * width, part] = kept.astype(target.dtype)
    product = lax.dot_general(
        grads[...], inputs[...], ROW_BY_ROW, preferred_element_type=jnp.float32
    )
    for p in range(sums.shape[0]):
        sums[p] = product[:, p * LANES : (p + 1) * LANES]

    scales = [1.0 / jnp.sqrt(size.astype(jnp.float32)) for size in sizes]
    low_half = lax.broadcasted_iota(jnp.int32, (doc_dev, LANES), 1) < width
    for m in range(width // 2):
        out = slice(m * LANES, (m + 1) * LANES)
        for s in range(0, tok_count, 2):
            first = sums[s // 2, pl.ds(2 * m, doc_dev, stride=width), :]
            second = sums[s // 2, pl.ds(2 * m + 1, doc_dev, stride=width), :]
            left = jnp.where(low_half, first, pltpu.roll(second, width, 1))
            right = jnp.where(low_half, pltpu.roll(first, width, 1), second)
            shares[s][:, out] = (left * scales[s]).astype(shares[s].dtype)
            shares[s + 1][:, out] = (right * scales[s + 1]).astype(shares[s + 1].dtype)


def feature_shares(proj_rows, doc_lengths, owner_map, tok_count):
    count, width = proj_rows.shape[0], proj_rows.shape[1] // 2
    doc_dev = doc_lengths.shape[1] // tok_count
    feat = width * width
    far = pl.BlockSpec(memory_space=pltpu.HBM)
    whole = pl.BlockSpec(memory_space=pltpu.VMEM)
    return pl.pallas_call(
        feature_kernel,
        out_shape=[
            jax.ShapeDtypeStruct((doc_dev, feat), jnp.bfloat16 if s else jnp.float32)
            for s in range(tok_count)
        ],
        in_specs=[far, far, far],
        out_specs=[whole] * tok_count,
        scratch_shapes=[
            pltpu.SMEM(doc_lengths.shape, jnp.int32),
            pltpu.SMEM(owner_map.shape, jnp.int32),
            pltpu.VMEM(proj_rows.shape, proj_rows.dtype),
            pltpu.VMEM((doc_dev * width, count), jnp.bfloat16),
            pltpu.VMEM((tok_count * width, count), jnp.bfloat16),
            pltpu.VMEM((tok_count // 2, doc_dev * width, LANES), jnp.float32),
            pltpu.SemaphoreType.DMA((3,)),
        ],
        compiler_params=pltpu.CompilerParams(vmem_limit_bytes=32 * 1024 * 1024),
        name="features",
    )(*(pltpu.with_memory_space_constraint(x, pltpu.HBM) for x in (doc_lengths, owner_map, proj_rows)))


def score_kernel(query, *refs):
    *blocks, scores = refs
    doc_dev = blocks[0].shape[0]
    features = jnp.concatenate([block[...] for block in blocks], axis=0)
    products = lax.dot_general(
        features, query[...], ROW_BY_ROW, preferred_element_type=jnp.float32
    )
    own, second, first, third, own_next, second_next, first_next, third_next = (
        products[i * doc_dev : (i + 1) * doc_dev] for i in range(len(blocks))
    )
    ex = lax.axis_index("ex")
    odd = lax.rem(ex, 2) == 1
    parts = [
        own,
        own_next,
        jnp.where(odd, first, second),
        jnp.where(odd, second_next, first_next),
        jnp.where(odd, second, first),
        jnp.where(odd, first_next, second_next),
        third,
        third_next,
    ]
    flip = 1
    while flip < len(parts):
        swap = lax.rem(lax.div(ex, flip), 2) == 1
        parts = [jnp.where(swap, parts[i ^ flip], parts[i]) for i in range(len(parts))]
        flip *= 2
    scores[...] = jnp.concatenate(parts, axis=0).T


def block_scores(query_features, held, held_next):
    whole = pl.BlockSpec(memory_space=pltpu.VMEM)
    operands = (query_features, *held, *held_next)
    docs = (len(operands) - 1) * held[0].shape[0]
    return pl.pallas_call(
        score_kernel,
        out_shape=jax.ShapeDtypeStruct((query_features.shape[0], docs), jnp.float32),
        in_specs=[whole] * len(operands),
        out_specs=whole,
        compiler_params=pltpu.CompilerParams(vmem_limit_bytes=16 * 1024 * 1024),
        name="scores",
    )(*(pltpu.with_memory_space_constraint(x, pltpu.VMEM) for x in operands))


def exchange(block, axis, flip):
    return lax.ppermute(block, axis, [(i, i ^ flip) for i in range(lax.axis_size(axis))])


def body(proj_rows, query_features, doc_lengths, owner_map):
    tok_count = lax.axis_size("tok")
    shares = feature_shares(proj_rows, doc_lengths, owner_map, tok_count)
    total = shares[0]
    for shift in sorted(range(1, tok_count), key=lambda shift: (2 * shift != tok_count, shift)):
        pairs = [(i, (i + shift) % tok_count) for i in range(tok_count)]
        total = total + lax.ppermute(shares[shift], "tok", pairs).astype(jnp.float32)
    features = total.astype(jnp.bfloat16)
    ex_count = lax.axis_size("ex")
    if ex_count != 8:
        gathered = lax.all_gather(features, "ex", axis=0, tiled=True)
        return jnp.einsum("qf,df->qd", query_features, gathered, preferred_element_type=jnp.float32)
    turns = [[(i, i ^ (first if i % 2 else 6 - first)) for i in range(ex_count)] for first in (2, 4)]
    third = exchange(features, "ex", 6)
    first, second = (lax.ppermute(features, "ex", turn) for turn in turns)
    held = (features, second, first, third)
    return block_scores(query_features, held, [exchange(block, "ex", 1) for block in held])


def solution(mesh):
    placed = (P(("ex", "tok"), None), P("ex", None), P("ex", None), P("ex", None))
    return jax.shard_map(
        body, mesh=mesh, in_specs=placed, out_specs=P("ex", "tok"), check_vma=False
    )
```

```python
import jax
import jax.numpy as jnp
from jax import lax
from jax.experimental import pallas as pl
from jax.experimental.pallas import tpu as pltpu
from jax.sharding import PartitionSpec as P

LANES = 128
ROW_BY_ROW = (((1,), (1,)), ((), ()))


def feature_kernel(lengths_hbm, owners_hbm, rows_hbm, *refs):
    *shares, lengths, owners, rows, grads, inputs, sums, arrived = refs
    count, width = rows.shape[0], rows.shape[1] // 2
    copies = [
        pltpu.make_async_copy(source, target, arrived.at[i])
        for i, (source, target) in enumerate(
            ((lengths_hbm, lengths), (owners_hbm, owners), (rows_hbm, rows))
        )
    ]
    for copy in copies:
        copy.start()
    docs, tok_count = lengths.shape[1], len(shares)
    doc_dev = docs // tok_count
    tok = lax.axis_index("tok")

    copies[0].wait()
    copies[1].wait()
    blocks, shift = count // LANES, doc_dev.bit_length() - 1
    token = lax.broadcasted_iota(jnp.int32, (blocks, LANES), 0) * LANES
    token = tok * count + token + lax.broadcasted_iota(jnp.int32, (blocks, LANES), 1)
    slot_of = jnp.zeros((blocks, LANES), jnp.int32)
    size_row = lax.broadcasted_iota(jnp.int32, (doc_dev, LANES), 0)
    odd = lax.rem(lax.axis_index("ex"), 2) == 1
    turn = tok_count - 1
    flips = [0] + [jnp.where(odd, s, s % turn + 1) for s in range(1, tok_count)]
    size_slots = [((tok ^ flip) << shift) + size_row for flip in flips]
    sizes = [jnp.ones((doc_dev, LANES), jnp.int32) for _ in shares]
    start = jnp.int32(0)
    for k in range(docs):
        slot, length = owners[0, k], lengths[0, k]
        slot_of = jnp.where(token >= start, slot, slot_of)
        sizes = [jnp.where(at == slot, length, size) for at, size in zip(size_slots, sizes)]
        start = start + length
    flip_of, row_of = (slot_of >> shift) ^ tok, slot_of & (doc_dev - 1)
    share_of = jnp.zeros_like(flip_of)
    for s in range(1, tok_count):
        share_of = jnp.where(flip_of == flips[s], s, share_of)

    eye = (
        lax.broadcasted_iota(jnp.int32, (2 * width, 2 * width), 0)
        == lax.broadcasted_iota(jnp.int32, (2 * width, 2 * width), 1)
    ).astype(rows.dtype)
    copies[2].wait()
    for b in range(blocks):
        part = slice(b * LANES, (b + 1) * LANES)
        turned = lax.dot_general(eye, rows[part, :], ROW_BY_ROW, preferred_element_type=jnp.float32)
        for digits, values, target in (
            (share_of, turned[:width], inputs),
            (row_of, turned[width:], grads),
        ):
            digit = jnp.broadcast_to(digits[b : b + 1, :], (8, LANES))[None]
            values = values.reshape(-1, 8, LANES)
            for at in range(target.shape[0] // width):
                kept = jnp.where(digit == at, values, 0.0).reshape(width, LANES)
                target[at * width : (at + 1) * width, part] = kept.astype(target.dtype)
    product = lax.dot_general(
        grads[...], inputs[...], ROW_BY_ROW, preferred_element_type=jnp.float32
    )
    for p in range(sums.shape[0]):
        sums[p] = product[:, p * LANES : (p + 1) * LANES]

    scales = [1.0 / jnp.sqrt(size.astype(jnp.float32)) for size in sizes]
    low_half = lax.broadcasted_iota(jnp.int32, (doc_dev, LANES), 1) < width
    for m in range(width // 2):
        out = slice(m * LANES, (m + 1) * LANES)
        for s in range(0, tok_count, 2):
            first = sums[s // 2, pl.ds(2 * m, doc_dev, stride=width), :]
            second = sums[s // 2, pl.ds(2 * m + 1, doc_dev, stride=width), :]
            left = jnp.where(low_half, first, pltpu.roll(second, width, 1))
            right = jnp.where(low_half, pltpu.roll(first, width, 1), second)
            shares[s][:, out] = (left * scales[s]).astype(shares[s].dtype)
            shares[s + 1][:, out] = (right * scales[s + 1]).astype(shares[s + 1].dtype)


def feature_shares(proj_rows, doc_lengths, owner_map, tok_count):
    count, width = proj_rows.shape[0], proj_rows.shape[1] // 2
    doc_dev = doc_lengths.shape[1] // tok_count
    feat = width * width
    far = pl.BlockSpec(memory_space=pltpu.HBM)
    whole = pl.BlockSpec(memory_space=pltpu.VMEM)
    return pl.pallas_call(
        feature_kernel,
        out_shape=[
            jax.ShapeDtypeStruct((doc_dev, feat), jnp.bfloat16 if s else jnp.float32)
            for s in range(tok_count)
        ],
        in_specs=[far, far, far],
        out_specs=[whole] * tok_count,
        scratch_shapes=[
            pltpu.SMEM(doc_lengths.shape, jnp.int32),
            pltpu.SMEM(owner_map.shape, jnp.int32),
            pltpu.VMEM(proj_rows.shape, proj_rows.dtype),
            pltpu.VMEM((doc_dev * width, count), jnp.bfloat16),
            pltpu.VMEM((tok_count * width, count), jnp.bfloat16),
            pltpu.VMEM((tok_count // 2, doc_dev * width, LANES), jnp.float32),
            pltpu.SemaphoreType.DMA((3,)),
        ],
        compiler_params=pltpu.CompilerParams(vmem_limit_bytes=32 * 1024 * 1024),
        name="features",
    )(*(pltpu.with_memory_space_constraint(x, pltpu.HBM) for x in (doc_lengths, owner_map, proj_rows)))


def score_kernel(query, *refs):
    *blocks, scores = refs
    doc_dev = blocks[0].shape[0]
    features = jnp.concatenate([block[...] for block in blocks], axis=0)
    products = lax.dot_general(
        features, query[...], ROW_BY_ROW, preferred_element_type=jnp.float32
    )
    own, second, first, third, own_next, second_next, first_next, third_next = (
        products[i * doc_dev : (i + 1) * doc_dev] for i in range(len(blocks))
    )
    ex = lax.axis_index("ex")
    odd = lax.rem(ex, 2) == 1
    parts = [
        own,
        own_next,
        jnp.where(odd, first, second),
        jnp.where(odd, second_next, first_next),
        jnp.where(odd, second, first),
        jnp.where(odd, first_next, second_next),
        third,
        third_next,
    ]
    flip = 1
    while flip < len(parts):
        swap = lax.rem(lax.div(ex, flip), 2) == 1
        parts = [jnp.where(swap, parts[i ^ flip], parts[i]) for i in range(len(parts))]
        flip *= 2
    scores[...] = jnp.concatenate(parts, axis=0).T


def block_scores(query_features, held, held_next):
    whole = pl.BlockSpec(memory_space=pltpu.VMEM)
    operands = (query_features, *held, *held_next)
    docs = (len(operands) - 1) * held[0].shape[0]
    return pl.pallas_call(
        score_kernel,
        out_shape=jax.ShapeDtypeStruct((query_features.shape[0], docs), jnp.float32),
        in_specs=[whole] * len(operands),
        out_specs=whole,
        compiler_params=pltpu.CompilerParams(vmem_limit_bytes=16 * 1024 * 1024),
        name="scores",
    )(*(pltpu.with_memory_space_constraint(x, pltpu.VMEM) for x in operands))


def exchange(block, axis, flip):
    return lax.ppermute(block, axis, [(i, i ^ flip) for i in range(lax.axis_size(axis))])


def body(proj_rows, query_features, doc_lengths, owner_map):
    tok_count = lax.axis_size("tok")
    shares = feature_shares(proj_rows, doc_lengths, owner_map, tok_count)
    total = shares[0]
    groups = range(lax.axis_size("ex"))
    for s in range(1, tok_count):
        flips = [s % (tok_count - 1) + 1, s]
        pairs = [
            (e * tok_count + i, e * tok_count + (i ^ flips[e % 2])) for e in groups for i in range(tok_count)
        ]
        total = total + lax.ppermute(shares[s], ("ex", "tok"), pairs).astype(jnp.float32)
    features = total.astype(jnp.bfloat16)
    ex_count = lax.axis_size("ex")
    if ex_count != 8:
        gathered = lax.all_gather(features, "ex", axis=0, tiled=True)
        return jnp.einsum("qf,df->qd", query_features, gathered, preferred_element_type=jnp.float32)
    turns = [[(i, i ^ (first if i % 2 else 6 - first)) for i in range(ex_count)] for first in (2, 4)]
    third = exchange(features, "ex", 6)
    first, second = (lax.ppermute(features, "ex", turn) for turn in turns)
    held = (features, second, first, third)
    return block_scores(query_features, held, [exchange(block, "ex", 1) for block in held])


def solution(mesh):
    placed = (P(("ex", "tok"), None), P("ex", None), P("ex", None), P("ex", None))
    return jax.shard_map(
        body, mesh=mesh, in_specs=placed, out_specs=P("ex", "tok"), check_vma=False
    )
```

```python
import jax
import jax.numpy as jnp
from jax import lax
from jax.experimental import pallas as pl
from jax.experimental.pallas import tpu as pltpu
from jax.sharding import PartitionSpec as P

LANES = 128
ROW_BY_ROW = (((1,), (1,)), ((), ()))


def feature_kernel(lengths_hbm, owners_hbm, rows_hbm, *refs):
    *shares, lengths, owners, rows, grads, inputs, sums, arrived = refs
    count, width = rows.shape[0], rows.shape[1] // 2
    copies = [
        pltpu.make_async_copy(source, target, arrived.at[i])
        for i, (source, target) in enumerate(
            ((lengths_hbm, lengths), (owners_hbm, owners), (rows_hbm, rows))
        )
    ]
    for copy in copies:
        copy.start()
    docs, tok_count = lengths.shape[1], len(shares)
    doc_dev = docs // tok_count
    tok = lax.axis_index("tok")

    copies[0].wait()
    copies[1].wait()
    blocks, shift = count // LANES, doc_dev.bit_length() - 1
    token = lax.broadcasted_iota(jnp.int32, (blocks, LANES), 0) * LANES
    token = tok * count + token + lax.broadcasted_iota(jnp.int32, (blocks, LANES), 1)
    slot_of = jnp.zeros((blocks, LANES), jnp.int32)
    size_row = lax.broadcasted_iota(jnp.int32, (doc_dev, LANES), 0)
    size_slots = [((tok ^ s) << shift) + size_row for s in range(tok_count)]
    sizes = [jnp.ones((doc_dev, LANES), jnp.int32) for _ in shares]
    start = jnp.int32(0)
    for k in range(docs):
        slot, length = owners[0, k], lengths[0, k]
        slot_of = jnp.where(token >= start, slot, slot_of)
        sizes = [jnp.where(at == slot, length, size) for at, size in zip(size_slots, sizes)]
        start = start + length
    share_of, row_of = (slot_of >> shift) ^ tok, slot_of & (doc_dev - 1)

    eye = (
        lax.broadcasted_iota(jnp.int32, (2 * width, 2 * width), 0)
        == lax.broadcasted_iota(jnp.int32, (2 * width, 2 * width), 1)
    ).astype(rows.dtype)
    copies[2].wait()
    for b in range(blocks):
        part = slice(b * LANES, (b + 1) * LANES)
        turned = lax.dot_general(eye, rows[part, :], ROW_BY_ROW, preferred_element_type=jnp.float32)
        for digits, values, target in (
            (share_of, turned[:width], inputs),
            (row_of, turned[width:], grads),
        ):
            digit = jnp.broadcast_to(digits[b : b + 1, :], (8, LANES))[None]
            values = values.reshape(-1, 8, LANES)
            for at in range(target.shape[0] // width):
                kept = jnp.where(digit == at, values, 0.0).reshape(width, LANES)
                target[at * width : (at + 1) * width, part] = kept.astype(target.dtype)
    product = lax.dot_general(
        grads[...], inputs[...], ROW_BY_ROW, preferred_element_type=jnp.float32
    )
    for p in range(sums.shape[0]):
        sums[p] = product[:, p * LANES : (p + 1) * LANES]

    scales = [1.0 / jnp.sqrt(size.astype(jnp.float32)) for size in sizes]
    low_half = lax.broadcasted_iota(jnp.int32, (doc_dev, LANES), 1) < width
    for m in range(width // 2):
        out = slice(m * LANES, (m + 1) * LANES)
        for s in range(0, tok_count, 2):
            first = sums[s // 2, pl.ds(2 * m, doc_dev, stride=width), :]
            second = sums[s // 2, pl.ds(2 * m + 1, doc_dev, stride=width), :]
            left = jnp.where(low_half, first, pltpu.roll(second, width, 1))
            right = jnp.where(low_half, pltpu.roll(first, width, 1), second)
            shares[s][:, out] = (left * scales[s]).astype(shares[s].dtype)
            shares[s + 1][:, out] = (right * scales[s + 1]).astype(shares[s + 1].dtype)


def feature_shares(proj_rows, doc_lengths, owner_map, tok_count):
    count, width = proj_rows.shape[0], proj_rows.shape[1] // 2
    doc_dev = doc_lengths.shape[1] // tok_count
    feat = width * width
    far = pl.BlockSpec(memory_space=pltpu.HBM)
    whole = pl.BlockSpec(memory_space=pltpu.VMEM)
    return pl.pallas_call(
        feature_kernel,
        out_shape=[
            jax.ShapeDtypeStruct((doc_dev, feat), jnp.bfloat16 if s else jnp.float32)
            for s in range(tok_count)
        ],
        in_specs=[far, far, far],
        out_specs=[whole] * tok_count,
        scratch_shapes=[
            pltpu.SMEM(doc_lengths.shape, jnp.int32),
            pltpu.SMEM(owner_map.shape, jnp.int32),
            pltpu.VMEM(proj_rows.shape, proj_rows.dtype),
            pltpu.VMEM((doc_dev * width, count), jnp.bfloat16),
            pltpu.VMEM((tok_count * width, count), jnp.bfloat16),
            pltpu.VMEM((tok_count // 2, doc_dev * width, LANES), jnp.float32),
            pltpu.SemaphoreType.DMA((3,)),
        ],
        compiler_params=pltpu.CompilerParams(vmem_limit_bytes=32 * 1024 * 1024),
        name="features",
    )(*(pltpu.with_memory_space_constraint(x, pltpu.HBM) for x in (doc_lengths, owner_map, proj_rows)))


def block_products(query, blocks):
    features = jnp.concatenate([block[...] for block in blocks], axis=0)
    return lax.dot_general(features, query[...], ROW_BY_ROW, preferred_element_type=jnp.float32)


def early_kernel(query, *refs):
    *blocks, products = refs
    products[...] = block_products(query, blocks)


def score_kernel(query, early, *refs):
    *blocks, scores = refs
    doc_dev = blocks[0].shape[0]
    late = block_products(query, blocks)
    own, second, first, third, own_next, third_next = (
        early[i : i + doc_dev, :] for i in range(0, early.shape[0], doc_dev)
    )
    second_next, first_next = late[:doc_dev], late[doc_dev:]
    ex = lax.axis_index("ex")
    odd = lax.rem(ex, 2) == 1
    parts = [
        own,
        own_next,
        jnp.where(odd, first, second),
        jnp.where(odd, second_next, first_next),
        jnp.where(odd, second, first),
        jnp.where(odd, first_next, second_next),
        third,
        third_next,
    ]
    flip = 1
    while flip < len(parts):
        swap = lax.rem(lax.div(ex, flip), 2) == 1
        parts = [jnp.where(swap, parts[i ^ flip], parts[i]) for i in range(len(parts))]
        flip *= 2
    scores[...] = jnp.concatenate(parts, axis=0).T


def call_on_vmem(kernel, name, shape, *operands):
    whole = pl.BlockSpec(memory_space=pltpu.VMEM)
    moved = sum(x.nbytes for x in operands)
    return pl.pallas_call(
        kernel,
        out_shape=jax.ShapeDtypeStruct(shape, jnp.float32),
        in_specs=[whole] * len(operands),
        out_specs=whole,
        cost_estimate=pl.CostEstimate(flops=0, bytes_accessed=moved, transcendentals=0),
        compiler_params=pltpu.CompilerParams(vmem_limit_bytes=16 * 1024 * 1024),
        name=name,
    )(*(pltpu.with_memory_space_constraint(x, pltpu.VMEM) for x in operands))


def block_scores(query, held, held_next):
    own_next, second_next, first_next, third_next = held_next
    ready = (*held, own_next, third_next)
    doc_dev, queries = held[0].shape[0], query.shape[0]
    early = call_on_vmem(
        early_kernel, "early_products", (len(ready) * doc_dev, queries), query, *ready
    )
    shape = (queries, (len(ready) + 2) * doc_dev)
    return call_on_vmem(score_kernel, "scores", shape, query, early, second_next, first_next)


def exchange(block, axis, flip):
    return lax.ppermute(block, axis, [(i, i ^ flip) for i in range(lax.axis_size(axis))])


def body(proj_rows, query_features, doc_lengths, owner_map):
    tok_count = lax.axis_size("tok")
    shares = feature_shares(proj_rows, doc_lengths, owner_map, tok_count)
    total = shares[0]
    for shift in sorted(range(1, tok_count), key=lambda flip: (flip < 2, flip)):
        total = total + exchange(shares[shift], "tok", shift).astype(jnp.float32)
    features = total.astype(jnp.bfloat16)
    ex_count = lax.axis_size("ex")
    if ex_count != 8:
        gathered = lax.all_gather(features, "ex", axis=0, tiled=True)
        return jnp.einsum("qf,df->qd", query_features, gathered, preferred_element_type=jnp.float32)
    turns = [[(i, i ^ (first if i % 2 else 6 - first)) for i in range(ex_count)] for first in (2, 4)]
    third = exchange(features, "ex", 6)
    first, second = (lax.ppermute(features, "ex", turn) for turn in turns)
    held = (features, second, first, third)
    return block_scores(query_features, held, [exchange(block, "ex", 1) for block in held])


def solution(mesh):
    placed = (P(("ex", "tok"), None), P("ex", None), P("ex", None), P("ex", None))
    return jax.shard_map(
        body, mesh=mesh, in_specs=placed, out_specs=P("ex", "tok"), check_vma=False
    )
```

```python
import jax
import jax.numpy as jnp
from jax import lax
from jax.experimental import pallas as pl
from jax.experimental.pallas import tpu as pltpu
from jax.sharding import PartitionSpec as P

LANES = 128
ROW_BY_ROW = (((1,), (1,)), ((), ()))


def feature_kernel(lengths_hbm, owners_hbm, rows_hbm, query_hbm, *refs):
    *shares, query, lengths, owners, rows, grads, inputs, sums, arrived = refs
    count, width = rows.shape[0], rows.shape[1] // 2
    copies = [
        pltpu.make_async_copy(source, target, arrived.at[i])
        for i, (source, target) in enumerate(
            ((lengths_hbm, lengths), (owners_hbm, owners), (rows_hbm, rows), (query_hbm, query))
        )
    ]
    for copy in copies[:3]:
        copy.start()
    docs, tok_count = lengths.shape[1], len(shares)
    doc_dev = docs // tok_count
    tok = lax.axis_index("tok")

    copies[0].wait()
    copies[1].wait()
    blocks, shift = count // LANES, doc_dev.bit_length() - 1
    token = lax.broadcasted_iota(jnp.int32, (blocks, LANES), 0) * LANES
    token = tok * count + token + lax.broadcasted_iota(jnp.int32, (blocks, LANES), 1)
    slot_of = jnp.zeros((blocks, LANES), jnp.int32)
    size_row = lax.broadcasted_iota(jnp.int32, (doc_dev, LANES), 0)
    size_slots = [((tok ^ s) << shift) + size_row for s in range(tok_count)]
    sizes = [jnp.ones((doc_dev, LANES), jnp.int32) for _ in shares]
    start = jnp.int32(0)
    for k in range(docs):
        slot, length = owners[0, k], lengths[0, k]
        slot_of = jnp.where(token >= start, slot, slot_of)
        sizes = [jnp.where(at == slot, length, size) for at, size in zip(size_slots, sizes)]
        start = start + length
    share_of, row_of = (slot_of >> shift) ^ tok, slot_of & (doc_dev - 1)

    eye = (
        lax.broadcasted_iota(jnp.int32, (2 * width, 2 * width), 0)
        == lax.broadcasted_iota(jnp.int32, (2 * width, 2 * width), 1)
    ).astype(rows.dtype)
    copies[2].wait()
    copies[3].start()
    for b in range(blocks):
        part = slice(b * LANES, (b + 1) * LANES)
        turned = lax.dot_general(eye, rows[part, :], ROW_BY_ROW, preferred_element_type=jnp.float32)
        for digits, values, target in (
            (share_of, turned[:width], inputs),
            (row_of, turned[width:], grads),
        ):
            digit = jnp.broadcast_to(digits[b : b + 1, :], (8, LANES))[None]
            values = values.reshape(-1, 8, LANES)
            for at in range(target.shape[0] // width):
                kept = jnp.where(digit == at, values, 0.0).reshape(width, LANES)
                target[at * width : (at + 1) * width, part] = kept.astype(target.dtype)
    product = lax.dot_general(
        grads[...], inputs[...], ROW_BY_ROW, preferred_element_type=jnp.float32
    )
    for p in range(sums.shape[0]):
        sums[p] = product[:, p * LANES : (p + 1) * LANES]

    scales = [1.0 / jnp.sqrt(size.astype(jnp.float32)) for size in sizes]
    low_half = lax.broadcasted_iota(jnp.int32, (doc_dev, LANES), 1) < width
    for m in range(width // 2):
        out = slice(m * LANES, (m + 1) * LANES)
        for s in range(0, tok_count, 2):
            first = sums[s // 2, pl.ds(2 * m, doc_dev, stride=width), :]
            second = sums[s // 2, pl.ds(2 * m + 1, doc_dev, stride=width), :]
            left = jnp.where(low_half, first, pltpu.roll(second, width, 1))
            right = jnp.where(low_half, pltpu.roll(first, width, 1), second)
            shares[s][:, out] = (left * scales[s]).astype(shares[s].dtype)
            shares[s + 1][:, out] = (right * scales[s + 1]).astype(shares[s + 1].dtype)
    copies[3].wait()


def feature_shares(proj_rows, query_features, doc_lengths, owner_map, tok_count):
    count, width = proj_rows.shape[0], proj_rows.shape[1] // 2
    doc_dev = doc_lengths.shape[1] // tok_count
    feat = width * width
    far = pl.BlockSpec(memory_space=pltpu.HBM)
    whole = pl.BlockSpec(memory_space=pltpu.VMEM)
    return pl.pallas_call(
        feature_kernel,
        out_shape=[
            jax.ShapeDtypeStruct((doc_dev, feat), jnp.bfloat16 if s else jnp.float32)
            for s in range(tok_count)
        ]
        + [jax.ShapeDtypeStruct(query_features.shape, query_features.dtype)],
        in_specs=[far] * 4,
        out_specs=[whole] * (tok_count + 1),
        scratch_shapes=[
            pltpu.SMEM(doc_lengths.shape, jnp.int32),
            pltpu.SMEM(owner_map.shape, jnp.int32),
            pltpu.VMEM(proj_rows.shape, proj_rows.dtype),
            pltpu.VMEM((doc_dev * width, count), jnp.bfloat16),
            pltpu.VMEM((tok_count * width, count), jnp.bfloat16),
            pltpu.VMEM((tok_count // 2, doc_dev * width, LANES), jnp.float32),
            pltpu.SemaphoreType.DMA((4,)),
        ],
        compiler_params=pltpu.CompilerParams(vmem_limit_bytes=32 * 1024 * 1024),
        name="features",
    )(*(pltpu.with_memory_space_constraint(x, pltpu.HBM) for x in (doc_lengths, owner_map, proj_rows, query_features)))


def block_products(query, blocks):
    features = jnp.concatenate([block[...] for block in blocks], axis=0)
    return lax.dot_general(features, query[...], ROW_BY_ROW, preferred_element_type=jnp.float32)


def early_kernel(query, *refs):
    *blocks, products = refs
    products[...] = block_products(query, blocks)


def score_kernel(query, early, *refs):
    *blocks, scores = refs
    doc_dev = blocks[0].shape[0]
    late = block_products(query, blocks)
    own, second, first, third, own_next, third_next = (
        early[i : i + doc_dev, :] for i in range(0, early.shape[0], doc_dev)
    )
    second_next, first_next = late[:doc_dev], late[doc_dev:]
    ex = lax.axis_index("ex")
    odd = lax.rem(ex, 2) == 1
    parts = [
        own,
        own_next,
        jnp.where(odd, first, second),
        jnp.where(odd, second_next, first_next),
        jnp.where(odd, second, first),
        jnp.where(odd, first_next, second_next),
        third,
        third_next,
    ]
    flip = 1
    while flip < len(parts):
        swap = lax.rem(lax.div(ex, flip), 2) == 1
        parts = [jnp.where(swap, parts[i ^ flip], parts[i]) for i in range(len(parts))]
        flip *= 2
    scores[...] = jnp.concatenate(parts, axis=0).T


def call_on_vmem(kernel, name, shape, *operands):
    whole = pl.BlockSpec(memory_space=pltpu.VMEM)
    moved = sum(x.nbytes for x in operands)
    return pl.pallas_call(
        kernel,
        out_shape=jax.ShapeDtypeStruct(shape, jnp.float32),
        in_specs=[whole] * len(operands),
        out_specs=whole,
        cost_estimate=pl.CostEstimate(flops=0, bytes_accessed=moved, transcendentals=0),
        compiler_params=pltpu.CompilerParams(vmem_limit_bytes=16 * 1024 * 1024),
        name=name,
    )(*(pltpu.with_memory_space_constraint(x, pltpu.VMEM) for x in operands))


def block_scores(query, held, held_next):
    own_next, second_next, first_next, third_next = held_next
    ready = (*held, own_next, third_next)
    doc_dev, queries = held[0].shape[0], query.shape[0]
    early = call_on_vmem(
        early_kernel, "early_products", (len(ready) * doc_dev, queries), query, *ready
    )
    shape = (queries, (len(ready) + 2) * doc_dev)
    return call_on_vmem(score_kernel, "scores", shape, query, early, second_next, first_next)


def exchange(block, axis, flip):
    return lax.ppermute(block, axis, [(i, i ^ flip) for i in range(lax.axis_size(axis))])


def body(proj_rows, query_features, doc_lengths, owner_map):
    tok_count = lax.axis_size("tok")
    *shares, query_features = feature_shares(
        proj_rows, query_features, doc_lengths, owner_map, tok_count
    )
    total = shares[0]
    for shift in sorted(range(1, tok_count), key=lambda flip: (flip < 2, flip)):
        total = total + exchange(shares[shift], "tok", shift).astype(jnp.float32)
    features = total.astype(jnp.bfloat16)
    ex_count = lax.axis_size("ex")
    if ex_count != 8:
        gathered = lax.all_gather(features, "ex", axis=0, tiled=True)
        return jnp.einsum("qf,df->qd", query_features, gathered, preferred_element_type=jnp.float32)
    turns = [[(i, i ^ (first if i % 2 else 6 - first)) for i in range(ex_count)] for first in (2, 4)]
    third = exchange(features, "ex", 6)
    first, second = (lax.ppermute(features, "ex", turn) for turn in turns)
    held = (features, second, first, third)
    return block_scores(query_features, held, [exchange(block, "ex", 1) for block in held])


def solution(mesh):
    placed = (P(("ex", "tok"), None), P("ex", None), P("ex", None), P("ex", None))
    return jax.shard_map(
        body, mesh=mesh, in_specs=placed, out_specs=P("ex", "tok"), check_vma=False
    )
```

```python
import jax
import jax.numpy as jnp
from jax import lax
from jax.experimental import pallas as pl
from jax.experimental.pallas import tpu as pltpu
from jax.sharding import PartitionSpec as P

LANES = 128
ROW_BY_ROW = (((1,), (1,)), ((), ()))


def feature_kernel(lengths_hbm, owners_hbm, rows_hbm, *refs):
    *shares, lengths, owners, rows, grads, inputs, sums, arrived = refs
    count, width = rows.shape[0], rows.shape[1] // 2
    copies = [
        pltpu.make_async_copy(source, target, arrived.at[i])
        for i, (source, target) in enumerate(
            ((lengths_hbm, lengths), (owners_hbm, owners), (rows_hbm, rows))
        )
    ]
    for copy in copies:
        copy.start()
    docs, tok_count = lengths.shape[1], len(shares)
    doc_dev = docs // tok_count
    tok = lax.axis_index("tok")

    copies[0].wait()
    copies[1].wait()
    blocks, shift = count // LANES, doc_dev.bit_length() - 1
    token = lax.broadcasted_iota(jnp.int32, (blocks, LANES), 0) * LANES
    token = tok * count + token + lax.broadcasted_iota(jnp.int32, (blocks, LANES), 1)
    slot_of = jnp.zeros((blocks, LANES), jnp.int32)
    size_row = lax.broadcasted_iota(jnp.int32, (doc_dev, LANES), 0)
    size_slots = [((tok ^ s) << shift) + size_row for s in range(tok_count)]
    sizes = [jnp.ones((doc_dev, LANES), jnp.int32) for _ in shares]
    start = jnp.int32(0)
    for k in range(docs):
        slot, length = owners[0, k], lengths[0, k]
        slot_of = jnp.where(token >= start, slot, slot_of)
        sizes = [jnp.where(at == slot, length, size) for at, size in zip(size_slots, sizes)]
        start = start + length
    share_of, row_of = (slot_of >> shift) ^ tok, slot_of & (doc_dev - 1)

    eye = (
        lax.broadcasted_iota(jnp.int32, (2 * width, 2 * width), 0)
        == lax.broadcasted_iota(jnp.int32, (2 * width, 2 * width), 1)
    ).astype(rows.dtype)
    copies[2].wait()
    for b in range(blocks):
        part = slice(b * LANES, (b + 1) * LANES)
        turned = lax.dot_general(eye, rows[part, :], ROW_BY_ROW, preferred_element_type=jnp.float32)
        for digits, values, target in (
            (share_of, turned[:width], inputs),
            (row_of, turned[width:], grads),
        ):
            digit = jnp.broadcast_to(digits[b : b + 1, :], (8, LANES))[None]
            values = values.reshape(-1, 8, LANES)
            for at in range(target.shape[0] // width):
                kept = jnp.where(digit == at, values, 0.0).reshape(width, LANES)
                target[at * width : (at + 1) * width, part] = kept.astype(target.dtype)
    product = lax.dot_general(
        grads[...], inputs[...], ROW_BY_ROW, preferred_element_type=jnp.float32
    )
    for p in range(sums.shape[0]):
        sums[p] = product[:, p * LANES : (p + 1) * LANES]

    scales = [1.0 / jnp.sqrt(size.astype(jnp.float32)) for size in sizes]
    low_half = lax.broadcasted_iota(jnp.int32, (doc_dev, LANES), 1) < width
    for m in range(width // 2):
        out = slice(m * LANES, (m + 1) * LANES)
        for s in range(0, tok_count, 2):
            first = sums[s // 2, pl.ds(2 * m, doc_dev, stride=width), :]
            second = sums[s // 2, pl.ds(2 * m + 1, doc_dev, stride=width), :]
            left = jnp.where(low_half, first, pltpu.roll(second, width, 1))
            right = jnp.where(low_half, pltpu.roll(first, width, 1), second)
            shares[s][:, out] = (left * scales[s]).astype(shares[s].dtype)
            shares[s + 1][:, out] = (right * scales[s + 1]).astype(shares[s + 1].dtype)


def feature_shares(proj_rows, doc_lengths, owner_map, tok_count):
    count, width = proj_rows.shape[0], proj_rows.shape[1] // 2
    doc_dev = doc_lengths.shape[1] // tok_count
    feat = width * width
    far = pl.BlockSpec(memory_space=pltpu.HBM)
    whole = pl.BlockSpec(memory_space=pltpu.VMEM)
    return pl.pallas_call(
        feature_kernel,
        out_shape=[
            jax.ShapeDtypeStruct((doc_dev, feat), jnp.bfloat16 if s else jnp.float32)
            for s in range(tok_count)
        ],
        in_specs=[far, far, far],
        out_specs=[whole] * tok_count,
        scratch_shapes=[
            pltpu.SMEM(doc_lengths.shape, jnp.int32),
            pltpu.SMEM(owner_map.shape, jnp.int32),
            pltpu.VMEM(proj_rows.shape, proj_rows.dtype),
            pltpu.VMEM((doc_dev * width, count), jnp.bfloat16),
            pltpu.VMEM((tok_count * width, count), jnp.bfloat16),
            pltpu.VMEM((tok_count // 2, doc_dev * width, LANES), jnp.float32),
            pltpu.SemaphoreType.DMA((3,)),
        ],
        compiler_params=pltpu.CompilerParams(vmem_limit_bytes=32 * 1024 * 1024),
        name="features",
    )(*(pltpu.with_memory_space_constraint(x, pltpu.HBM) for x in (doc_lengths, owner_map, proj_rows)))


def score_kernel(query, *refs):
    *blocks, scores = refs
    doc_dev = blocks[0].shape[0]
    features = jnp.concatenate([block[...] for block in blocks], axis=0)
    products = lax.dot_general(
        features, query[...], ROW_BY_ROW, preferred_element_type=jnp.float32
    )
    own, second, third, first, own_next, second_next, third_next, first_next = (
        products[i * doc_dev : (i + 1) * doc_dev] for i in range(len(blocks))
    )
    ex = lax.axis_index("ex")
    odd = lax.rem(ex, 2) == 1
    parts = [
        own,
        own_next,
        jnp.where(odd, first, second),
        jnp.where(odd, second_next, first_next),
        jnp.where(odd, second, first),
        jnp.where(odd, first_next, second_next),
        third,
        third_next,
    ]
    flip = 1
    while flip < len(parts):
        swap = lax.rem(lax.div(ex, flip), 2) == 1
        parts = [jnp.where(swap, parts[i ^ flip], parts[i]) for i in range(len(parts))]
        flip *= 2
    scores[...] = jnp.concatenate(parts, axis=0).T


def block_scores(query_features, held, held_next):
    whole = pl.BlockSpec(memory_space=pltpu.VMEM)
    operands = (query_features, *held, *held_next)
    docs = (len(operands) - 1) * held[0].shape[0]
    return pl.pallas_call(
        score_kernel,
        out_shape=jax.ShapeDtypeStruct((query_features.shape[0], docs), jnp.float32),
        in_specs=[whole] * len(operands),
        out_specs=whole,
        compiler_params=pltpu.CompilerParams(vmem_limit_bytes=16 * 1024 * 1024),
        name="scores",
    )(*(pltpu.with_memory_space_constraint(x, pltpu.VMEM) for x in operands))


def exchange(block, axis, flip):
    return lax.ppermute(block, axis, [(i, i ^ flip) for i in range(lax.axis_size(axis))])


def body(proj_rows, query_features, doc_lengths, owner_map):
    tok_count = lax.axis_size("tok")
    shares = feature_shares(proj_rows, doc_lengths, owner_map, tok_count)
    total = shares[0]
    for shift in sorted(range(1, tok_count), key=lambda flip: (flip < 2, flip)):
        total = total + exchange(shares[shift], "tok", shift).astype(jnp.float32)
    features = total.astype(jnp.bfloat16)
    ex_count = lax.axis_size("ex")
    if ex_count != 8:
        gathered = lax.all_gather(features, "ex", axis=0, tiled=True)
        return jnp.einsum("qf,df->qd", query_features, gathered, preferred_element_type=jnp.float32)
    turns = [[(i, i ^ (first if i % 2 else 6 - first)) for i in range(ex_count)] for first in (2, 4)]
    third = exchange(features, "ex", 6)
    first, second = (lax.ppermute(features, "ex", turn) for turn in turns)
    held = (features, second, third, first)
    return block_scores(query_features, held, [exchange(block, "ex", 1) for block in held])


def solution(mesh):
    placed = (P(("ex", "tok"), None), P("ex", None), P("ex", None), P("ex", None))
    return jax.shard_map(
        body, mesh=mesh, in_specs=placed, out_specs=P("ex", "tok"), check_vma=False
    )
```

```python
import jax
import jax.numpy as jnp
from jax import lax
from jax.experimental import pallas as pl
from jax.experimental.pallas import tpu as pltpu
from jax.sharding import PartitionSpec as P

LANES = 128
ROW_BY_ROW = (((1,), (1,)), ((), ()))


def feature_kernel(lengths_hbm, owners_hbm, rows_hbm, query_hbm, *refs):
    *shares, query, lengths, owners, rows, grads, inputs, sums, arrived = refs
    count, width = rows.shape[0], rows.shape[1] // 2
    copies = [
        pltpu.make_async_copy(source, target, arrived.at[i])
        for i, (source, target) in enumerate(
            ((lengths_hbm, lengths), (owners_hbm, owners), (rows_hbm, rows), (query_hbm, query))
        )
    ]
    for copy in copies[:3]:
        copy.start()
    docs, tok_count = lengths.shape[1], len(shares)
    doc_dev = docs // tok_count
    tok = lax.axis_index("tok")

    copies[0].wait()
    copies[1].wait()
    blocks, shift = count // LANES, doc_dev.bit_length() - 1
    token = lax.broadcasted_iota(jnp.int32, (blocks, LANES), 0) * LANES
    token = tok * count + token + lax.broadcasted_iota(jnp.int32, (blocks, LANES), 1)
    slot_of = jnp.zeros((blocks, LANES), jnp.int32)
    size_row = lax.broadcasted_iota(jnp.int32, (doc_dev, LANES), 0)
    size_slots = [((tok ^ s) << shift) + size_row for s in range(tok_count)]
    sizes = [jnp.ones((doc_dev, LANES), jnp.int32) for _ in shares]
    start = jnp.int32(0)
    for k in range(docs):
        slot, length = owners[0, k], lengths[0, k]
        slot_of = jnp.where(token >= start, slot, slot_of)
        sizes = [jnp.where(at == slot, length, size) for at, size in zip(size_slots, sizes)]
        start = start + length
    share_of, row_of = (slot_of >> shift) ^ tok, slot_of & (doc_dev - 1)

    eye = (
        lax.broadcasted_iota(jnp.int32, (2 * width, 2 * width), 0)
        == lax.broadcasted_iota(jnp.int32, (2 * width, 2 * width), 1)
    ).astype(rows.dtype)
    copies[2].wait()
    copies[3].start()
    for b in range(blocks):
        part = slice(b * LANES, (b + 1) * LANES)
        turned = lax.dot_general(eye, rows[part, :], ROW_BY_ROW, preferred_element_type=jnp.float32)
        turned = turned.astype(rows.dtype)
        for digits, values, target in (
            (share_of, turned[:width], inputs),
            (row_of, turned[width:], grads),
        ):
            digit = jnp.broadcast_to(digits[b : b + 1, :], (16, LANES))
            values = values.reshape(-1, 16, LANES)
            for at in range(target.shape[0] // width):
                mask = jnp.where(digit == at, 1.0, 0.0).astype(values.dtype)
                target[at * width : (at + 1) * width, part] = (values * mask[None]).reshape(width, LANES)
    product = lax.dot_general(
        grads[...], inputs[...], ROW_BY_ROW, preferred_element_type=jnp.float32
    )
    for p in range(sums.shape[0]):
        sums[p] = product[:, p * LANES : (p + 1) * LANES]

    scales = [1.0 / jnp.sqrt(size.astype(jnp.float32)) for size in sizes]
    low_half = lax.broadcasted_iota(jnp.int32, (doc_dev, LANES), 1) < width
    for m in range(width // 2):
        out = slice(m * LANES, (m + 1) * LANES)
        for s in range(0, tok_count, 2):
            first = sums[s // 2, pl.ds(2 * m, doc_dev, stride=width), :]
            second = sums[s // 2, pl.ds(2 * m + 1, doc_dev, stride=width), :]
            left = jnp.where(low_half, first, pltpu.roll(second, width, 1))
            right = jnp.where(low_half, pltpu.roll(first, width, 1), second)
            shares[s][:, out] = (left * scales[s]).astype(shares[s].dtype)
            shares[s + 1][:, out] = (right * scales[s + 1]).astype(shares[s + 1].dtype)
    copies[3].wait()


def feature_shares(proj_rows, query_features, doc_lengths, owner_map, tok_count):
    count, width = proj_rows.shape[0], proj_rows.shape[1] // 2
    doc_dev = doc_lengths.shape[1] // tok_count
    feat = width * width
    far = pl.BlockSpec(memory_space=pltpu.HBM)
    whole = pl.BlockSpec(memory_space=pltpu.VMEM)
    return pl.pallas_call(
        feature_kernel,
        out_shape=[
            jax.ShapeDtypeStruct((doc_dev, feat), jnp.bfloat16 if s else jnp.float32)
            for s in range(tok_count)
        ]
        + [jax.ShapeDtypeStruct(query_features.shape, query_features.dtype)],
        in_specs=[far] * 4,
        out_specs=[whole] * (tok_count + 1),
        scratch_shapes=[
            pltpu.SMEM(doc_lengths.shape, jnp.int32),
            pltpu.SMEM(owner_map.shape, jnp.int32),
            pltpu.VMEM(proj_rows.shape, proj_rows.dtype),
            pltpu.VMEM((doc_dev * width, count), jnp.bfloat16),
            pltpu.VMEM((tok_count * width, count), jnp.bfloat16),
            pltpu.VMEM((tok_count // 2, doc_dev * width, LANES), jnp.float32),
            pltpu.SemaphoreType.DMA((4,)),
        ],
        compiler_params=pltpu.CompilerParams(vmem_limit_bytes=32 * 1024 * 1024),
        name="features",
    )(*(pltpu.with_memory_space_constraint(x, pltpu.HBM) for x in (doc_lengths, owner_map, proj_rows, query_features)))


def block_products(query, blocks):
    features = jnp.concatenate([block[...] for block in blocks], axis=0)
    return lax.dot_general(features, query[...], ROW_BY_ROW, preferred_element_type=jnp.float32)


def early_kernel(query, *refs):
    *blocks, products = refs
    products[...] = block_products(query, blocks)


def score_kernel(query, early, *refs):
    *blocks, scores = refs
    doc_dev = blocks[0].shape[0]
    late = block_products(query, blocks)
    own, second, first, third, own_next, third_next = (
        early[i : i + doc_dev, :] for i in range(0, early.shape[0], doc_dev)
    )
    second_next, first_next = late[:doc_dev], late[doc_dev:]
    ex = lax.axis_index("ex")
    odd = lax.rem(ex, 2) == 1
    parts = [
        own,
        own_next,
        jnp.where(odd, first, second),
        jnp.where(odd, second_next, first_next),
        jnp.where(odd, second, first),
        jnp.where(odd, first_next, second_next),
        third,
        third_next,
    ]
    flip = 1
    while flip < len(parts):
        swap = lax.rem(lax.div(ex, flip), 2) == 1
        parts = [jnp.where(swap, parts[i ^ flip], parts[i]) for i in range(len(parts))]
        flip *= 2
    scores[...] = jnp.concatenate(parts, axis=0).T


def call_on_vmem(kernel, name, shape, *operands):
    whole = pl.BlockSpec(memory_space=pltpu.VMEM)
    moved = sum(x.nbytes for x in operands)
    return pl.pallas_call(
        kernel,
        out_shape=jax.ShapeDtypeStruct(shape, jnp.float32),
        in_specs=[whole] * len(operands),
        out_specs=whole,
        cost_estimate=pl.CostEstimate(flops=0, bytes_accessed=moved, transcendentals=0),
        compiler_params=pltpu.CompilerParams(vmem_limit_bytes=16 * 1024 * 1024),
        name=name,
    )(*(pltpu.with_memory_space_constraint(x, pltpu.VMEM) for x in operands))


def block_scores(query, held, held_next):
    own_next, second_next, first_next, third_next = held_next
    ready = (*held, own_next, third_next)
    doc_dev, queries = held[0].shape[0], query.shape[0]
    early = call_on_vmem(
        early_kernel, "early_products", (len(ready) * doc_dev, queries), query, *ready
    )
    shape = (queries, (len(ready) + 2) * doc_dev)
    return call_on_vmem(score_kernel, "scores", shape, query, early, second_next, first_next)


def exchange(block, axis, flip):
    return lax.ppermute(block, axis, [(i, i ^ flip) for i in range(lax.axis_size(axis))])


def body(proj_rows, query_features, doc_lengths, owner_map):
    tok_count = lax.axis_size("tok")
    *shares, query_features = feature_shares(
        proj_rows, query_features, doc_lengths, owner_map, tok_count
    )
    total = shares[0]
    for shift in sorted(range(1, tok_count), key=lambda flip: (flip < 2, flip)):
        total = total + exchange(shares[shift], "tok", shift).astype(jnp.float32)
    features = total.astype(jnp.bfloat16)
    ex_count = lax.axis_size("ex")
    if ex_count != 8:
        gathered = lax.all_gather(features, "ex", axis=0, tiled=True)
        return jnp.einsum("qf,df->qd", query_features, gathered, preferred_element_type=jnp.float32)
    turns = [[(i, i ^ (first if i % 2 else 6 - first)) for i in range(ex_count)] for first in (2, 4)]
    third = exchange(features, "ex", 6)
    first, second = (lax.ppermute(features, "ex", turn) for turn in turns)
    held = (features, second, first, third)
    return block_scores(query_features, held, [exchange(block, "ex", 1) for block in held])


def solution(mesh):
    placed = (P(("ex", "tok"), None), P("ex", None), P("ex", None), P("ex", None))
    return jax.shard_map(
        body, mesh=mesh, in_specs=placed, out_specs=P("ex", "tok"), check_vma=False
    )
```

```python
import jax
import jax.numpy as jnp
from jax import lax
from jax.experimental import pallas as pl
from jax.experimental.pallas import tpu as pltpu
from jax.sharding import PartitionSpec as P

LANES = 128
ROW_BY_ROW = (((1,), (1,)), ((), ()))


def feature_kernel(lengths_hbm, owners_hbm, rows_hbm, query_hbm, *refs):
    *shares, query, lengths, owners, rows, grads, inputs, sums, arrived = refs
    count, width = rows.shape[0], rows.shape[1] // 2
    copies = [
        pltpu.make_async_copy(source, target, arrived.at[i])
        for i, (source, target) in enumerate(
            ((lengths_hbm, lengths), (owners_hbm, owners), (rows_hbm, rows), (query_hbm, query))
        )
    ]
    for copy in copies[:3]:
        copy.start()
    docs, tok_count = lengths.shape[1], len(shares)
    doc_dev = docs // tok_count
    tok = lax.axis_index("tok")

    copies[0].wait()
    copies[1].wait()
    blocks, shift = count // LANES, doc_dev.bit_length() - 1
    token = lax.broadcasted_iota(jnp.int32, (blocks, LANES), 0) * LANES
    token = tok * count + token + lax.broadcasted_iota(jnp.int32, (blocks, LANES), 1)
    slot_of = jnp.zeros((blocks, LANES), jnp.int32)
    size_row = lax.broadcasted_iota(jnp.int32, (doc_dev, LANES), 0)
    size_slots = [((tok ^ s) << shift) + size_row for s in range(tok_count)]
    sizes = [jnp.ones((doc_dev, LANES), jnp.int32) for _ in shares]
    start = jnp.int32(0)
    for k in range(docs):
        slot, length = owners[0, k], lengths[0, k]
        slot_of = jnp.where(token >= start, slot, slot_of)
        sizes = [jnp.where(at == slot, length, size) for at, size in zip(size_slots, sizes)]
        start = start + length
    share_of, row_of = (slot_of >> shift) ^ tok, slot_of & (doc_dev - 1)

    eye = (
        lax.broadcasted_iota(jnp.int32, (2 * width, 2 * width), 0)
        == lax.broadcasted_iota(jnp.int32, (2 * width, 2 * width), 1)
    ).astype(rows.dtype)
    copies[2].wait()
    copies[3].start()
    for b in range(blocks):
        part = slice(b * LANES, (b + 1) * LANES)
        turned = lax.dot_general(eye, rows[part, :], ROW_BY_ROW, preferred_element_type=jnp.float32)
        turned = turned.astype(rows.dtype)
        for digits, values, target in (
            (share_of, turned[:width], inputs),
            (row_of, turned[width:], grads),
        ):
            digit = jnp.broadcast_to(digits[b : b + 1, :], (16, LANES))
            values = values.reshape(-1, 16, LANES)
            for at in range(target.shape[0] // width):
                mask = jnp.where(digit == at, 1.0, 0.0).astype(values.dtype)
                target[at * width : (at + 1) * width, part] = (values * mask[None]).reshape(width, LANES)
    product = lax.dot_general(
        grads[...], inputs[...], ROW_BY_ROW, preferred_element_type=jnp.float32
    )
    for p in range(sums.shape[0]):
        sums[p] = product[:, p * LANES : (p + 1) * LANES]

    scales = [1.0 / jnp.sqrt(size.astype(jnp.float32)) for size in sizes]
    low_half = lax.broadcasted_iota(jnp.int32, (doc_dev, LANES), 1) < width
    for m in range(width // 2):
        out = slice(m * LANES, (m + 1) * LANES)
        for s in range(0, tok_count, 2):
            first = sums[s // 2, pl.ds(2 * m, doc_dev, stride=width), :]
            second = sums[s // 2, pl.ds(2 * m + 1, doc_dev, stride=width), :]
            left = jnp.where(low_half, first, pltpu.roll(second, width, 1))
            right = jnp.where(low_half, pltpu.roll(first, width, 1), second)
            shares[s][:, out] = (left * scales[s]).astype(shares[s].dtype)
            shares[s + 1][:, out] = (right * scales[s + 1]).astype(shares[s + 1].dtype)
    copies[3].wait()


def feature_shares(proj_rows, query_features, doc_lengths, owner_map, tok_count):
    count, width = proj_rows.shape[0], proj_rows.shape[1] // 2
    doc_dev = doc_lengths.shape[1] // tok_count
    feat = width * width
    far = pl.BlockSpec(memory_space=pltpu.HBM)
    whole = pl.BlockSpec(memory_space=pltpu.VMEM)
    return pl.pallas_call(
        feature_kernel,
        out_shape=[
            jax.ShapeDtypeStruct((doc_dev, feat), jnp.bfloat16 if s else jnp.float32)
            for s in range(tok_count)
        ]
        + [jax.ShapeDtypeStruct(query_features.shape, query_features.dtype)],
        in_specs=[far] * 4,
        out_specs=[whole] * (tok_count + 1),
        scratch_shapes=[
            pltpu.SMEM(doc_lengths.shape, jnp.int32),
            pltpu.SMEM(owner_map.shape, jnp.int32),
            pltpu.VMEM(proj_rows.shape, proj_rows.dtype),
            pltpu.VMEM((doc_dev * width, count), jnp.bfloat16),
            pltpu.VMEM((tok_count * width, count), jnp.bfloat16),
            pltpu.VMEM((tok_count // 2, doc_dev * width, LANES), jnp.float32),
            pltpu.SemaphoreType.DMA((4,)),
        ],
        compiler_params=pltpu.CompilerParams(vmem_limit_bytes=32 * 1024 * 1024),
        name="features",
    )(*(pltpu.with_memory_space_constraint(x, pltpu.HBM) for x in (doc_lengths, owner_map, proj_rows, query_features)))


def block_products(query, blocks):
    features = jnp.concatenate([block[...] for block in blocks], axis=0)
    return lax.dot_general(features, query[...], ROW_BY_ROW, preferred_element_type=jnp.float32)


def early_kernel(query, *refs):
    *blocks, products = refs
    products[...] = block_products(query, blocks)


def score_kernel(query, early, *refs):
    *blocks, scores = refs
    doc_dev = blocks[0].shape[0]
    late = block_products(query, blocks)
    own, second, first, third, own_next, third_next = (
        early[i : i + doc_dev, :] for i in range(0, early.shape[0], doc_dev)
    )
    first_next, second_next = late[:doc_dev], late[doc_dev:]
    ex = lax.axis_index("ex")
    odd = lax.rem(ex, 2) == 1
    parts = [
        own,
        own_next,
        jnp.where(odd, first, second),
        jnp.where(odd, second_next, first_next),
        jnp.where(odd, second, first),
        jnp.where(odd, first_next, second_next),
        third,
        third_next,
    ]
    flip = 1
    while flip < len(parts):
        swap = lax.rem(lax.div(ex, flip), 2) == 1
        parts = [jnp.where(swap, parts[i ^ flip], parts[i]) for i in range(len(parts))]
        flip *= 2
    scores[...] = jnp.concatenate(parts, axis=0).T


def call_on_vmem(kernel, name, shape, *operands):
    whole = pl.BlockSpec(memory_space=pltpu.VMEM)
    moved = sum(x.nbytes for x in operands)
    return pl.pallas_call(
        kernel,
        out_shape=jax.ShapeDtypeStruct(shape, jnp.float32),
        in_specs=[whole] * len(operands),
        out_specs=whole,
        cost_estimate=pl.CostEstimate(flops=0, bytes_accessed=moved, transcendentals=0),
        compiler_params=pltpu.CompilerParams(vmem_limit_bytes=16 * 1024 * 1024),
        name=name,
    )(*(pltpu.with_memory_space_constraint(x, pltpu.VMEM) for x in operands))


def block_scores(query, held, held_next):
    own_next, second_next, first_next, third_next = held_next
    ready = (*held, own_next, third_next)
    doc_dev, queries = held[0].shape[0], query.shape[0]
    early = call_on_vmem(
        early_kernel, "early_products", (len(ready) * doc_dev, queries), query, *ready
    )
    shape = (queries, (len(ready) + 2) * doc_dev)
    return call_on_vmem(score_kernel, "scores", shape, query, early, first_next, second_next)


def exchange(block, axis, flip):
    return lax.ppermute(block, axis, [(i, i ^ flip) for i in range(lax.axis_size(axis))])


def body(proj_rows, query_features, doc_lengths, owner_map):
    tok_count = lax.axis_size("tok")
    *shares, query_features = feature_shares(
        proj_rows, query_features, doc_lengths, owner_map, tok_count
    )
    total = shares[0]
    for shift in sorted(range(1, tok_count), key=lambda flip: (flip < 2, flip)):
        total = total + exchange(shares[shift], "tok", shift).astype(jnp.float32)
    features = total.astype(jnp.bfloat16)
    ex_count = lax.axis_size("ex")
    if ex_count != 8:
        gathered = lax.all_gather(features, "ex", axis=0, tiled=True)
        return jnp.einsum("qf,df->qd", query_features, gathered, preferred_element_type=jnp.float32)
    turns = [[(i, i ^ (first if i % 2 else 6 - first)) for i in range(ex_count)] for first in (2, 4)]
    third = exchange(features, "ex", 6)
    first, second = (lax.ppermute(features, "ex", turn) for turn in turns)
    held = (features, second, first, third)
    return block_scores(query_features, held, [exchange(block, "ex", 1) for block in held])


def solution(mesh):
    placed = (P(("ex", "tok"), None), P("ex", None), P("ex", None), P("ex", None))
    return jax.shard_map(
        body, mesh=mesh, in_specs=placed, out_specs=P("ex", "tok"), check_vma=False
    )
```
